32 devices in a mesh: fsdp: 8 (over z, y), tp: 4 (over x, core).
Axes of the slice: x: 2, y: 2, z: 4, core: 2. Of those that a mesh axis runs over, the one named last changes fastest.
Arguments:
- base_weight: bfloat16 [16384, 26624], P(('fsdp', 'tp')), may hold values from -0.09375 to 0.09375
- left_factor: bfloat16 [16384, 64], P(('fsdp', 'tp')), may hold values from -0.75 to 0.75
- right_factor: bfloat16 [64, 26624], P(None, 'tp'), may hold values from -0.029907227 to 0.029907227
- magnitude: float32 [26624], replicated, may hold values from 6 to 96
Outputs:
- quantized: bfloat16 [16384, 26624], P('fsdp', 'tp')
- block_scales: float32 [128, 208], P('fsdp', 'tp')
The draws below stay inside these ranges and needn't reach their ends.
All inputs are finite; a program needn't handle non-finite values. Where the reference program divides by a largest or mean magnitude, that divisor is 1e-20 or more.
Results may differ from the reference program's by a relative error of at most 0.01.
Values may be sent and summed in bfloat16 or wider, within the bound.
No kernel may reach another device: no remote copies, remote signals or barrier semaphores. Data moves between devices by JAX's collectives and lax.ppermute only.
A program may use at most 320 MiB of HBM per device.

```python
import math
import jax
import jax.numpy as jnp
from jax import lax

DIN = 16384
DOUT = 26624
RANK = 64
BLOCK = 128


def spiked(result, own_key, source, target, shards_of, factor):
    def block_of(position):
        return (jnp.arange(result.shape[position]) // (result.shape[position] // shards_of)).reshape((-1,) + (1,) * (result.ndim - 1 - position))

    one_side = jax.random.permutation(own_key, shards_of)[block_of(target)]
    other_side = (block_of(target) + shards_of // 2) % shards_of
    return jnp.where((block_of(source) == one_side) | (block_of(source) == other_side), factor * result, result)


def steps_of(own_key, dims, cuts, low, high):
    def one(dim, blocks):
        steps = jax.random.uniform(jax.random.fold_in(jax.random.fold_in(own_key, 6), dim), (blocks,), jnp.float32, low / len(cuts), high / len(cuts))
        return jnp.repeat(jnp.exp(steps), dims[dim] // blocks).reshape((-1,) + (1,) * (len(dims) - dim - 1))

    gain = one(*cuts[0])
    for cut in cuts[1:]:
        gain = gain * one(*cut)
    return gain


def noise(key, dims, deviation, most, split=(), kind=jnp.bfloat16):
    values = jax.random.normal(key, dims, jnp.float32) * deviation
    if len(split) > 0:
        values = steps_of(key, dims, split, -0.22, 0.18) * values
    return jnp.clip(values, min=-most, max=most).astype(kind)


def noise_with(rng, dims, scale, bound, pieces, heavy, kind=jnp.bfloat16):
    entries = scale * jax.random.normal(rng, dims, jnp.float32)
    if pieces:
        entries = entries * steps_of(rng, dims, pieces, -0.22, 0.18)
    return jnp.clip(spiked(entries, jax.random.fold_in(rng, 3), *heavy), -bound, bound).astype(kind)


def setup_inputs(seed: int = 0) -> dict:
    key_of = jax.random.split(jax.random.key(seed), 5)
    return {
        "base_weight": noise_with(key_of[0], (DIN, DOUT), DIN ** -0.5, 0.09375, ((0, 32),), (0, 1, 32, 2.75)),
        "left_factor": noise(key_of[1], (DIN, RANK), RANK ** -0.5, 0.75, ((0, 32),)),
        "right_factor": noise(key_of[2], (RANK, DOUT), 0.005, 0.029907227, ((1, 4),)),
        "magnitude": jnp.clip(jnp.exp(jax.random.uniform(key_of[3], (DOUT,), jnp.float32, math.log(6.0), math.log(96.0))), 6.0, 96.0),
    }


epsilon = 1e-06

def reference(base_weight, left_factor, right_factor, magnitude):
    block_total = DOUT // BLOCK

    def one_block(block_index):
        start = (block_index * BLOCK).astype(jnp.int32)
        base_cols = lax.dynamic_slice_in_dim(base_weight, start, BLOCK, 1)
        right_cols = lax.dynamic_slice_in_dim(right_factor, start, BLOCK, 1)
        mag_cols = lax.dynamic_slice_in_dim(magnitude, start, BLOCK, 0)
        combined = base_cols.astype(jnp.float32) + jnp.dot(left_factor, right_cols, preferred_element_type=jnp.float32)
        col_norm = jnp.sqrt(lax.optimization_barrier(jnp.sum(combined * combined, axis=0)) + epsilon)
        merged = (mag_cols * combined / col_norm).astype(jnp.bfloat16)
        tile_view = merged.astype(jnp.float32).reshape(DIN // BLOCK, BLOCK, BLOCK)
        block_max = lax.optimization_barrier(jnp.max(jnp.abs(tile_view), axis=(1, 2)))
        scaled = (tile_view / (block_max[:, None, None] + epsilon)).reshape(DIN, BLOCK).astype(jnp.bfloat16)
        return (scaled, block_max)
    scaled_all, max_all = lax.map(one_block, jnp.arange(block_total, dtype=jnp.int32))
    quantized = jnp.transpose(scaled_all, (1, 0, 2)).reshape(DIN, DOUT)
    block_scales = jnp.transpose(max_all, (1, 0))
    return (quantized, block_scales)
```

```python
import functools

import jax
import jax.numpy as jnp
from jax import lax
from jax.experimental import pallas as pl
from jax.experimental.pallas import tpu as pltpu
from jax.sharding import PartitionSpec as P

BLOCK = 128
EPSILON = 1e-06
PARTS = (2, 3, 3, 3, 2)


def chunk_units(total, parts):
    bounds = [0]
    whole = sum(parts)
    for i in range(len(parts)):
        bounds.append(round(total * sum(parts[: i + 1]) / whole))
    return [(a, b) for a, b in zip(bounds, bounds[1:]) if b > a]


def pack_kernel(base_ref, out_ref):
    out_ref[...] = base_ref[...]


def pack(base, tp, unit, first, count):
    rows = base.shape[0]
    group_units = base.shape[1] // (tp * unit)
    return pl.pallas_call(
        pack_kernel,
        out_shape=jax.ShapeDtypeStruct((tp * rows, count * unit), base.dtype),
        grid=(tp, count),
        in_specs=[pl.BlockSpec((rows, unit), lambda g, j: (0, g * group_units + first + j))],
        out_specs=pl.BlockSpec((rows, unit), lambda g, j: (g, j)),
        compiler_params=pltpu.CompilerParams(vmem_limit_bytes=40 * 2**20),
        cost_estimate=pl.CostEstimate(
            flops=0, bytes_accessed=4 * tp * rows * count * unit, transcendentals=0
        ),
    )(base)


def squares_kernel(piece_ref, left_ref, right_ref, out_ref):
    rows, cols = piece_ref.shape
    total = jnp.zeros((8, cols), jnp.float32)
    for r in range(0, rows, BLOCK):
        span = pl.ds(r, BLOCK)
        low_rank = jnp.dot(left_ref[span, :], right_ref[...], preferred_element_type=jnp.float32)
        combined = piece_ref[span, :].astype(jnp.float32) + low_rank
        squares = combined * combined
        total = total + jnp.sum(squares.reshape(BLOCK // 8, 8, cols), axis=0)
    out_ref[...] = jnp.sum(total, axis=0, keepdims=True)


def column_squares(piece, left, right, unit, first):
    rows, cols = piece.shape
    rank = left.shape[1]
    return pl.pallas_call(
        squares_kernel,
        out_shape=jax.ShapeDtypeStruct((1, cols), jnp.float32),
        grid=(cols // unit,),
        in_specs=[
            pl.BlockSpec((rows, unit), lambda j: (0, j)),
            pl.BlockSpec((rows, rank), lambda j: (0, 0)),
            pl.BlockSpec((rank, unit), lambda j: (0, first + j)),
        ],
        out_specs=pl.BlockSpec((1, unit), lambda j: (0, j)),
        compiler_params=pltpu.CompilerParams(vmem_limit_bytes=40 * 2**20),
        cost_estimate=pl.CostEstimate(
            flops=2 * rows * cols * rank, bytes_accessed=2 * rows * cols, transcendentals=0
        ),
    )(piece, left, right)


def export_kernel(first, piece_ref, left_ref, right_ref, squares_ref, mag_ref, *rest):
    out_ref, scales_ref = rest[-2:]
    rows, cols = piece_ref.shape
    step = pl.program_id(0)
    if len(rest) > 2:
        @pl.when(step == 0)
        def _():
            scales_ref[...] = rest[1][...]

    factor = mag_ref[...] / jnp.sqrt(squares_ref[...] + EPSILON)
    lane = lax.broadcasted_iota(jnp.int32, (1, scales_ref.shape[1]), 1)
    per_step = cols // BLOCK
    for i in range(rows // BLOCK):
        span = pl.ds(i * BLOCK, BLOCK)
        low_rank = jnp.dot(left_ref[span, :], right_ref[...], preferred_element_type=jnp.float32)
        combined = piece_ref[span, :].astype(jnp.float32) + low_rank
        merged = (combined * factor).astype(jnp.bfloat16).astype(jnp.float32)
        line = scales_ref[pl.ds(i, 1), :]
        for j in range(per_step):
            tile = merged[:, j * BLOCK : (j + 1) * BLOCK]
            largest = jnp.max(jnp.max(jnp.abs(tile), axis=0, keepdims=True), axis=1, keepdims=True)
            out_ref[span, pl.ds(j * BLOCK, BLOCK)] = (tile * (1.0 / (largest + EPSILON))).astype(jnp.bfloat16)
            line = jnp.where(lane == (first + step) * per_step + j, largest, line)
        scales_ref[pl.ds(i, 1), :] = line


def export_chunk(piece, left, right, squares, mag, unit, first, previous):
    rows, cols = piece.shape
    rank, all_cols = right.shape
    scale_shape = (rows // BLOCK, all_cols // BLOCK)
    in_specs = [
        pl.BlockSpec((rows, unit), lambda j: (0, j)),
        pl.BlockSpec((rows, rank), lambda j: (0, 0)),
        pl.BlockSpec((rank, unit), lambda j: (0, first + j)),
        pl.BlockSpec((1, unit), lambda j: (0, j)),
        pl.BlockSpec((1, unit), lambda j: (0, first + j)),
    ]
    args = [piece, left, right, squares, mag]
    aliases = {}
    if previous is not None:
        in_specs += [pl.BlockSpec(memory_space=pl.ANY), pl.BlockSpec(scale_shape, lambda j: (0, 0))]
        args += list(previous)
        aliases = {5: 0, 6: 1}
    return pl.pallas_call(
        functools.partial(export_kernel, first),
        out_shape=(
            jax.ShapeDtypeStruct((rows, all_cols), jnp.bfloat16),
            jax.ShapeDtypeStruct(scale_shape, jnp.float32),
        ),
        grid=(cols // unit,),
        in_specs=in_specs,
        out_specs=(
            pl.BlockSpec((rows, unit), lambda j: (0, first + j)),
            pl.BlockSpec(scale_shape, lambda j: (0, 0)),
        ),
        input_output_aliases=aliases,
        compiler_params=pltpu.CompilerParams(vmem_limit_bytes=40 * 2**20),
        cost_estimate=pl.CostEstimate(
            flops=2 * rows * cols * rank, bytes_accessed=4 * rows * cols, transcendentals=0
        ),
    )(*args)


def body(tp, base_weight, left_factor, right_factor, magnitude):
    rows, rank = left_factor.shape
    cols = right_factor.shape[1]
    blocks = cols // BLOCK
    unit = max(d for d in (4, 2, 1) if blocks % d == 0) * BLOCK
    left = lax.all_gather(left_factor, "tp", axis=0, tiled=True)
    left, base_weight = lax.optimization_barrier((left, base_weight))
    mag = lax.dynamic_slice_in_dim(magnitude, lax.axis_index("tp") * cols, cols, 0).reshape(1, cols)
    result = squares = None
    for a, b in chunk_units(cols // unit, PARTS):
        packed = pack(base_weight, tp, unit, a, b - a)
        piece = lax.all_to_all(packed, "tp", split_axis=0, concat_axis=0, tiled=True)
        local = column_squares(piece, left, right_factor, unit, a)
        if squares is not None:
            local, _ = lax.optimization_barrier((local, squares))
        squares = lax.psum(local, "fsdp")
        result = export_chunk(piece, left, right_factor, squares, mag, unit, a, result)
    return result


def solution(mesh):
    in_specs = (P(("fsdp", "tp"), None), P(("fsdp", "tp"), None), P(None, "tp"), P())
    out_specs = (P("fsdp", "tp"), P("fsdp", "tp"))
    return jax.shard_map(
        functools.partial(body, mesh.shape["tp"]), mesh=mesh, in_specs=in_specs, out_specs=out_specs, check_vma=False
    )
```

```python
import functools

import jax
import jax.numpy as jnp
from jax import lax
from jax.experimental import pallas as pl
from jax.experimental.pallas import tpu as pltpu
from jax.sharding import PartitionSpec as P

BLOCK = 128
EPSILON = 1e-06
PARTS = (1, 2, 2, 2, 2, 2, 1, 1)
LATE = 2
AHEAD = 2
PARAMS = pltpu.CompilerParams(vmem_limit_bytes=56 * 2**20)


def chunk_units(total, parts):
    bounds = [0]
    whole = sum(parts)
    for i in range(len(parts)):
        bounds.append(round(total * sum(parts[: i + 1]) / whole))
    return [(a, b) for a, b in zip(bounds, bounds[1:]) if b > a]


def after(value, *others):
    return lax.optimization_barrier((value, *others))[0]


def exchange(arrays, tp):
    return [
        lax.ppermute(array, "tp", [(i, i ^ d) for i in range(tp)])
        for d, array in zip(range(1, tp), arrays)
    ]


def copy_kernel(me_ref, *refs):
    half = len(refs) // 2
    for source, target in zip(refs[:half], refs[half:]):
        target[...] = source[...]


def pack(me, base, tp, unit, first, count):
    rows = base.shape[0]
    group = base.shape[1] // (tp * unit)

    def source(d):
        return pl.BlockSpec((rows, unit), lambda j, me: (0, (me[0] ^ d) * group + first + j))

    return pl.pallas_call(
        copy_kernel,
        out_shape=[jax.ShapeDtypeStruct((rows, count * unit), base.dtype)] * (tp - 1),
        grid_spec=pltpu.PrefetchScalarGridSpec(
            num_scalar_prefetch=1,
            grid=(count,),
            in_specs=[source(d) for d in range(1, tp)],
            out_specs=[pl.BlockSpec((rows, unit), lambda j, me: (0, j))] * (tp - 1),
        ),
        compiler_params=PARAMS,
        cost_estimate=pl.CostEstimate(
            flops=0, bytes_accessed=4 * (tp - 1) * rows * count * unit, transcendentals=0
        ),
    )(me, *[base] * (tp - 1))


def squares_of(piece_ref, left_ref, right_ref):
    rows, cols = piece_ref.shape
    step = min(rows, BLOCK)
    total = jnp.zeros((8, cols), jnp.float32)
    for r in range(0, rows, step):
        span = pl.ds(r, step)
        low_rank = jnp.dot(left_ref[span, :], right_ref[...], preferred_element_type=jnp.float32)
        combined = piece_ref[span, :].astype(jnp.float32) + low_rank
        total = total + jnp.sum((combined * combined).reshape(step // 8, 8, cols), axis=0)
    return total


def squares_kernel(tp, me_ref, *refs):
    pieces, lefts, right_ref, out_ref = refs[:tp], refs[tp : 2 * tp], refs[-2], refs[-1]
    total = sum(squares_of(piece, left, right_ref) for piece, left in zip(pieces, lefts))
    out_ref[...] = jnp.sum(total, axis=0, keepdims=True)


def sender_squares_kernel(tp, me_ref, *refs):
    pieces, left_ref, rights, outs = refs[:tp], refs[tp], refs[tp + 1 : 2 * tp + 1], refs[2 * tp + 1 :]
    for piece, right, out_ref in zip(pieces, rights, outs):
        out_ref[...] = jnp.sum(squares_of(piece, left_ref, right), axis=0, keepdims=True)


def own_spec(rows, unit, group, first):
    return pl.BlockSpec((rows, unit), lambda j, me: (0, me[0] * group + first + j))


def whole_spec(array):
    return pl.BlockSpec(array.shape, lambda j, me: (0, 0))


def chunk_spec(rows, unit):
    return pl.BlockSpec((rows, unit), lambda j, me: (0, j))


def matmul_cost(rows, cols, rank, passes):
    return pl.CostEstimate(
        flops=2 * rows * cols * rank, bytes_accessed=2 * passes * rows * cols, transcendentals=0
    )


def column_squares(me, base, received, lefts, right, unit, first, count):
    rows, rank = lefts[0].shape
    tp = len(lefts)
    group = right.shape[1] // unit
    return pl.pallas_call(
        functools.partial(squares_kernel, tp),
        out_shape=jax.ShapeDtypeStruct((1, count * unit), jnp.float32),
        grid_spec=pltpu.PrefetchScalarGridSpec(
            num_scalar_prefetch=1,
            grid=(count,),
            in_specs=[own_spec(rows, unit, group, first)]
            + [chunk_spec(rows, unit)] * (tp - 1)
            + [whole_spec(left) for left in lefts]
            + [pl.BlockSpec((rank, unit), lambda j, me: (0, first + j))],
            out_specs=chunk_spec(1, unit),
        ),
        compiler_params=PARAMS,
        cost_estimate=matmul_cost(tp * rows, count * unit, rank, 1),
    )(me, base, *received, *lefts, right)


def sender_squares(me, base, packed, left, right, rights, unit, first, count):
    rows, rank = left.shape
    tp = len(packed) + 1
    group = right.shape[1] // unit
    return pl.pallas_call(
        functools.partial(sender_squares_kernel, tp),
        out_shape=[jax.ShapeDtypeStruct((1, count * unit), jnp.float32)] * tp,
        grid_spec=pltpu.PrefetchScalarGridSpec(
            num_scalar_prefetch=1,
            grid=(count,),
            in_specs=[own_spec(rows, unit, group, first)]
            + [chunk_spec(rows, unit)] * (tp - 1)
            + [whole_spec(left), pl.BlockSpec((rank, unit), lambda j, me: (0, first + j))]
            + [chunk_spec(rank, unit)] * (tp - 1),
            out_specs=[chunk_spec(1, unit)] * tp,
        ),
        compiler_params=PARAMS,
        cost_estimate=matmul_cost(tp * rows, count * unit, rank, 1),
    )(me, base, *packed, left, right, *rights)


def export_kernel(tp, first, me_ref, *refs):
    pieces, lefts = refs[:tp], refs[tp : 2 * tp]
    right_ref, squares_ref, mag_ref = refs[2 * tp : 2 * tp + 3]
    out_ref, scales_ref = refs[-2:]
    rows, cols = pieces[0].shape
    step = pl.program_id(0)
    if len(refs) > 2 * tp + 5:
        @pl.when(step == 0)
        def _():
            scales_ref[...] = refs[2 * tp + 4][...]

    factor = mag_ref[...] / jnp.sqrt(squares_ref[...] + EPSILON)
    height = min(rows, BLOCK)
    for d in range(tp):
        start = (me_ref[0] ^ d) * rows
        for r in range(0, rows, height):
            low_rank = jnp.dot(lefts[d][pl.ds(r, height), :], right_ref[...], preferred_element_type=jnp.float32)
            combined = pieces[d][pl.ds(r, height), :].astype(jnp.float32) + low_rank
            span = pl.ds(pl.multiple_of(start + r, height), height)
            out_ref[span, :] = (combined * factor).astype(jnp.bfloat16)

    lane = lax.broadcasted_iota(jnp.int32, (1, scales_ref.shape[1]), 1)
    per_step = cols // BLOCK
    for i in range(tp * rows // BLOCK):
        span = pl.ds(i * BLOCK, BLOCK)
        line = scales_ref[pl.ds(i, 1), :]
        for j in range(per_step):
            tile = out_ref[span, pl.ds(j * BLOCK, BLOCK)].astype(jnp.float32)
            largest = jnp.max(jnp.max(jnp.abs(tile), axis=0, keepdims=True), axis=1, keepdims=True)
            out_ref[span, pl.ds(j * BLOCK, BLOCK)] = (tile * (1.0 / (largest + EPSILON))).astype(jnp.bfloat16)
            line = jnp.where(lane == (first + step) * per_step + j, largest, line)
        scales_ref[pl.ds(i, 1), :] = line


def export_chunk(me, base, received, lefts, right, squares, mag, unit, first, count, previous):
    rows, rank = lefts[0].shape
    tp = len(lefts)
    all_cols = right.shape[1]
    group = all_cols // unit
    result = (
        jax.ShapeDtypeStruct((tp * rows, all_cols), jnp.bfloat16),
        jax.ShapeDtypeStruct((tp * rows // BLOCK, all_cols // BLOCK), jnp.float32),
    )
    in_specs = (
        [own_spec(rows, unit, group, first)]
        + [chunk_spec(rows, unit)] * (tp - 1)
        + [whole_spec(left) for left in lefts]
        + [
            pl.BlockSpec((rank, unit), lambda j, me: (0, first + j)),
            chunk_spec(1, unit),
            own_spec(1, unit, group, first),
        ]
    )
    args = [base, *received, *lefts, right, squares, mag]
    aliases = {}
    if previous is not None:
        in_specs += [pl.BlockSpec(memory_space=pl.ANY), whole_spec(previous[1])]
        args += list(previous)
        aliases = {len(args) - 1: 0}
    return pl.pallas_call(
        functools.partial(export_kernel, tp, first),
        out_shape=result,
        grid_spec=pltpu.PrefetchScalarGridSpec(
            num_scalar_prefetch=1,
            grid=(count,),
            in_specs=in_specs,
            out_specs=(pl.BlockSpec((tp * rows, unit), lambda j, me: (0, first + j)), whole_spec(result[1])),
        ),
        input_output_aliases=aliases,
        compiler_params=PARAMS,
        cost_estimate=matmul_cost(tp * rows, count * unit, rank, 2),
    )(me, *args)


def body(tp, base, left, right, magnitude):
    cols = right.shape[1]
    blocks = cols // BLOCK
    unit = max(d for d in (4, 2, 1) if blocks % d == 0) * BLOCK
    chunks = chunk_units(cols // unit, PARTS)
    mag = magnitude.reshape(1, -1)
    me = lax.axis_index("tp").astype(jnp.int32).reshape(1)
    early = len(chunks) - LATE

    lefts = [left] + exchange([left] * (tp - 1), tp)

    def send(k, me):
        a, b = chunks[k]
        return exchange(pack(me, base, tp, unit, a, b - a), tp)

    received = {}
    for k in range(AHEAD):
        received[k] = send(k, me)

    totals = {}
    packed = {}
    begin = after(me, received[0][0])
    for k in range(early, len(chunks)):
        a, b = chunks[k]
        packed[k] = pack(begin, base, tp, unit, a, b - a)
        rights = exchange([right[:, a * unit : b * unit]] * (tp - 1), tp)
        sums = sender_squares(begin, base, packed[k], left, right, rights, unit, a, b - a)
        totals[k] = sum(exchange(sums[1:], tp), sums[0])
    last = ()

    result = None
    scales = []
    for k in range(len(chunks)):
        a, b = chunks[k]
        following = k + AHEAD
        if following < len(chunks):
            done = list(received[k])
            if scales:
                done.append(scales[-1])
            done += last
            if following < early:
                received[following] = send(following, after(me, *done))
            else:
                sent = lax.optimization_barrier((*packed[following], *done))[: tp - 1]
                received[following] = exchange(sent, tp)
        if k < early:
            local = column_squares(me, base, received[k], lefts, right, unit, a, b - a)
            totals[k] = lax.psum(after(local, *last), "fsdp")
            last = (totals[k],)
        if k == 0:
            held = [after(totals[i], *last) for i in range(early, len(chunks))]
            last = lax.psum(tuple(held), "fsdp")
            totals.update({early + i: total for i, total in enumerate(last)})
        result = export_chunk(me, base, received[k], lefts, right, totals[k], mag, unit, a, b - a, result)
        scales.append(result[1])
    return result


def solution(mesh):
    in_specs = (P(("fsdp", "tp"), None), P(("fsdp", "tp"), None), P(None, "tp"), P())
    out_specs = (P("fsdp", "tp"), P("fsdp", "tp"))
    return jax.shard_map(
        functools.partial(body, mesh.shape["tp"]), mesh=mesh, in_specs=in_specs, out_specs=out_specs, check_vma=False
    )
```

```python
import functools

import jax
import jax.numpy as jnp
from jax import lax
from jax.experimental import pallas as pl
from jax.experimental.pallas import tpu as pltpu
from jax.sharding import PartitionSpec as P

BLOCK = 128
EPSILON = 1e-06
PARTS = (1, 2, 2, 2, 2, 2, 1, 1)
LATE = 2
AHEAD = 2
CARRIER = 3
TERMS = 3
SUMS_ROWS = 16
PARAMS = pltpu.CompilerParams(vmem_limit_bytes=56 * 2**20)


def chunk_units(total, parts):
    bounds = [0]
    whole = sum(parts)
    for i in range(len(parts)):
        bounds.append(round(total * sum(parts[: i + 1]) / whole))
    return [(a, b) for a, b in zip(bounds, bounds[1:]) if b > a]


def after(value, *others):
    return lax.optimization_barrier((value, *others))[0]


def swap(array, d, tp):
    return lax.ppermute(array, "tp", [(i, i ^ d) for i in range(tp)])


def copy_kernel(distances, me_ref, *refs):
    number = len(distances)
    outs = refs[-number:]
    rows = refs[0].shape[0]
    for i, d in enumerate(distances):
        outs[i][pl.ds(0, rows), :] = refs[i][...]
        if len(refs) > 2 * number:
            sums = refs[number][pl.ds(d, 1), :]
            height = outs[i].shape[0] - rows
            line = lax.broadcasted_iota(jnp.int32, (height, sums.shape[1]), 0)
            block = jnp.zeros((height, sums.shape[1]), jnp.float32)
            for term in range(TERMS):
                part = sums.astype(jnp.bfloat16).astype(jnp.float32)
                block = jnp.where(line == term, part, block)
                sums = sums - part
            outs[i][pl.ds(rows, height), :] = block.astype(jnp.bfloat16)


def group_spec(rows, unit, groups, first, d=0):
    return pl.BlockSpec((rows, unit), lambda j, me: (0, (me[0] ^ d) * groups + first + j))


def chunk_spec(rows, unit, first=0):
    return pl.BlockSpec((rows, unit), lambda j, me: (0, first + j))


def whole_spec(array):
    return pl.BlockSpec(array.shape, lambda j, me: (0, 0))


def cost(rows, cols, rank, passes):
    return pl.CostEstimate(
        flops=2 * rows * cols * rank, bytes_accessed=2 * passes * rows * cols, transcendentals=0
    )


def pack(me, base, tp, distances, unit, first, count, sums=None):
    rows = base.shape[0]
    groups = base.shape[1] // (tp * unit)
    number = len(distances)
    in_specs = [group_spec(rows, unit, groups, first, d) for d in distances]
    args = [base] * number
    height = rows
    if sums is not None:
        in_specs.append(chunk_spec(tp, unit))
        args.append(sums)
        height += SUMS_ROWS
    return pl.pallas_call(
        functools.partial(copy_kernel, distances),
        out_shape=[jax.ShapeDtypeStruct((height, count * unit), base.dtype)] * number,
        grid_spec=pltpu.PrefetchScalarGridSpec(
            num_scalar_prefetch=1,
            grid=(count,),
            in_specs=in_specs,
            out_specs=[chunk_spec(height, unit)] * number,
        ),
        compiler_params=PARAMS,
        cost_estimate=cost(number * rows, count * unit, 0, 2),
    )(me, *args)


def low_rank(extra_ref, start, height, right):
    left = extra_ref[pl.ds(0, right.shape[0]), pl.ds(start, height)]
    return lax.dot_general(left, right, (((0,), (0,)), ((), ())), preferred_element_type=jnp.float32)


def squares_of(piece_ref, extra_ref, right):
    rows, cols = piece_ref.shape
    height = min(rows, BLOCK)
    total = jnp.zeros((8, cols), jnp.float32)
    for r in range(0, rows, height):
        combined = piece_ref[pl.ds(r, height), :].astype(jnp.float32) + low_rank(extra_ref, r, height, right)
        total = total + jnp.sum((combined * combined).reshape(height // 8, 8, cols), axis=0)
    return total


def squares_kernel(tp, me_ref, *refs):
    pieces, extras, right_ref, out_ref = refs[:tp], refs[tp : 2 * tp], refs[-2], refs[-1]
    right = right_ref[...]
    total = sum(squares_of(piece, extra, right) for piece, extra in zip(pieces, extras))
    out_ref[...] = jnp.sum(total, axis=0, keepdims=True)


def sender_squares_kernel(tp, rank, me_ref, *refs):
    pieces, extras, out_ref = refs[:tp], refs[tp : 2 * tp], refs[-1]
    start = pl.multiple_of((1 + pl.program_id(0)) * rank, rank)
    for d in range(tp):
        right = extras[d][pl.ds(start, rank), :]
        total = squares_of(pieces[d], extras[0], right)
        out_ref[pl.ds(d, 1), :] = jnp.sum(total, axis=0, keepdims=True)


def column_squares(me, base, near, received, extras, right, unit, first, count):
    rows = base.shape[0]
    rank, cols = right.shape
    tp = len(extras)
    return pl.pallas_call(
        functools.partial(squares_kernel, tp),
        out_shape=jax.ShapeDtypeStruct((1, count * unit), jnp.float32),
        grid_spec=pltpu.PrefetchScalarGridSpec(
            num_scalar_prefetch=1,
            grid=(count,),
            in_specs=[group_spec(rows, unit, cols // unit, first), chunk_spec(rows, unit, first)]
            + [chunk_spec(rows, unit)] * (tp - 2)
            + [whole_spec(extra) for extra in extras]
            + [chunk_spec(rank, unit, first)],
            out_specs=chunk_spec(1, unit),
        ),
        compiler_params=PARAMS,
        cost_estimate=cost(tp * rows, count * unit, rank, 1),
    )(me, base, near, *received, *extras, right)


def sender_squares(me, base, extras, rank, unit, first, count):
    rows = base.shape[0]
    tp = len(extras)
    groups = base.shape[1] // (tp * unit)
    return pl.pallas_call(
        functools.partial(sender_squares_kernel, tp, rank),
        out_shape=jax.ShapeDtypeStruct((tp, count * unit), jnp.float32),
        grid_spec=pltpu.PrefetchScalarGridSpec(
            num_scalar_prefetch=1,
            grid=(count,),
            in_specs=[group_spec(rows, unit, groups, first, d) for d in range(tp)]
            + [whole_spec(extra) for extra in extras],
            out_specs=chunk_spec(tp, unit),
        ),
        compiler_params=PARAMS,
        cost_estimate=cost(tp * rows, count * unit, rank, 1),
    )(me, *[base] * tp, *extras)


def export_kernel(tp, first, me_ref, *refs):
    pieces, extras = refs[:tp], refs[tp : 2 * tp]
    right_ref, squares_ref, mag_ref = refs[2 * tp : 2 * tp + 3]
    out_ref, scales_ref = refs[-2:]
    rows, cols = pieces[0].shape
    step = pl.program_id(0)
    if len(refs) > 2 * tp + 5:
        @pl.when(step == 0)
        def _():
            scales_ref[...] = refs[2 * tp + 4][...]

    factor = mag_ref[...] / jnp.sqrt(squares_ref[...] + EPSILON)
    right = right_ref[...]
    height = min(rows, BLOCK)
    for d in range(tp):
        start = (me_ref[0] ^ d) * rows
        for r in range(0, rows, height):
            combined = pieces[d][pl.ds(r, height), :].astype(jnp.float32) + low_rank(extras[d], r, height, right)
            span = pl.ds(pl.multiple_of(start + r, height), height)
            out_ref[span, :] = (combined * factor).astype(jnp.bfloat16)

    lane = lax.broadcasted_iota(jnp.int32, (1, scales_ref.shape[1]), 1)
    per_step = cols // BLOCK
    for i in range(tp * rows // BLOCK):
        span = pl.ds(i * BLOCK, BLOCK)
        line = scales_ref[pl.ds(i, 1), :]
        for j in range(per_step):
            tile = out_ref[span, pl.ds(j * BLOCK, BLOCK)].astype(jnp.float32)
            largest = jnp.max(jnp.max(jnp.abs(tile), axis=0, keepdims=True), axis=1, keepdims=True)
            out_ref[span, pl.ds(j * BLOCK, BLOCK)] = (tile * (1.0 / (largest + EPSILON))).astype(jnp.bfloat16)
            line = jnp.where(lane == (first + step) * per_step + j, largest, line)
        scales_ref[pl.ds(i, 1), :] = line


def export_chunk(me, base, near, received, extras, right, squares, mag, unit, first, count, previous):
    rows = base.shape[0]
    rank, cols = right.shape
    tp = len(extras)
    groups = cols // unit
    result = (
        jax.ShapeDtypeStruct((tp * rows, cols), jnp.bfloat16),
        jax.ShapeDtypeStruct((tp * rows // BLOCK, cols // BLOCK), jnp.float32),
    )
    in_specs = (
        [group_spec(rows, unit, groups, first), chunk_spec(rows, unit, first)]
        + [chunk_spec(rows, unit)] * (tp - 2)
        + [whole_spec(extra) for extra in extras]
        + [chunk_spec(rank, unit, first), chunk_spec(1, unit), group_spec(1, unit, groups, first)]
    )
    args = [base, near, *received, *extras, right, squares, mag]
    aliases = {}
    if previous is not None:
        in_specs += [pl.BlockSpec(memory_space=pl.ANY), whole_spec(previous[1])]
        args += list(previous)
        aliases = {len(args) - 1: 0}
    return pl.pallas_call(
        functools.partial(export_kernel, tp, first),
        out_shape=result,
        grid_spec=pltpu.PrefetchScalarGridSpec(
            num_scalar_prefetch=1,
            grid=(count,),
            in_specs=in_specs,
            out_specs=(chunk_spec(tp * rows, unit, first), whole_spec(result[1])),
        ),
        input_output_aliases=aliases,
        compiler_params=PARAMS,
        cost_estimate=cost(tp * rows, count * unit, rank, 2),
    )(me, *args)


def body(tp, base, left, right, magnitude):
    rows, rank = left.shape
    cols = right.shape[1]
    blocks = cols // BLOCK
    unit = max(d for d in (4, 2, 1) if blocks % d == 0) * BLOCK
    chunks = chunk_units(cols // unit, PARTS)
    mag = magnitude.reshape(1, -1)
    me = lax.axis_index("tp").astype(jnp.int32).reshape(1)
    early = len(chunks) - LATE
    late_first = chunks[early][0]
    late_count = chunks[-1][1] - late_first
    far = range(2, tp)

    late_right = [right[:, u * unit : (u + 1) * unit] for u in range(late_first, late_first + late_count)]
    own = jnp.concatenate([jnp.pad(left.T, ((0, 0), (0, unit - rows)))] + late_right)
    me_first = after(me, own)
    extras = [own, swap(own, 1, tp)]
    for d in far:
        extras.append(swap(extras[d - 1], 1, tp) if d % 2 else swap(own, d, tp))

    received = {}

    def send(k, me, sums=None):
        a, b = chunks[k]
        packed = pack(me, base, tp, far, unit, a, b - a, sums)
        if k == 1:
            packed = lax.optimization_barrier((*packed, *received[0]))[: len(far)]
        received[k] = [swap(piece, d, tp) for d, piece in zip(far, packed)]
        return packed

    first = send(0, me_first)
    second = send(1, after(me, *first))
    near = pack(after(me, *second), base, tp, (1,), unit, 0, cols // unit)[0]
    near = swap(after(near, extras[-1]), 1, tp)

    result = None
    last = ()
    totals = {}
    for k in range(len(chunks)):
        a, b = chunks[k]
        following = k + AHEAD
        if following < len(chunks):
            token = last if result is None else (*last, result[1])
            turn = after(me, *received[k], *token)
            sums = None
            if following == CARRIER:
                sums = sender_squares(turn, base, extras, rank, unit, late_first, late_count)
                late = sums[:1] + swap(sums[1:2], 1, tp)
            send(following, turn, sums)
        if k < early:
            local = after(column_squares(me, base, near, received[k], extras, right, unit, a, b - a), *last)
            if k == CARRIER:
                for piece in received[k]:
                    terms = piece[rows : rows + TERMS].astype(jnp.float32)
                    late = late + jnp.sum(terms, axis=0, keepdims=True)
                totals[k], late = lax.psum((local, late), "fsdp")
                for i in range(early, len(chunks)):
                    start, end = ((u - late_first) * unit for u in chunks[i])
                    totals[i] = late[:, start:end]
            else:
                totals[k] = lax.psum(local, "fsdp")
            last = (totals[k],)
        width = unit if k < early else max(unit // 2, BLOCK)
        parts = unit // width
        result = export_chunk(
            me, base, near, received[k], extras, right, totals[k], mag, width, a * parts, (b - a) * parts, result
        )
    return result


def solution(mesh):
    in_specs = (P(("fsdp", "tp"), None), P(("fsdp", "tp"), None), P(None, "tp"), P())
    out_specs = (P("fsdp", "tp"), P("fsdp", "tp"))
    return jax.shard_map(
        functools.partial(body, mesh.shape["tp"]), mesh=mesh, in_specs=in_specs, out_specs=out_specs, check_vma=False
    )
```

```python
import functools

import jax
import jax.numpy as jnp
from jax import lax
from jax.experimental import pallas as pl
from jax.experimental.pallas import tpu as pltpu
from jax.sharding import PartitionSpec as P

BLOCK = 128
EPSILON = 1e-06
PARTS = (3, 3, 3, 2, 1, 1)
LATE = 2
AHEAD = 2
SCALE = 3
CARRIER = 3
TERMS = 3
SUMS_ROWS = 16
PARAMS = pltpu.CompilerParams(vmem_limit_bytes=56 * 2**20)


def chunk_units(total, parts):
    bounds = [0]
    whole = sum(parts)
    for i in range(len(parts)):
        bounds.append(round(total * sum(parts[: i + 1]) / whole))
    return [(a, b) for a, b in zip(bounds, bounds[1:]) if b > a]


def after(value, *others):
    return lax.optimization_barrier((value, *others))[0]


def swap(array, d, tp):
    return lax.ppermute(array, "tp", [(i, i ^ d) for i in range(tp)])


def copy_kernel(number, me_ref, *refs):
    for source, target in zip(refs[:number], refs[number:]):
        target[...] = source[...]


def first_kernel(far, me_ref, *refs):
    pieces, (left, right), outs = refs[: len(far)], refs[len(far) : len(far) + 2], refs[len(far) + 2 :]
    own = outs[-1]
    rows = pieces[0].shape[0]
    step = pl.program_id(0)

    @pl.when(step == 0)
    def _():
        if left.shape[1] < own.shape[1]:
            own[...] = jnp.zeros_like(own)
        own[:, pl.ds(0, left.shape[1])] = left[...]

    @pl.when(step > 0)
    def _():
        own[...] = right[...]

    for d, piece, out in zip(far, pieces, outs):
        out[pl.ds(0, rows), :] = piece[...]
        if d % 2 == 0:
            out[pl.ds(rows, own.shape[0]), :] = own[...]


def carrier_kernel(far, me_ref, *refs):
    pieces, sums_ref, outs = refs[: len(far)], refs[len(far)], refs[len(far) + 1 :]
    rows, cols = pieces[0].shape
    line = lax.broadcasted_iota(jnp.int32, (SUMS_ROWS, cols), 0)
    for d, piece, out in zip(far, pieces, outs):
        out[pl.ds(0, rows), :] = piece[...]
        rest = sums_ref[pl.ds(d, 1), :]
        block = jnp.zeros((SUMS_ROWS, cols), jnp.float32)
        for term in range(TERMS):
            part = rest.astype(jnp.bfloat16).astype(jnp.float32)
            block = jnp.where(line == term, part, block)
            rest = rest - part
        out[pl.ds(rows, SUMS_ROWS), :] = block.astype(jnp.bfloat16)


def group_spec(rows, unit, groups, first, d=0):
    return pl.BlockSpec((rows, unit), lambda j, me: (0, (me[0] ^ d) * groups + first + j))


def chunk_spec(rows, unit, first=0):
    return pl.BlockSpec((rows, unit), lambda j, me: (0, first + j))


def left_spec(rank, unit):
    return pl.BlockSpec((rank, unit), lambda j, me: (0, 0))


def whole_spec(array):
    return pl.BlockSpec(array.shape, lambda j, me: (0, 0))


def cost(rows, cols, rank, passes):
    return pl.CostEstimate(
        flops=2 * rows * cols * rank // SCALE, bytes_accessed=2 * passes * rows * cols // SCALE, transcendentals=0
    )


def pack(me, base, tp, distances, unit, first, count):
    rows = base.shape[0]
    groups = base.shape[1] // (tp * unit)
    number = len(distances)
    return pl.pallas_call(
        functools.partial(copy_kernel, number),
        out_shape=[jax.ShapeDtypeStruct((rows, count * unit), base.dtype)] * number,
        grid_spec=pltpu.PrefetchScalarGridSpec(
            num_scalar_prefetch=1,
            grid=(count,),
            in_specs=[group_spec(rows, unit, groups, first, d) for d in distances],
            out_specs=[chunk_spec(rows, unit)] * number,
        ),
        compiler_params=PARAMS,
        cost_estimate=cost(number * rows, count * unit, 0, 2),
    )(me, *[base] * number)


def pack_near(me, base, tp):
    rows = base.shape[0]
    cols = base.shape[1] // tp
    height = max(rows // 4, 16)
    steps = rows // height
    return pl.pallas_call(
        functools.partial(copy_kernel, 1),
        out_shape=jax.ShapeDtypeStruct((2 * rows, cols), base.dtype),
        grid_spec=pltpu.PrefetchScalarGridSpec(
            num_scalar_prefetch=1,
            grid=(2, steps),
            in_specs=[pl.BlockSpec((height, cols), lambda s, i, me: (i, (me[0] // 2) * 2 + s))],
            out_specs=pl.BlockSpec((height, cols), lambda s, i, me: (s * steps + i, 0)),
        ),
        compiler_params=PARAMS,
        cost_estimate=cost(rows, cols, 0, 2),
    )(me, base)


def near_spec(rows, unit, first):
    return pl.BlockSpec((rows, unit), lambda j, me: ((me[0] % 2) ^ 1, first + j))


def pack_first(me, base, tp, far, left, right, unit, late):
    rows, rank = left.shape
    groups = base.shape[1] // (tp * unit)
    count = 1 + len(late)
    shapes = [(rows + (rank if d % 2 == 0 else 0), unit) for d in far] + [(rank, unit)]
    return pl.pallas_call(
        functools.partial(first_kernel, far),
        out_shape=[jax.ShapeDtypeStruct((height, count * unit), base.dtype) for height, _ in shapes],
        grid_spec=pltpu.PrefetchScalarGridSpec(
            num_scalar_prefetch=1,
            grid=(count,),
            in_specs=[group_spec(rows, unit, groups, 0, d) for d in far]
            + [left_spec(rank, rows), chunk_spec(rank, unit, late[0] - 1)],
            out_specs=[chunk_spec(*shape) for shape in shapes],
        ),
        compiler_params=PARAMS,
        cost_estimate=cost(len(far) * rows, count * unit, 0, 2),
    )(me, *[base] * len(far), left.T, right)


def pack_carrier(me, base, tp, far, sums, unit, first, count):
    rows = base.shape[0]
    groups = base.shape[1] // (tp * unit)
    width = sums.shape[1] // unit
    return pl.pallas_call(
        functools.partial(carrier_kernel, far),
        out_shape=[jax.ShapeDtypeStruct((rows + SUMS_ROWS, count * unit), base.dtype)] * len(far),
        grid_spec=pltpu.PrefetchScalarGridSpec(
            num_scalar_prefetch=1,
            grid=(count,),
            in_specs=[group_spec(rows, unit, groups, first, d) for d in far]
            + [pl.BlockSpec((tp, unit), lambda j, me: (0, jnp.minimum(j, width - 1)))],
            out_specs=[chunk_spec(rows + SUMS_ROWS, unit)] * len(far),
        ),
        compiler_params=PARAMS,
        cost_estimate=cost(len(far) * rows, count * unit, 0, 2),
    )(me, *[base] * len(far), sums)


def low_rank(extra_ref, start, height, right):
    left = extra_ref[pl.ds(0, right.shape[0]), pl.ds(start, height)]
    return lax.dot_general(left, right, (((0,), (0,)), ((), ())), preferred_element_type=jnp.float32)


def squares_of(piece_ref, extra_ref, right):
    rows, cols = piece_ref.shape
    height = min(rows, BLOCK)
    total = jnp.zeros((8, cols), jnp.float32)
    for r in range(0, rows, height):
        combined = piece_ref[pl.ds(r, height), :].astype(jnp.float32) + low_rank(extra_ref, r, height, right)
        total = total + jnp.sum((combined * combined).reshape(height // 8, 8, cols), axis=0)
    return total


def squares_kernel(tp, me_ref, *refs):
    pieces, extras, right_ref, out_ref = refs[:tp], refs[tp : 2 * tp], refs[-2], refs[-1]
    right = right_ref[...]
    total = sum(squares_of(piece, extra, right) for piece, extra in zip(pieces, extras))
    out_ref[...] = jnp.sum(total, axis=0, keepdims=True)


def sender_squares_kernel(tp, me_ref, *refs):
    pieces, rights, left, out_ref = refs[:tp], refs[tp : 2 * tp], refs[-2], refs[-1]
    for d in range(tp):
        total = squares_of(pieces[d], left, rights[d][...])
        out_ref[pl.ds(d, 1), :] = jnp.sum(total, axis=0, keepdims=True)


def column_squares(me, base, near, received, extras, right, unit, first, count):
    rows = base.shape[0]
    rank, cols = right.shape
    tp = len(extras)
    return pl.pallas_call(
        functools.partial(squares_kernel, tp),
        out_shape=jax.ShapeDtypeStruct((1, count * unit), jnp.float32),
        grid_spec=pltpu.PrefetchScalarGridSpec(
            num_scalar_prefetch=1,
            grid=(count,),
            in_specs=[group_spec(rows, unit, cols // unit, first), near_spec(rows, unit, first)]
            + [chunk_spec(rows, unit)] * (tp - 2)
            + [left_spec(rank, max(rows, BLOCK))] * tp
            + [chunk_spec(rank, unit, first)],
            out_specs=chunk_spec(1, unit),
        ),
        compiler_params=PARAMS,
        cost_estimate=cost(tp * rows, count * unit, rank, 1),
    )(me, base, near, *received, *extras, right)


def sender_squares(me, base, extras, rank, unit, first, count):
    rows = base.shape[0]
    tp = len(extras)
    groups = base.shape[1] // (tp * unit)
    return pl.pallas_call(
        functools.partial(sender_squares_kernel, tp),
        out_shape=jax.ShapeDtypeStruct((tp, count * unit), jnp.float32),
        grid_spec=pltpu.PrefetchScalarGridSpec(
            num_scalar_prefetch=1,
            grid=(count,),
            in_specs=[group_spec(rows, unit, groups, first, d) for d in range(tp)]
            + [chunk_spec(rank, unit, 1)] * tp
            + [left_spec(rank, unit)],
            out_specs=chunk_spec(tp, unit),
        ),
        compiler_params=PARAMS,
        cost_estimate=cost(tp * rows, count * unit, rank, 1),
    )(me, *[base] * tp, *extras, extras[0])


def export_kernel(tp, first, me_ref, *refs):
    pieces, extras = refs[:tp], refs[tp : 2 * tp]
    right_ref, squares_ref, mag_ref = refs[2 * tp : 2 * tp + 3]
    out_ref, scales_ref = refs[-2:]
    rows, cols = pieces[0].shape
    step = pl.program_id(0)
    if len(refs) > 2 * tp + 5:
        @pl.when(step == 0)
        def _():
            scales_ref[...] = refs[2 * tp + 4][...]

    factor = mag_ref[...] / jnp.sqrt(squares_ref[...] + EPSILON)
    right = right_ref[...]
    height = min(rows, BLOCK)
    for d in range(tp):
        start = (me_ref[0] ^ d) * rows
        for r in range(0, rows, height):
            combined = pieces[d][pl.ds(r, height), :].astype(jnp.float32) + low_rank(extras[d], r, height, right)
            span = pl.ds(pl.multiple_of(start + r, height), height)
            out_ref[span, :] = (combined * factor).astype(jnp.bfloat16)

    lane = lax.broadcasted_iota(jnp.int32, (1, scales_ref.shape[1]), 1)
    per_step = cols // BLOCK
    for i in range(tp * rows // BLOCK):
        span = pl.ds(i * BLOCK, BLOCK)
        line = scales_ref[pl.ds(i, 1), :]
        for j in range(per_step):
            tile = out_ref[span, pl.ds(j * BLOCK, BLOCK)].astype(jnp.float32)
            largest = jnp.max(jnp.max(jnp.abs(tile), axis=0, keepdims=True), axis=1, keepdims=True)
            out_ref[span, pl.ds(j * BLOCK, BLOCK)] = (tile * (1.0 / (largest + EPSILON))).astype(jnp.bfloat16)
            line = jnp.where(lane == (first + step) * per_step + j, largest, line)
        scales_ref[pl.ds(i, 1), :] = line


def export_chunk(me, base, near, received, extras, right, squares, mag, unit, first, count, previous):
    rows = base.shape[0]
    rank, cols = right.shape
    tp = len(extras)
    groups = cols // unit
    result = (
        jax.ShapeDtypeStruct((tp * rows, cols), jnp.bfloat16),
        jax.ShapeDtypeStruct((tp * rows // BLOCK, cols // BLOCK), jnp.float32),
    )
    in_specs = (
        [group_spec(rows, unit, groups, first), near_spec(rows, unit, first)]
        + [chunk_spec(rows, unit)] * (tp - 2)
        + [left_spec(rank, max(rows, BLOCK))] * tp
        + [chunk_spec(rank, unit, first), chunk_spec(1, unit), group_spec(1, unit, groups, first)]
    )
    args = [base, near, *received, *extras, right, squares, mag]
    aliases = {}
    if previous is not None:
        in_specs += [pl.BlockSpec(memory_space=pl.ANY), whole_spec(previous[1])]
        args += list(previous)
        aliases = {len(args) - 1: 0}
    return pl.pallas_call(
        functools.partial(export_kernel, tp, first),
        out_shape=result,
        grid_spec=pltpu.PrefetchScalarGridSpec(
            num_scalar_prefetch=1,
            grid=(count,),
            in_specs=in_specs,
            out_specs=(chunk_spec(tp * rows, unit, first), whole_spec(result[1])),
        ),
        input_output_aliases=aliases,
        compiler_params=PARAMS,
        cost_estimate=cost(tp * rows, count * unit, rank, 2),
    )(me, *args)


def body(tp, base, left, right, magnitude):
    rows, rank = left.shape
    cols = right.shape[1]
    blocks = cols // BLOCK
    unit = max(d for d in (4, 2, 1) if blocks % d == 0) * BLOCK
    chunks = chunk_units(cols // unit, PARTS)
    mag = magnitude.reshape(1, -1)
    me = lax.axis_index("tp").astype(jnp.int32).reshape(1)
    early = len(chunks) - LATE
    late = range(chunks[early][0], chunks[-1][1])
    far = range(2, tp)
    received = {}

    def send(k, pieces):
        received[k] = [swap(piece, d, tp) for d, piece in zip(far, pieces)]

    *pieces, own = pack_first(me, base, tp, far, left, right, unit, late)
    send(0, pieces)
    a, b = chunks[1]
    pieces = pack(after(me, own), base, tp, far, unit, a, b - a)
    send(1, pieces)
    near = lax.all_to_all(
        pack_near(after(me, *pieces), base, tp), "tp", 0, 0, tiled=True,
        axis_index_groups=[[i, i + 1] for i in range(0, tp, 2)],
    )

    even = [own] + [received[0][d - 2][rows:] for d in far[::2]]
    odd = swap(jnp.concatenate(even), 1, tp)
    extras = []
    for i in range(tp // 2):
        extras += [even[i], odd[i * rank : (i + 1) * rank]]

    result = None
    token = ()
    totals = {}
    waiting = []
    for k, (a, b) in enumerate(chunks):
        following = k + AHEAD
        if following < len(chunks):
            c, d = chunks[following]
            turn = after(me, *received[k], *token)
            if following == CARRIER:
                sums = sender_squares(turn, base, extras, rank, unit, late[0], len(late))
                late_sums = sums[:1] + swap(sums[1:2], 1, tp)
                send(following, pack_carrier(turn, base, tp, far, sums, unit, c, d - c))
            else:
                send(following, pack(turn, base, tp, far, unit, c, d - c))
        waiting.append(k)
        parts = [i for i in waiting if i < early]
        if parts:
            turn = after(me, *token)
            local = [
                column_squares(turn, base, near, received[i], extras, right, unit, chunks[i][0], chunks[i][1] - chunks[i][0])
                for i in parts
            ]
            if k == CARRIER:
                for piece in received[k]:
                    terms = after(piece, *token)[rows : rows + TERMS, : late_sums.shape[1]].astype(jnp.float32)
                    late_sums = late_sums + jnp.sum(terms, axis=0, keepdims=True)
                local.append(late_sums)
                parts += range(early, len(chunks))
            local = jnp.concatenate(local, axis=1)
            total = lax.psum(local, "fsdp")
            start = 0
            for i in parts:
                end = start + (chunks[i][1] - chunks[i][0]) * unit
                totals[i] = total[:, start:end]
                start = end
        for i in waiting:
            c, d = chunks[i]
            result = export_chunk(me, base, near, received[i], extras, right, totals[i], mag, unit, c, d - c, result)
        waiting = []
        token = (result[1],)
    return result


def solution(mesh):
    in_specs = (P(("fsdp", "tp"), None), P(("fsdp", "tp"), None), P(None, "tp"), P())
    out_specs = (P("fsdp", "tp"), P("fsdp", "tp"))
    return jax.shard_map(
        functools.partial(body, mesh.shape["tp"]), mesh=mesh, in_specs=in_specs, out_specs=out_specs, check_vma=False
    )
```

```python
import functools

import jax
import jax.numpy as jnp
from jax import lax
from jax.experimental import pallas as pl
from jax.experimental.pallas import tpu as pltpu
from jax.sharding import PartitionSpec as P

BLOCK = 128
EPSILON = 1e-06
EARLY = (8, 8, 8, 8, 8, 8)
LATE = (4,)
AHEAD = 2
SCALE = 3
CARRIER = 3
TERMS = 3
SUMS_ROWS = 16
PARAMS = pltpu.CompilerParams(vmem_limit_bytes=52 * 2**20)
MOVE_PARAMS = pltpu.CompilerParams(vmem_limit_bytes=56 * 2**20)


def chunk_blocks(total):
    parts = EARLY + LATE
    bounds = [total * sum(parts[:i]) // sum(parts) for i in range(len(parts) + 1)]
    chunks = [(a, b) for a, b in zip(bounds, bounds[1:]) if b > a]
    return chunks, sum(a < bounds[len(EARLY)] for a, _ in chunks)


def width_of(*counts):
    return max(d for d in (4, 2, 1) if all(count % d == 0 for count in counts))


def after(value, *others):
    return lax.optimization_barrier((value, *others))[0]


def swap(array, d, size, axis="tp"):
    return lax.ppermute(array, axis, [(i, i ^ d) for i in range(size)])


def total_of(array, size, axis):
    d = 1
    while d < size:
        array = array + swap(array, d, size, axis)
        d *= 2
    return array


def move_kernel(moves, number, me_ref, *refs):
    sources, targets, sems = refs[:number], refs[number:-1], refs[-1]
    copies = []
    for i, (source, row, col, rows, cols, target, to_row, to_col) in enumerate(moves(me_ref[0])):
        copies.append(
            pltpu.make_async_copy(
                sources[source].at[pl.ds(row, rows), pl.ds(col, cols)],
                targets[target].at[pl.ds(to_row, rows), pl.ds(to_col, cols)],
                sems.at[i],
            )
        )
    for copy in copies:
        copy.start()
    for copy in copies:
        copy.wait()


def move(me, arrays, shapes, moves):
    return pl.pallas_call(
        functools.partial(move_kernel, moves, len(arrays)),
        out_shape=[jax.ShapeDtypeStruct(shape, arrays[0].dtype) for shape in shapes],
        grid_spec=pltpu.PrefetchScalarGridSpec(
            num_scalar_prefetch=1,
            grid=(1,),
            in_specs=[pl.BlockSpec(memory_space=pl.ANY)] * len(arrays),
            out_specs=[pl.BlockSpec(memory_space=pl.ANY)] * len(shapes),
            scratch_shapes=[pltpu.SemaphoreType.DMA((len(moves(0)),))],
        ),
        compiler_params=MOVE_PARAMS,
        cost_estimate=cost(sum(rows * cols for rows, cols in shapes), 1, 0, 2),
    )(me, *arrays)


def parts_of(rows):
    height = rows // 4 if rows % (4 * BLOCK) == 0 else rows
    return [(r, height) for r in range(0, rows, height)]


def column_moves(me, rows, cols, group, first, target):
    col = pl.multiple_of(me * group + first, BLOCK)
    return [(0, r, col, height, cols, target, r, 0) for r, height in parts_of(rows)]


def group_spec(rows, unit, groups, first, d=0):
    return pl.BlockSpec((rows, unit), lambda j, me: (0, (me[0] ^ d) * groups + first + j))


def chunk_spec(rows, unit, first=0):
    return pl.BlockSpec((rows, unit), lambda j, me: (0, first + j))


def left_spec(rank, unit):
    return pl.BlockSpec((rank, unit), lambda j, me: (0, 0))


def whole_spec(array):
    return pl.BlockSpec(array.shape, lambda j, me: (0, 0))


def cost(rows, cols, rank, passes):
    return pl.CostEstimate(
        flops=2 * rows * cols * rank // SCALE, bytes_accessed=2 * passes * rows * cols // SCALE, transcendentals=0
    )


def pack(me, base, tp, distances, first, cols):
    rows, group = base.shape[0], base.shape[1] // tp

    def moves(me):
        return [m for i, d in enumerate(distances) for m in column_moves(me ^ d, rows, cols, group, first, i)]

    return move(me, [base], [(rows, cols)] * len(distances), moves)


def pack_first(me, base, tp, d, left, right, late, cols):
    rows, group = base.shape[0], base.shape[1] // tp
    rank, lane = left.shape
    late_cols = late[1] - late[0]

    def moves(me):
        extras = [
            (1, 0, 0, rank, lane, 0, rows, 0),
            (1, 0, 0, rank, lane, 1, 0, 0),
            (2, 0, late[0], rank, late_cols, 0, rows, lane),
            (2, 0, late[0], rank, late_cols, 1, 0, lane),
        ]
        return column_moves(me ^ d, rows, cols, group, 0, 0) + extras

    return move(me, [base, left, right], [(rows + rank, cols), (rank, lane + late_cols)], moves)


def pack_carrier(me, base, tp, distances, terms, first, cols):
    rows, group = base.shape[0], base.shape[1] // tp

    def moves(me):
        result = []
        for i, d in enumerate(distances):
            result += column_moves(me ^ d, rows, cols, group, first, i)
            result.append((1, d * SUMS_ROWS, 0, SUMS_ROWS, terms.shape[1], i, rows, 0))
        return result

    return move(me, [base, terms], [(rows + SUMS_ROWS, cols)] * len(distances), moves)


def pack_near(me, base, tp):
    rows, group = base.shape[0], base.shape[1] // tp

    def moves(me):
        result = []
        for s in range(2):
            for source, r, col, *rest in column_moves((me // 2) * 2 + s, rows, group, group, 0, 0):
                result.append((source, r, col, *rest[:-2], s * rows + r, 0))
        return result

    return move(me, [base], [(2 * rows, group)], moves)[0]


def near_spec(rows, unit, first):
    return pl.BlockSpec((rows, unit), lambda j, me: ((me[0] % 2) ^ 1, first + j))


def low_rank(extra_ref, start, height, right):
    left = extra_ref[pl.ds(0, right.shape[0]), pl.ds(start, height)]
    return lax.dot_general(left, right, (((0,), (0,)), ((), ())), preferred_element_type=jnp.float32)


def squares_of(piece_ref, extra_ref, right):
    rows, cols = piece_ref.shape
    height = min(rows, BLOCK)
    total = jnp.zeros((8, cols), jnp.float32)
    for r in range(0, rows, height):
        combined = piece_ref[pl.ds(r, height), :].astype(jnp.float32) + low_rank(extra_ref, r, height, right)
        total = total + jnp.sum((combined * combined).reshape(height // 8, 8, cols), axis=0)
    return total


def squares_kernel(tp, me_ref, *refs):
    pieces, extras, right_ref, out_ref = refs[:tp], refs[tp : 2 * tp], refs[-2], refs[-1]
    right = right_ref[...]
    total = sum(squares_of(piece, extra, right) for piece, extra in zip(pieces, extras))
    out_ref[...] = jnp.sum(total, axis=0, keepdims=True)


def sender_squares_kernel(tp, me_ref, *refs):
    pieces, rights, left, sums_ref, terms_ref = refs[:tp], refs[tp : 2 * tp], refs[-3], refs[-2], refs[-1]
    line = lax.broadcasted_iota(jnp.int32, (SUMS_ROWS, sums_ref.shape[1]), 0)
    for d in range(tp):
        sums = jnp.sum(squares_of(pieces[d], left, rights[d][...]), axis=0, keepdims=True)
        sums_ref[pl.ds(d, 1), :] = sums
        block = jnp.zeros(line.shape, jnp.float32)
        for term in range(TERMS):
            part = sums.astype(jnp.bfloat16).astype(jnp.float32)
            block = jnp.where(line == term, part, block)
            sums = sums - part
        terms_ref[pl.ds(d * SUMS_ROWS, SUMS_ROWS), :] = block.astype(jnp.bfloat16)


def column_squares(me, base, near, received, extras, right, unit, first, count):
    rows = base.shape[0]
    rank, cols = right.shape
    tp = len(extras)
    return pl.pallas_call(
        functools.partial(squares_kernel, tp),
        out_shape=jax.ShapeDtypeStruct((1, count * unit), jnp.float32),
        grid_spec=pltpu.PrefetchScalarGridSpec(
            num_scalar_prefetch=1,
            grid=(count,),
            in_specs=[group_spec(rows, unit, cols // unit, first), near_spec(rows, unit, first)]
            + [chunk_spec(rows, unit)] * (tp - 2)
            + [left_spec(rank, max(rows, BLOCK))] * tp
            + [chunk_spec(rank, unit, first)],
            out_specs=chunk_spec(1, unit),
        ),
        compiler_params=PARAMS,
        cost_estimate=cost(tp * rows, count * unit, rank, 1),
    )(me, base, near, *received, *extras, right)


def sender_squares(me, base, extras, rank, unit, first, count, lane):
    rows = base.shape[0]
    tp = len(extras)
    groups = base.shape[1] // (tp * unit)
    return pl.pallas_call(
        functools.partial(sender_squares_kernel, tp),
        out_shape=[
            jax.ShapeDtypeStruct((tp, count * unit), jnp.float32),
            jax.ShapeDtypeStruct((tp * SUMS_ROWS, count * unit), jnp.bfloat16),
        ],
        grid_spec=pltpu.PrefetchScalarGridSpec(
            num_scalar_prefetch=1,
            grid=(count,),
            in_specs=[group_spec(rows, unit, groups, first, d) for d in range(tp)]
            + [chunk_spec(rank, unit, lane // unit)] * tp
            + [left_spec(rank, lane)],
            out_specs=[chunk_spec(tp, unit), chunk_spec(tp * SUMS_ROWS, unit)],
        ),
        compiler_params=PARAMS,
        cost_estimate=cost(tp * rows, count * unit, rank, 1),
    )(me, *[base] * tp, *extras, extras[0])


def export_kernel(tp, first, me_ref, *refs):
    pieces, extras = refs[:tp], refs[tp : 2 * tp]
    right_ref, squares_ref, mag_ref = refs[2 * tp : 2 * tp + 3]
    out_ref, scales_ref = refs[-2:]
    rows, cols = pieces[0].shape
    step = pl.program_id(0)
    if len(refs) > 2 * tp + 5:
        @pl.when(step == 0)
        def _():
            scales_ref[...] = refs[2 * tp + 4][...]

    factor = mag_ref[...] / jnp.sqrt(squares_ref[...] + EPSILON)
    right = right_ref[...]
    height = min(rows, BLOCK)
    for d in range(tp):
        start = (me_ref[0] ^ d) * rows
        for r in range(0, rows, height):
            combined = pieces[d][pl.ds(r, height), :].astype(jnp.float32) + low_rank(extras[d], r, height, right)
            span = pl.ds(pl.multiple_of(start + r, height), height)
            out_ref[span, :] = (combined * factor).astype(jnp.bfloat16)

    lane = lax.broadcasted_iota(jnp.int32, (1, scales_ref.shape[1]), 1)
    per_step = cols // BLOCK
    for i in range(tp * rows // BLOCK):
        span = pl.ds(i * BLOCK, BLOCK)
        line = scales_ref[pl.ds(i, 1), :]
        for j in range(per_step):
            tile = out_ref[span, pl.ds(j * BLOCK, BLOCK)].astype(jnp.float32)
            largest = jnp.max(jnp.max(jnp.abs(tile), axis=0, keepdims=True), axis=1, keepdims=True)
            out_ref[span, pl.ds(j * BLOCK, BLOCK)] = (tile * (1.0 / (largest + EPSILON))).astype(jnp.bfloat16)
            line = jnp.where(lane == (first + step) * per_step + j, largest, line)
        scales_ref[pl.ds(i, 1), :] = line


def export_chunk(me, base, near, received, extras, right, squares, mag, unit, first, count, previous):
    rows = base.shape[0]
    rank, cols = right.shape
    tp = len(extras)
    groups = cols // unit
    result = (
        jax.ShapeDtypeStruct((tp * rows, cols), jnp.bfloat16),
        jax.ShapeDtypeStruct((tp * rows // BLOCK, cols // BLOCK), jnp.float32),
    )
    in_specs = (
        [group_spec(rows, unit, groups, first), near_spec(rows, unit, first)]
        + [chunk_spec(rows, unit)] * (tp - 2)
        + [left_spec(rank, max(rows, BLOCK))] * tp
        + [chunk_spec(rank, unit, first), chunk_spec(1, unit), group_spec(1, unit, groups, first)]
    )
    args = [base, near, *received, *extras, right, squares, mag]
    aliases = {}
    if previous is not None:
        in_specs += [pl.BlockSpec(memory_space=pl.ANY), whole_spec(previous[1])]
        args += list(previous)
        aliases = {len(args) - 1: 0}
    return pl.pallas_call(
        functools.partial(export_kernel, tp, first),
        out_shape=result,
        grid_spec=pltpu.PrefetchScalarGridSpec(
            num_scalar_prefetch=1,
            grid=(count,),
            in_specs=in_specs,
            out_specs=(chunk_spec(tp * rows, unit, first), whole_spec(result[1])),
        ),
        input_output_aliases=aliases,
        compiler_params=PARAMS,
        cost_estimate=cost(tp * rows, count * unit, rank, 2),
    )(me, *args)


def body(tp, fsdp, base, left, right, magnitude):
    rows, rank = left.shape
    cols = right.shape[1]
    blocks = cols // BLOCK
    chunks, early = chunk_blocks(blocks)
    mag = magnitude.reshape(1, -1)
    me = lax.axis_index("tp").astype(jnp.int32).reshape(1)
    lane = -(-rows // BLOCK) * BLOCK
    left = jnp.pad(left.T, ((0, 0), (0, lane - rows)))
    late = (chunks[early][0], chunks[-1][1])
    far = range(2, tp)
    received = {}

    def span(k):
        a, b = chunks[k]
        return a * BLOCK, (b - a) * BLOCK

    def units(k):
        a, b = chunks[k]
        width = width_of(a, b, blocks)
        return width * BLOCK, a // width, (b - a) // width

    def send(k, pieces):
        received[k] = [swap(piece, d, tp) for d, piece in zip(far, pieces)]

    pieces = []
    for d in far:
        if d % 2 == 0:
            piece, own = pack_first(me, base, tp, d, left, right, (late[0] * BLOCK, late[1] * BLOCK), span(0)[1])
        else:
            piece = pack(after(me, own), base, tp, (d,), *span(0))[0]
        pieces.append(piece)
    send(0, pieces)
    pieces = pack(after(me, *pieces), base, tp, far, *span(1))
    send(1, pieces)
    near = lax.all_to_all(
        pack_near(after(me, *pieces), base, tp), "tp", 0, 0, tiled=True,
        axis_index_groups=[[i, i + 1] for i in range(0, tp, 2)],
    )

    even = [own] + [received[0][d - 2][rows:, : own.shape[1]] for d in far[::2]]
    odd = swap(jnp.concatenate(even), 1, tp)
    extras = []
    for i in range(tp // 2):
        extras += [even[i], odd[i * rank : (i + 1) * rank]]

    result = None
    token = ()
    totals = {}
    for k in range(len(chunks)):
        following = k + AHEAD
        if following < len(chunks):
            turn = after(me, *received[k], *token)
            if following == CARRIER:
                width = width_of(late[0], late[1] - late[0], blocks, lane // BLOCK)
                sums, terms = sender_squares(
                    turn, base, extras, rank, width * BLOCK, late[0] // width, (late[1] - late[0]) // width, lane
                )
                late_sums = sums[:1] + swap(sums[1:2], 1, tp)
                send(following, pack_carrier(turn, base, tp, far, terms, *span(following)))
            else:
                send(following, pack(turn, base, tp, far, *span(following)))
        if k < early:
            local = column_squares(after(me, *token), base, near, received[k], extras, right, *units(k))
            if k == CARRIER:
                for piece in received[k]:
                    parts = after(piece, *token)[rows : rows + TERMS, : late_sums.shape[1]].astype(jnp.float32)
                    late_sums = late_sums + jnp.sum(parts, axis=0, keepdims=True)
                local = jnp.concatenate([local, late_sums], axis=1)
            total = lax.psum(local, "fsdp") if k < early - 1 else total_of(local, fsdp, "fsdp")
            totals[k] = total[:, : span(k)[1]]
            if k == CARRIER:
                for i in range(early, len(chunks)):
                    start = span(k)[1] + span(i)[0] - late[0] * BLOCK
                    totals[i] = total[:, start : start + span(i)[1]]
        result = export_chunk(me, base, near, received[k], extras, right, totals[k], mag, *units(k), result)
        token = (result[1],)
    return result


def solution(mesh):
    in_specs = (P(("fsdp", "tp"), None), P(("fsdp", "tp"), None), P(None, "tp"), P())
    out_specs = (P("fsdp", "tp"), P("fsdp", "tp"))
    return jax.shard_map(
        functools.partial(body, mesh.shape["tp"], mesh.shape["fsdp"]), mesh=mesh, in_specs=in_specs, out_specs=out_specs, check_vma=False
    )
```

```python
import functools

import jax
import jax.numpy as jnp
from jax import lax
from jax.experimental import pallas as pl
from jax.experimental.pallas import tpu as pltpu
from jax.sharding import PartitionSpec as P

BLOCK = 128
EPSILON = 1e-06
EARLY = (8, 8, 8, 8, 8, 8)
LATE = (4,)
AHEAD = 2
SCALE = 3
CARRIER = 3
TERMS = 3
SUMS_ROWS = 16
PARAMS = pltpu.CompilerParams(vmem_limit_bytes=52 * 2**20)
MOVE_PARAMS = pltpu.CompilerParams(vmem_limit_bytes=56 * 2**20)


def chunk_blocks(total):
    parts = EARLY + LATE
    bounds = [total * sum(parts[:i]) // sum(parts) for i in range(len(parts) + 1)]
    chunks = [(a, b) for a, b in zip(bounds, bounds[1:]) if b > a]
    return chunks, sum(a < bounds[len(EARLY)] for a, _ in chunks)


def width_of(*counts):
    return max(d for d in (4, 2, 1) if all(count % d == 0 for count in counts))


def after(value, *others):
    return lax.optimization_barrier((value, *others))[0]


def swap(array, d, size, axis="tp"):
    return lax.ppermute(array, axis, [(i, i ^ d) for i in range(size)])


def total_of(array, size, axis):
    d = 1
    while d < size:
        array = array + swap(array, d, size, axis)
        d *= 2
    return array


def move_kernel(moves, number, me_ref, *refs):
    plan = moves(me_ref[0])
    sources, targets = refs[:number], refs[number : -len(plan) - 2]
    holds, came, went = refs[-len(plan) - 2 : -2], refs[-2], refs[-1]
    ins, outs = [], []
    for i, (source, row, col, rows, cols, target, to_row, to_col) in enumerate(plan):
        block = sources[source].at[pl.ds(row, rows), pl.ds(col, cols)]
        place = targets[target].at[pl.ds(to_row, rows), pl.ds(to_col, cols)]
        ins.append(pltpu.make_async_copy(block, holds[i], came.at[i]))
        outs.append(pltpu.make_async_copy(holds[i], place, went.at[i]))
    for copy in ins:
        copy.start()
    for copy, onward in zip(ins, outs):
        copy.wait()
        onward.start()
    for copy in outs:
        copy.wait()


def move(me, arrays, shapes, moves):
    dtype = arrays[0].dtype
    plan = moves(0)
    return pl.pallas_call(
        functools.partial(move_kernel, moves, len(arrays)),
        out_shape=[jax.ShapeDtypeStruct(shape, dtype) for shape in shapes],
        grid_spec=pltpu.PrefetchScalarGridSpec(
            num_scalar_prefetch=1,
            grid=(1,),
            in_specs=[pl.BlockSpec(memory_space=pl.ANY)] * len(arrays),
            out_specs=[pl.BlockSpec(memory_space=pl.ANY)] * len(shapes),
            scratch_shapes=[pltpu.VMEM((rows, cols), dtype) for _, _, _, rows, cols, *_ in plan]
            + [pltpu.SemaphoreType.DMA((len(plan),))] * 2,
        ),
        compiler_params=MOVE_PARAMS,
        cost_estimate=cost(sum(rows * cols for rows, cols in shapes), 1, 0, 2),
    )(me, *arrays)


def parts_of(rows):
    height = rows // 4 if rows % (4 * BLOCK) == 0 else rows
    return [(r, height) for r in range(0, rows, height)]


def column_moves(me, rows, cols, group, first, target):
    col = pl.multiple_of(me * group + first, BLOCK)
    return [(0, r, col, height, cols, target, r, 0) for r, height in parts_of(rows)]


def group_spec(rows, unit, groups, first, d=0):
    return pl.BlockSpec((rows, unit), lambda j, me: (0, (me[0] ^ d) * groups + first + j))


def chunk_spec(rows, unit, first=0):
    return pl.BlockSpec((rows, unit), lambda j, me: (0, first + j))


def left_spec(rank, unit):
    return pl.BlockSpec((rank, unit), lambda j, me: (0, 0))


def whole_spec(array):
    return pl.BlockSpec(array.shape, lambda j, me: (0, 0))


def cost(rows, cols, rank, passes):
    return pl.CostEstimate(
        flops=2 * rows * cols * rank // SCALE, bytes_accessed=2 * passes * rows * cols // SCALE, transcendentals=0
    )


def pack(me, base, tp, distances, first, cols):
    rows, group = base.shape[0], base.shape[1] // tp

    def moves(me):
        return [m for i, d in enumerate(distances) for m in column_moves(me ^ d, rows, cols, group, first, i)]

    return move(me, [base], [(rows, cols)] * len(distances), moves)


def pack_first(me, base, tp, d, left, right, late, cols):
    rows, group = base.shape[0], base.shape[1] // tp
    rank, lane = left.shape
    late_cols = late[1] - late[0]

    def moves(me):
        extras = [
            (1, 0, 0, rank, lane, 0, rows, 0),
            (1, 0, 0, rank, lane, 1, 0, 0),
            (2, 0, late[0], rank, late_cols, 0, rows, lane),
            (2, 0, late[0], rank, late_cols, 1, 0, lane),
        ]
        return column_moves(me ^ d, rows, cols, group, 0, 0) + extras

    return move(me, [base, left, right], [(rows + rank, cols), (rank, lane + late_cols)], moves)


def pack_carrier(me, base, tp, distances, terms, first, cols):
    rows, group = base.shape[0], base.shape[1] // tp

    def moves(me):
        result = []
        for i, d in enumerate(distances):
            result += column_moves(me ^ d, rows, cols, group, first, i)
            result.append((1, d * SUMS_ROWS, 0, SUMS_ROWS, terms.shape[1], i, rows, 0))
        return result

    return move(me, [base, terms], [(rows + SUMS_ROWS, cols)] * len(distances), moves)


def pack_near(me, base, tp):
    rows, group = base.shape[0], base.shape[1] // tp

    def moves(me):
        result = []
        for s in range(2):
            for source, r, col, *rest in column_moves((me // 2) * 2 + s, rows, group, group, 0, 0):
                result.append((source, r, col, *rest[:-2], s * rows + r, 0))
        return result

    return move(me, [base], [(2 * rows, group)], moves)[0]


def near_spec(rows, unit, first):
    return pl.BlockSpec((rows, unit), lambda j, me: ((me[0] % 2) ^ 1, first + j))


def low_rank(extra_ref, start, height, right):
    left = extra_ref[pl.ds(0, right.shape[0]), pl.ds(start, height)]
    return lax.dot_general(left, right, (((0,), (0,)), ((), ())), preferred_element_type=jnp.float32)


def squares_of(piece_ref, extra_ref, right):
    rows, cols = piece_ref.shape
    height = min(rows, BLOCK)
    total = jnp.zeros((8, cols), jnp.float32)
    for r in range(0, rows, height):
        combined = piece_ref[pl.ds(r, height), :].astype(jnp.float32) + low_rank(extra_ref, r, height, right)
        total = total + jnp.sum((combined * combined).reshape(height // 8, 8, cols), axis=0)
    return total


def squares_kernel(tp, me_ref, *refs):
    pieces, extras, right_ref, out_ref = refs[:tp], refs[tp : 2 * tp], refs[-2], refs[-1]
    right = right_ref[...]
    total = sum(squares_of(piece, extra, right) for piece, extra in zip(pieces, extras))
    out_ref[...] = jnp.sum(total, axis=0, keepdims=True)


def sender_squares_kernel(tp, me_ref, *refs):
    pieces, rights, left, sums_ref, terms_ref = refs[:tp], refs[tp : 2 * tp], refs[-3], refs[-2], refs[-1]
    line = lax.broadcasted_iota(jnp.int32, (SUMS_ROWS, sums_ref.shape[1]), 0)
    for d in range(tp):
        sums = jnp.sum(squares_of(pieces[d], left, rights[d][...]), axis=0, keepdims=True)
        sums_ref[pl.ds(d, 1), :] = sums
        block = jnp.zeros(line.shape, jnp.float32)
        for term in range(TERMS):
            part = sums.astype(jnp.bfloat16).astype(jnp.float32)
            block = jnp.where(line == term, part, block)
            sums = sums - part
        terms_ref[pl.ds(d * SUMS_ROWS, SUMS_ROWS), :] = block.astype(jnp.bfloat16)


def column_squares(me, base, near, received, extras, right, unit, first, count):
    rows = base.shape[0]
    rank, cols = right.shape
    tp = len(extras)
    return pl.pallas_call(
        functools.partial(squares_kernel, tp),
        out_shape=jax.ShapeDtypeStruct((1, count * unit), jnp.float32),
        grid_spec=pltpu.PrefetchScalarGridSpec(
            num_scalar_prefetch=1,
            grid=(count,),
            in_specs=[group_spec(rows, unit, cols // unit, first), near_spec(rows, unit, first)]
            + [chunk_spec(rows, unit)] * (tp - 2)
            + [left_spec(rank, max(rows, BLOCK))] * tp
            + [chunk_spec(rank, unit, first)],
            out_specs=chunk_spec(1, unit),
        ),
        compiler_params=PARAMS,
        cost_estimate=cost(tp * rows, count * unit, rank, 1),
    )(me, base, near, *received, *extras, right)


def sender_squares(me, base, extras, rank, unit, first, count, lane):
    rows = base.shape[0]
    tp = len(extras)
    groups = base.shape[1] // (tp * unit)
    return pl.pallas_call(
        functools.partial(sender_squares_kernel, tp),
        out_shape=[
            jax.ShapeDtypeStruct((tp, count * unit), jnp.float32),
            jax.ShapeDtypeStruct((tp * SUMS_ROWS, count * unit), jnp.bfloat16),
        ],
        grid_spec=pltpu.PrefetchScalarGridSpec(
            num_scalar_prefetch=1,
            grid=(count,),
            in_specs=[group_spec(rows, unit, groups, first, d) for d in range(tp)]
            + [chunk_spec(rank, unit, lane // unit)] * tp
            + [left_spec(rank, lane)],
            out_specs=[chunk_spec(tp, unit), chunk_spec(tp * SUMS_ROWS, unit)],
        ),
        compiler_params=PARAMS,
        cost_estimate=cost(tp * rows, count * unit, rank, 1),
    )(me, *[base] * tp, *extras, extras[0])


def export_kernel(tp, first, me_ref, *refs):
    pieces, extras = refs[:tp], refs[tp : 2 * tp]
    right_ref, squares_ref, mag_ref = refs[2 * tp : 2 * tp + 3]
    out_ref, scales_ref = refs[-2:]
    rows, cols = pieces[0].shape
    step = pl.program_id(0)
    if len(refs) > 2 * tp + 5:
        @pl.when(step == 0)
        def _():
            scales_ref[...] = refs[2 * tp + 4][...]

    factor = mag_ref[...] / jnp.sqrt(squares_ref[...] + EPSILON)
    right = right_ref[...]
    height = min(rows, BLOCK)
    for d in range(tp):
        start = (me_ref[0] ^ d) * rows
        for r in range(0, rows, height):
            combined = pieces[d][pl.ds(r, height), :].astype(jnp.float32) + low_rank(extras[d], r, height, right)
            span = pl.ds(pl.multiple_of(start + r, height), height)
            out_ref[span, :] = (combined * factor).astype(jnp.bfloat16)

    lane = lax.broadcasted_iota(jnp.int32, (1, scales_ref.shape[1]), 1)
    per_step = cols // BLOCK
    for i in range(tp * rows // BLOCK):
        span = pl.ds(i * BLOCK, BLOCK)
        line = scales_ref[pl.ds(i, 1), :]
        for j in range(per_step):
            tile = out_ref[span, pl.ds(j * BLOCK, BLOCK)].astype(jnp.float32)
            largest = jnp.max(jnp.max(jnp.abs(tile), axis=0, keepdims=True), axis=1, keepdims=True)
            out_ref[span, pl.ds(j * BLOCK, BLOCK)] = (tile * (1.0 / (largest + EPSILON))).astype(jnp.bfloat16)
            line = jnp.where(lane == (first + step) * per_step + j, largest, line)
        scales_ref[pl.ds(i, 1), :] = line


def export_chunk(me, base, near, received, extras, right, squares, mag, unit, first, count, previous):
    rows = base.shape[0]
    rank, cols = right.shape
    tp = len(extras)
    groups = cols // unit
    result = (
        jax.ShapeDtypeStruct((tp * rows, cols), jnp.bfloat16),
        jax.ShapeDtypeStruct((tp * rows // BLOCK, cols // BLOCK), jnp.float32),
    )
    in_specs = (
        [group_spec(rows, unit, groups, first), near_spec(rows, unit, first)]
        + [chunk_spec(rows, unit)] * (tp - 2)
        + [left_spec(rank, max(rows, BLOCK))] * tp
        + [chunk_spec(rank, unit, first), chunk_spec(1, unit), group_spec(1, unit, groups, first)]
    )
    args = [base, near, *received, *extras, right, squares, mag]
    aliases = {}
    if previous is not None:
        in_specs += [pl.BlockSpec(memory_space=pl.ANY), whole_spec(previous[1])]
        args += list(previous)
        aliases = {len(args) - 1: 0}
    return pl.pallas_call(
        functools.partial(export_kernel, tp, first),
        out_shape=result,
        grid_spec=pltpu.PrefetchScalarGridSpec(
            num_scalar_prefetch=1,
            grid=(count,),
            in_specs=in_specs,
            out_specs=(chunk_spec(tp * rows, unit, first), whole_spec(result[1])),
        ),
        input_output_aliases=aliases,
        compiler_params=PARAMS,
        cost_estimate=cost(tp * rows, count * unit, rank, 2),
    )(me, *args)


def body(tp, fsdp, base, left, right, magnitude):
    rows, rank = left.shape
    cols = right.shape[1]
    blocks = cols // BLOCK
    chunks, early = chunk_blocks(blocks)
    mag = magnitude.reshape(1, -1)
    me = lax.axis_index("tp").astype(jnp.int32).reshape(1)
    lane = -(-rows // BLOCK) * BLOCK
    left = jnp.pad(left.T, ((0, 0), (0, lane - rows)))
    late = (chunks[early][0], chunks[-1][1])
    far = range(2, tp)
    received = {}

    def span(k):
        a, b = chunks[k]
        return a * BLOCK, (b - a) * BLOCK

    def units(k):
        a, b = chunks[k]
        width = width_of(a, b, blocks)
        return width * BLOCK, a // width, (b - a) // width

    def send(k, pieces):
        received[k] = [swap(piece, d, tp) for d, piece in zip(far, pieces)]

    pieces = []
    for d in far:
        if d % 2 == 0:
            piece, own = pack_first(me, base, tp, d, left, right, (late[0] * BLOCK, late[1] * BLOCK), span(0)[1])
        else:
            piece = pack(after(me, own), base, tp, (d,), *span(0))[0]
        pieces.append(piece)
    send(0, pieces)
    pieces = pack(after(me, *pieces), base, tp, far, *span(1))
    send(1, pieces)
    near = lax.all_to_all(
        pack_near(after(me, *pieces), base, tp), "tp", 0, 0, tiled=True,
        axis_index_groups=[[i, i + 1] for i in range(0, tp, 2)],
    )

    even = [own] + [received[0][d - 2][rows:, : own.shape[1]] for d in far[::2]]
    odd = swap(jnp.concatenate(even), 1, tp)
    extras = []
    for i in range(tp // 2):
        extras += [even[i], odd[i * rank : (i + 1) * rank]]

    result = None
    token = ()
    totals = {}
    for k in range(len(chunks)):
        following = k + AHEAD
        if following < len(chunks):
            turn = after(me, *received[k], *token)
            if following == CARRIER:
                width = width_of(late[0], late[1] - late[0], blocks, lane // BLOCK)
                sums, terms = sender_squares(
                    turn, base, extras, rank, width * BLOCK, late[0] // width, (late[1] - late[0]) // width, lane
                )
                late_sums = sums[:1] + swap(sums[1:2], 1, tp)
                send(following, pack_carrier(turn, base, tp, far, terms, *span(following)))
            else:
                send(following, pack(turn, base, tp, far, *span(following)))
        if k < early:
            local = column_squares(after(me, *token), base, near, received[k], extras, right, *units(k))
            if k == CARRIER:
                for piece in received[k]:
                    parts = after(piece, *token)[rows : rows + TERMS, : late_sums.shape[1]].astype(jnp.float32)
                    late_sums = late_sums + jnp.sum(parts, axis=0, keepdims=True)
                local = jnp.concatenate([local, late_sums], axis=1)
            total = lax.psum(local, "fsdp") if k < early - 1 else total_of(local, fsdp, "fsdp")
            totals[k] = total[:, : span(k)[1]]
            if k == CARRIER:
                for i in range(early, len(chunks)):
                    start = span(k)[1] + span(i)[0] - late[0] * BLOCK
                    totals[i] = total[:, start : start + span(i)[1]]
        result = export_chunk(me, base, near, received[k], extras, right, totals[k], mag, *units(k), result)
        token = (result[1],)
    return result


def solution(mesh):
    in_specs = (P(("fsdp", "tp"), None), P(("fsdp", "tp"), None), P(None, "tp"), P())
    out_specs = (P("fsdp", "tp"), P("fsdp", "tp"))
    return jax.shard_map(
        functools.partial(body, mesh.shape["tp"], mesh.shape["fsdp"]), mesh=mesh, in_specs=in_specs, out_specs=out_specs, check_vma=False
    )
```

```python
import functools

import jax
import jax.numpy as jnp
from jax import lax
from jax.experimental import pallas as pl
from jax.experimental.pallas import tpu as pltpu
from jax.sharding import PartitionSpec as P

BLOCK = 128
EPSILON = 1e-06
EARLY = (8, 8, 8, 8, 8, 8)
LATE = (4,)
AHEAD = 2
SCALE = 3
CARRIER = 3
TERMS = 3
SUMS_ROWS = 16
PARAMS = pltpu.CompilerParams(vmem_limit_bytes=52 * 2**20)
MOVE_PARAMS = pltpu.CompilerParams(vmem_limit_bytes=56 * 2**20)


def chunk_blocks(total):
    parts = EARLY + LATE
    bounds = [total * sum(parts[:i]) // sum(parts) for i in range(len(parts) + 1)]
    chunks = [(a, b) for a, b in zip(bounds, bounds[1:]) if b > a]
    return chunks, sum(a < bounds[len(EARLY)] for a, _ in chunks)


def width_of(*counts):
    return max(d for d in (4, 2, 1) if all(count % d == 0 for count in counts))


def after(value, *others):
    return lax.optimization_barrier((value, *others))[0]


def swap(array, d, size, axis="tp"):
    return lax.ppermute(array, axis, [(i, i ^ d) for i in range(size)])


def total_of(array, size, axis):
    d = 1
    while d < size:
        others = (d,) if 2 * d == size else (d, 2 * d, 3 * d)
        array = array + sum(swap(array, other, size, axis) for other in others)
        d *= 1 + len(others)
    return array


def move_kernel(moves, number, me_ref, *refs):
    plan = moves(me_ref[0])
    sources, targets = refs[:number], refs[number : -len(plan) - 2]
    holds, came, went = refs[-len(plan) - 2 : -2], refs[-2], refs[-1]
    ins, outs = [], []
    for i, (source, row, col, rows, cols, target, to_row, to_col) in enumerate(plan):
        block = sources[source].at[pl.ds(row, rows), pl.ds(col, cols)]
        place = targets[target].at[pl.ds(to_row, rows), pl.ds(to_col, cols)]
        ins.append(pltpu.make_async_copy(block, holds[i], came.at[i]))
        outs.append(pltpu.make_async_copy(holds[i], place, went.at[i]))
    for copy in ins:
        copy.start()
    for copy, onward in zip(ins, outs):
        copy.wait()
        onward.start()
    for copy in outs:
        copy.wait()


def move(me, arrays, shapes, moves):
    dtype = arrays[0].dtype
    plan = moves(0)
    return pl.pallas_call(
        functools.partial(move_kernel, moves, len(arrays)),
        out_shape=[jax.ShapeDtypeStruct(shape, dtype) for shape in shapes],
        grid_spec=pltpu.PrefetchScalarGridSpec(
            num_scalar_prefetch=1,
            grid=(1,),
            in_specs=[pl.BlockSpec(memory_space=pl.ANY)] * len(arrays),
            out_specs=[pl.BlockSpec(memory_space=pl.ANY)] * len(shapes),
            scratch_shapes=[pltpu.VMEM((rows, cols), dtype) for _, _, _, rows, cols, *_ in plan]
            + [pltpu.SemaphoreType.DMA((len(plan),))] * 2,
        ),
        compiler_params=MOVE_PARAMS,
        cost_estimate=cost(sum(rows * cols for rows, cols in shapes), 1, 0, 2),
    )(me, *arrays)


def parts_of(rows):
    height = rows // 8 if rows % BLOCK == 0 else rows
    return [(r, height) for r in range(0, rows, height)]


def column_moves(me, rows, cols, group, first, target):
    col = pl.multiple_of(me * group + first, BLOCK)
    return [(0, r, col, height, cols, target, r, 0) for r, height in parts_of(rows)]


def group_spec(rows, unit, groups, first, d=0):
    return pl.BlockSpec((rows, unit), lambda j, me: (0, (me[0] ^ d) * groups + first + j))


def chunk_spec(rows, unit, first=0):
    return pl.BlockSpec((rows, unit), lambda j, me: (0, first + j))


def left_spec(rank, unit):
    return pl.BlockSpec((rank, unit), lambda j, me: (0, 0))


def whole_spec(array):
    return pl.BlockSpec(array.shape, lambda j, me: (0, 0))


def cost(rows, cols, rank, passes):
    return pl.CostEstimate(
        flops=2 * rows * cols * rank // SCALE, bytes_accessed=2 * passes * rows * cols // SCALE, transcendentals=0
    )


def pack(me, base, tp, distances, first, cols):
    rows, group = base.shape[0], base.shape[1] // tp

    def moves(me):
        return [m for i, d in enumerate(distances) for m in column_moves(me ^ d, rows, cols, group, first, i)]

    return move(me, [base], [(rows, cols)] * len(distances), moves)


def pack_first(me, base, tp, d, left, right, late, cols):
    rows, group = base.shape[0], base.shape[1] // tp
    rank, lane = left.shape
    late_cols = late[1] - late[0]

    def moves(me):
        extras = [
            (1, 0, 0, rank, lane, 0, rows, 0),
            (1, 0, 0, rank, lane, 1, 0, 0),
            (2, 0, late[0], rank, late_cols, 0, rows, lane),
            (2, 0, late[0], rank, late_cols, 1, 0, lane),
        ]
        return column_moves(me ^ d, rows, cols, group, 0, 0) + extras

    return move(me, [base, left, right], [(rows + rank, cols), (rank, lane + late_cols)], moves)


def pack_carrier(me, base, tp, distances, terms, first, cols):
    rows, group = base.shape[0], base.shape[1] // tp

    def moves(me):
        result = []
        for i, d in enumerate(distances):
            result += column_moves(me ^ d, rows, cols, group, first, i)
            if d % 2 == 0:
                result.append((1, d // 2 * SUMS_ROWS, 0, SUMS_ROWS, terms.shape[1], i, rows, 0))
        return result

    return move(me, [base, terms], [(rows + (d + 1) % 2 * SUMS_ROWS, cols) for d in distances], moves)


def pack_near(me, base, tp):
    rows, group = base.shape[0], base.shape[1] // tp

    def moves(me):
        result = []
        for s in range(2):
            for source, r, col, *rest in column_moves((me // 2) * 2 + s, rows, group, group, 0, 0):
                result.append((source, r, col, *rest[:-2], s * rows + r, 0))
        return result

    return move(me, [base], [(2 * rows, group)], moves)[0]


def near_spec(rows, unit, first):
    return pl.BlockSpec((rows, unit), lambda j, me: ((me[0] % 2) ^ 1, first + j))


def low_rank(extra_ref, start, height, right):
    left = extra_ref[pl.ds(0, right.shape[0]), pl.ds(start, height)]
    return lax.dot_general(left, right, (((0,), (0,)), ((), ())), preferred_element_type=jnp.float32)


def squares_of(piece_ref, extra_ref, right):
    rows, cols = piece_ref.shape
    height = min(rows, BLOCK)
    total = jnp.zeros((8, cols), jnp.float32)
    for r in range(0, rows, height):
        combined = piece_ref[pl.ds(r, height), :].astype(jnp.float32) + low_rank(extra_ref, r, height, right)
        total = total + jnp.sum((combined * combined).reshape(height // 8, 8, cols), axis=0)
    return total


def squares_kernel(tp, me_ref, *refs):
    pieces, extras, right_ref, out_ref = refs[:tp], refs[tp : 2 * tp], refs[-2], refs[-1]
    right = right_ref[...]
    total = sum(squares_of(piece, extra, right) for piece, extra in zip(pieces, extras))
    out_ref[...] = jnp.sum(total, axis=0, keepdims=True)


def sender_squares_kernel(tp, me_ref, *refs):
    pieces, rights, left, sums_ref = refs[:tp], refs[tp : 2 * tp], refs[-2], refs[-1]
    for d in range(tp):
        sums_ref[pl.ds(d, 1), :] = jnp.sum(squares_of(pieces[d], left, rights[d][...]), axis=0, keepdims=True)


def terms_kernel(sums_ref, terms_ref):
    line = lax.broadcasted_iota(jnp.int32, (SUMS_ROWS, sums_ref.shape[1]), 0)
    for i in range(sums_ref.shape[0]):
        sums = sums_ref[pl.ds(i, 1), :]
        block = jnp.zeros(line.shape, jnp.float32)
        for term in range(TERMS):
            part = sums.astype(jnp.bfloat16).astype(jnp.float32)
            block = jnp.where(line == term, part, block)
            sums = sums - part
        terms_ref[pl.ds(i * SUMS_ROWS, SUMS_ROWS), :] = block.astype(jnp.bfloat16)


def terms_of(sums):
    rows, cols = sums.shape
    return pl.pallas_call(
        terms_kernel,
        out_shape=jax.ShapeDtypeStruct((rows * SUMS_ROWS, cols), jnp.bfloat16),
        compiler_params=PARAMS,
        cost_estimate=cost(rows, cols, 0, 2),
    )(sums)


def column_squares(me, base, near, received, extras, right, unit, first, count):
    rows = base.shape[0]
    rank, cols = right.shape
    tp = len(extras)
    return pl.pallas_call(
        functools.partial(squares_kernel, tp),
        out_shape=jax.ShapeDtypeStruct((1, count * unit), jnp.float32),
        grid_spec=pltpu.PrefetchScalarGridSpec(
            num_scalar_prefetch=1,
            grid=(count,),
            in_specs=[group_spec(rows, unit, cols // unit, first), near_spec(rows, unit, first)]
            + [chunk_spec(rows, unit)] * (tp - 2)
            + [left_spec(rank, max(rows, BLOCK))] * tp
            + [chunk_spec(rank, unit, first)],
            out_specs=chunk_spec(1, unit),
        ),
        compiler_params=PARAMS,
        cost_estimate=cost(tp * rows, count * unit, rank, 1),
    )(me, base, near, *received, *extras, right)


def sender_squares(me, base, extras, rank, unit, first, count, lane):
    rows = base.shape[0]
    tp = len(extras)
    groups = base.shape[1] // (tp * unit)
    return pl.pallas_call(
        functools.partial(sender_squares_kernel, tp),
        out_shape=jax.ShapeDtypeStruct((tp, count * unit), jnp.float32),
        grid_spec=pltpu.PrefetchScalarGridSpec(
            num_scalar_prefetch=1,
            grid=(count,),
            in_specs=[group_spec(rows, unit, groups, first, d) for d in range(tp)]
            + [chunk_spec(rank, unit, lane // unit)] * tp
            + [left_spec(rank, lane)],
            out_specs=chunk_spec(tp, unit),
        ),
        compiler_params=PARAMS,
        cost_estimate=cost(tp * rows, count * unit, rank, 1),
    )(me, *[base] * tp, *extras, extras[0])


def export_kernel(tp, ds, first, me_ref, *refs):
    number = len(ds)
    pieces, extras = refs[:number], refs[number : 2 * number]
    right_ref, squares_ref, mag_ref = refs[2 * number : 2 * number + 3]
    out_ref, scales_ref = refs[-2:]
    rows, cols = pieces[0].shape
    step = pl.program_id(0)
    if len(refs) > 2 * number + 5:
        @pl.when(step == 0)
        def _():
            scales_ref[...] = refs[2 * number + 4][...]

    factor = mag_ref[...] / jnp.sqrt(squares_ref[...] + EPSILON)
    right = right_ref[...]
    lane = lax.broadcasted_iota(jnp.int32, (1, scales_ref.shape[1]), 1)
    per_step = cols // BLOCK

    def merge(i, r, height):
        combined = pieces[i][pl.ds(r, height), :].astype(jnp.float32) + low_rank(extras[i], r, height, right)
        return (combined * factor).astype(jnp.bfloat16)

    def finish(merged, span, block):
        line = scales_ref[pl.ds(block, 1), :]
        for j in range(per_step):
            tile = merged[:, j * BLOCK : (j + 1) * BLOCK].astype(jnp.float32)
            largest = jnp.max(jnp.max(jnp.abs(tile), axis=0, keepdims=True), axis=1, keepdims=True)
            out_ref[span, pl.ds(j * BLOCK, BLOCK)] = (tile * (1.0 / (largest + EPSILON))).astype(jnp.bfloat16)
            line = jnp.where(lane == (first + step) * per_step + j, largest, line)
        scales_ref[pl.ds(block, 1), :] = line

    if rows % BLOCK == 0:
        for i, d in enumerate(ds):
            place = me_ref[0] ^ d
            start = place * rows if out_ref.shape[0] > rows else 0
            for r in range(0, rows, BLOCK):
                span = pl.ds(pl.multiple_of(start + r, BLOCK), BLOCK)
                finish(merge(i, r, BLOCK), span, place * (rows // BLOCK) + r // BLOCK)
    else:
        for i, d in enumerate(ds):
            out_ref[pl.ds(pl.multiple_of((me_ref[0] ^ d) * rows, rows), rows), :] = merge(i, 0, rows)
        for block in range(tp * rows // BLOCK):
            span = pl.ds(block * BLOCK, BLOCK)
            finish(out_ref[span, :], span, block)


def export_chunk(me, base, near, received, extras, right, squares, mag, ds, unit, first, count, previous):
    rows = base.shape[0]
    rank, cols = right.shape
    tp = len(extras)
    groups = cols // unit
    result = (
        jax.ShapeDtypeStruct((tp * rows, cols), jnp.bfloat16),
        jax.ShapeDtypeStruct((tp * rows // BLOCK, cols // BLOCK), jnp.float32),
    )
    pieces = [base, near, *received]
    piece_specs = [group_spec(rows, unit, groups, first), near_spec(rows, unit, first)]
    piece_specs += [chunk_spec(rows, unit)] * (tp - 2)
    in_specs = (
        [piece_specs[d] for d in ds]
        + [left_spec(rank, max(rows, BLOCK))] * len(ds)
        + [chunk_spec(rank, unit, first), chunk_spec(1, unit), group_spec(1, unit, groups, first)]
    )
    args = [pieces[d] for d in ds] + [extras[d] for d in ds] + [right, squares, mag]
    aliases = {}
    if previous is not None:
        in_specs += [pl.BlockSpec(memory_space=pl.ANY), whole_spec(previous[1])]
        args += list(previous)
        aliases = {len(args) - 1: 0}
    if len(ds) == 1:
        out_spec = pl.BlockSpec((rows, unit), lambda j, me: (me[0] ^ ds[0], first + j))
    else:
        out_spec = chunk_spec(tp * rows, unit, first)
    return pl.pallas_call(
        functools.partial(export_kernel, tp, ds, first),
        out_shape=result,
        grid_spec=pltpu.PrefetchScalarGridSpec(
            num_scalar_prefetch=1,
            grid=(count,),
            in_specs=in_specs,
            out_specs=(out_spec, whole_spec(result[1])),
        ),
        input_output_aliases=aliases,
        compiler_params=PARAMS,
        cost_estimate=cost(len(ds) * rows, count * unit, rank, 2),
    )(me, *args)


def body(tp, fsdp, base, left, right, magnitude):
    rows, rank = left.shape
    cols = right.shape[1]
    blocks = cols // BLOCK
    chunks, early = chunk_blocks(blocks)
    mag = magnitude.reshape(1, -1)
    me = lax.axis_index("tp").astype(jnp.int32).reshape(1)
    lane = -(-rows // BLOCK) * BLOCK
    left = jnp.pad(left.T, ((0, 0), (0, lane - rows)))
    late = (chunks[early][0], chunks[-1][1])
    far = range(2, tp)
    received = {}

    def span(k):
        a, b = chunks[k]
        return a * BLOCK, (b - a) * BLOCK

    def units(k):
        a, b = chunks[k]
        width = width_of(a, b, blocks)
        return width * BLOCK, a // width, (b - a) // width

    def send(k, pieces):
        received[k] = [swap(piece, d, tp) for d, piece in zip(far, pieces)]

    pieces = []
    for d in far:
        if d % 2 == 0:
            piece, own = pack_first(me, base, tp, d, left, right, (late[0] * BLOCK, late[1] * BLOCK), span(0)[1])
        else:
            piece = pack(after(me, own), base, tp, (d,), *span(0))[0]
        pieces.append(piece)
    send(0, pieces)
    pieces = pack(after(me, *pieces), base, tp, far, *span(1))
    send(1, pieces)
    near = lax.all_to_all(
        pack_near(after(me, *pieces), base, tp), "tp", 0, 0, tiled=True,
        axis_index_groups=[[i, i + 1] for i in range(0, tp, 2)],
    )

    even = [own] + [received[0][d - 2][rows:, : own.shape[1]] for d in far[::2]]
    odd = swap(jnp.concatenate(even), 1, tp)
    extras = []
    for i in range(tp // 2):
        extras += [even[i], odd[i * rank : (i + 1) * rank]]

    result = None
    token = ()
    totals = {}
    for k in range(len(chunks)):
        following = k + AHEAD
        if following < len(chunks):
            turn = after(me, *received[k], *token)
            if following == CARRIER:
                width = width_of(late[0], late[1] - late[0], blocks, lane // BLOCK)
                sums = sender_squares(
                    turn, base, extras, rank, width * BLOCK, late[0] // width, (late[1] - late[0]) // width, lane
                )
                sums = sums[0::2] + swap(sums[1::2], 1, tp)
                late_sums = sums[:1]
                send(following, pack_carrier(turn, base, tp, far, terms_of(sums), *span(following)))
            else:
                send(following, pack(turn, base, tp, far, *span(following)))
        if k < early:
            local = column_squares(after(me, *token), base, near, received[k], extras, right, *units(k))
            if k == CARRIER:
                for piece in received[k][::2]:
                    parts = after(piece, *token)[rows : rows + TERMS, : late_sums.shape[1]].astype(jnp.float32)
                    late_sums = late_sums + jnp.sum(parts, axis=0, keepdims=True)
                local = jnp.concatenate([local, late_sums], axis=1)
            total = lax.psum(local, "fsdp") if k < early - 1 else total_of(local, fsdp, "fsdp")
            totals[k] = total[:, : span(k)[1]]
            if k == CARRIER:
                for i in range(early, len(chunks)):
                    start = span(k)[1] + span(i)[0] - late[0] * BLOCK
                    totals[i] = total[:, start : start + span(i)[1]]
        split = k == len(chunks) - 1 and rows % BLOCK == 0 and tp > 2
        for ds in (tuple(range(tp - 1)), (tp - 1,)) if split else (tuple(range(tp)),):
            result = export_chunk(me, base, near, received[k], extras, right, totals[k], mag, ds, *units(k), result)
        token = (result[1],)
    return result


def solution(mesh):
    in_specs = (P(("fsdp", "tp"), None), P(("fsdp", "tp"), None), P(None, "tp"), P())
    out_specs = (P("fsdp", "tp"), P("fsdp", "tp"))
    return jax.shard_map(
        functools.partial(body, mesh.shape["tp"], mesh.shape["fsdp"]), mesh=mesh, in_specs=in_specs, out_specs=out_specs, check_vma=False
    )
```

```python
import functools

import jax
import jax.numpy as jnp
from jax import lax
from jax.experimental import pallas as pl
from jax.experimental.pallas import tpu as pltpu
from jax.sharding import PartitionSpec as P

BLOCK = 128
EPSILON = 1e-06
EARLY = (8, 8, 8, 8, 8, 8)
LATE = (4,)
AHEAD = 2
SCALE = 3
CARRIER = 3
TERMS = 3
SUMS_ROWS = 16
PARAMS = pltpu.CompilerParams(vmem_limit_bytes=52 * 2**20)
MOVE_PARAMS = pltpu.CompilerParams(vmem_limit_bytes=56 * 2**20)


def chunk_blocks(total):
    parts = EARLY + LATE
    bounds = [total * sum(parts[:i]) // sum(parts) for i in range(len(parts) + 1)]
    chunks = [(a, b) for a, b in zip(bounds, bounds[1:]) if b > a]
    return chunks, sum(a < bounds[len(EARLY)] for a, _ in chunks)


def width_of(*counts):
    return max(d for d in (4, 2, 1) if all(count % d == 0 for count in counts))


def after(value, *others):
    return lax.optimization_barrier((value, *others))[0]


def swap(array, d, size, axis="tp"):
    return lax.ppermute(array, axis, [(i, i ^ d) for i in range(size)])


def total_of(array, size, axis):
    d = 1
    while d < size:
        others = (d,) if 2 * d == size else (d, 2 * d, 3 * d)
        array = array + sum(swap(array, other, size, axis) for other in others)
        d *= 1 + len(others)
    return array


def move_kernel(moves, number, me_ref, *refs):
    plan = moves(me_ref[0])
    sources, targets = refs[:number], refs[number : -len(plan) - 2]
    holds, came, went = refs[-len(plan) - 2 : -2], refs[-2], refs[-1]
    ins, outs = [], []
    for i, (source, row, col, rows, cols, target, to_row, to_col) in enumerate(plan):
        block = sources[source].at[pl.ds(row, rows), pl.ds(col, cols)]
        place = targets[target].at[pl.ds(to_row, rows), pl.ds(to_col, cols)]
        ins.append(pltpu.make_async_copy(block, holds[i], came.at[i]))
        outs.append(pltpu.make_async_copy(holds[i], place, went.at[i]))
    for copy in ins:
        copy.start()
    for copy, onward in zip(ins, outs):
        copy.wait()
        onward.start()
    for copy in outs:
        copy.wait()


def move(me, arrays, shapes, moves):
    dtype = arrays[0].dtype
    plan = moves(0)
    return pl.pallas_call(
        functools.partial(move_kernel, moves, len(arrays)),
        out_shape=[jax.ShapeDtypeStruct(shape, dtype) for shape in shapes],
        grid_spec=pltpu.PrefetchScalarGridSpec(
            num_scalar_prefetch=1,
            grid=(1,),
            in_specs=[pl.BlockSpec(memory_space=pl.ANY)] * len(arrays),
            out_specs=[pl.BlockSpec(memory_space=pl.ANY)] * len(shapes),
            scratch_shapes=[pltpu.VMEM((rows, cols), dtype) for _, _, _, rows, cols, *_ in plan]
            + [pltpu.SemaphoreType.DMA((len(plan),))] * 2,
        ),
        compiler_params=MOVE_PARAMS,
        cost_estimate=cost(sum(rows * cols for rows, cols in shapes), 1, 0, 2),
    )(me, *arrays)


def parts_of(rows):
    height = rows // 8 if rows % BLOCK == 0 else rows
    return [(r, height) for r in range(0, rows, height)]


def column_moves(me, rows, cols, group, first, target):
    col = pl.multiple_of(me * group + first, BLOCK)
    return [(0, r, col, height, cols, target, r, 0) for r, height in parts_of(rows)]


def group_spec(rows, unit, groups, first, d=0):
    return pl.BlockSpec((rows, unit), lambda j, me: (0, (me[0] ^ d) * groups + first + j))


def chunk_spec(rows, unit, first=0):
    return pl.BlockSpec((rows, unit), lambda j, me: (0, first + j))


def left_spec(rank, unit):
    return pl.BlockSpec((rank, unit), lambda j, me: (0, 0))


def whole_spec(array):
    return pl.BlockSpec(array.shape, lambda j, me: (0, 0))


def cost(rows, cols, rank, passes):
    return pl.CostEstimate(
        flops=2 * rows * cols * rank // SCALE, bytes_accessed=2 * passes * rows * cols // SCALE, transcendentals=0
    )


def pack(me, base, tp, distances, first, cols):
    rows, group = base.shape[0], base.shape[1] // tp

    def moves(me):
        return [m for i, d in enumerate(distances) for m in column_moves(me ^ d, rows, cols, group, first, i)]

    return move(me, [base], [(rows, cols)] * len(distances), moves)


def pack_first(me, base, tp, d, left, right, late, cols):
    rows, group = base.shape[0], base.shape[1] // tp
    rank, lane = left.shape
    late_cols = late[1] - late[0]

    def moves(me):
        extras = [
            (1, 0, 0, rank, lane, 0, rows, 0),
            (1, 0, 0, rank, lane, 1, 0, 0),
            (2, 0, late[0], rank, late_cols, 0, rows, lane),
            (2, 0, late[0], rank, late_cols, 1, 0, lane),
        ]
        return column_moves(me ^ d, rows, cols, group, 0, 0) + extras

    return move(me, [base, left, right], [(rows + rank, cols), (rank, lane + late_cols)], moves)


def pack_carrier(me, base, tp, distances, terms, first, cols):
    rows, group = base.shape[0], base.shape[1] // tp

    def moves(me):
        result = []
        for i, d in enumerate(distances):
            result += column_moves(me ^ d, rows, cols, group, first, i)
            if d % 2 == 0:
                result.append((1, d // 2 * SUMS_ROWS, 0, SUMS_ROWS, terms.shape[1], i, rows, 0))
        return result

    return move(me, [base, terms], [(rows + (d + 1) % 2 * SUMS_ROWS, cols) for d in distances], moves)


def pack_near(me, base, tp):
    rows, group = base.shape[0], base.shape[1] // tp

    def moves(me):
        result = []
        for s in range(2):
            for source, r, col, *rest in column_moves((me // 2) * 2 + s, rows, group, group, 0, 0):
                result.append((source, r, col, *rest[:-2], s * rows + r, 0))
        return result

    return move(me, [base], [(2 * rows, group)], moves)[0]


def near_spec(rows, unit, first):
    return pl.BlockSpec((rows, unit), lambda j, me: ((me[0] % 2) ^ 1, first + j))


def low_rank(extra_ref, start, height, right):
    left = extra_ref[pl.ds(0, right.shape[0]), pl.ds(start, height)]
    return lax.dot_general(left, right, (((0,), (0,)), ((), ())), preferred_element_type=jnp.float32)


def squares_of(piece_ref, extra_ref, right):
    rows, cols = piece_ref.shape
    height = min(rows, BLOCK)
    total = jnp.zeros((8, cols), jnp.float32)
    for r in range(0, rows, height):
        combined = piece_ref[pl.ds(r, height), :].astype(jnp.float32) + low_rank(extra_ref, r, height, right)
        total = total + jnp.sum((combined * combined).reshape(height // 8, 8, cols), axis=0)
    return total


def squares_kernel(number, me_ref, *refs):
    pieces, extras, right_ref, out_ref = refs[:number], refs[number : 2 * number], refs[2 * number], refs[-1]
    right = right_ref[...]
    total = sum(squares_of(piece, extra, right) for piece, extra in zip(pieces, extras))
    total = jnp.sum(total, axis=0, keepdims=True)
    out_ref[...] = total + refs[-2][...] if len(refs) > 2 * number + 2 else total


def sender_squares_kernel(tp, me_ref, *refs):
    pieces, rights, left, sums_ref = refs[:tp], refs[tp : 2 * tp], refs[-2], refs[-1]
    for d in range(tp):
        sums_ref[pl.ds(d, 1), :] = jnp.sum(squares_of(pieces[d], left, rights[d][...]), axis=0, keepdims=True)


def terms_kernel(sums_ref, terms_ref):
    line = lax.broadcasted_iota(jnp.int32, (SUMS_ROWS, sums_ref.shape[1]), 0)
    for i in range(sums_ref.shape[0]):
        sums = sums_ref[pl.ds(i, 1), :]
        block = jnp.zeros(line.shape, jnp.float32)
        for term in range(TERMS):
            part = sums.astype(jnp.bfloat16).astype(jnp.float32)
            block = jnp.where(line == term, part, block)
            sums = sums - part
        terms_ref[pl.ds(i * SUMS_ROWS, SUMS_ROWS), :] = block.astype(jnp.bfloat16)


def terms_of(sums):
    rows, cols = sums.shape
    return pl.pallas_call(
        terms_kernel,
        out_shape=jax.ShapeDtypeStruct((rows * SUMS_ROWS, cols), jnp.bfloat16),
        compiler_params=PARAMS,
        cost_estimate=cost(rows, cols, 0, 2),
    )(sums)


def piece_specs(tp, rows, unit, groups, first):
    specs = [group_spec(rows, unit, groups, first), near_spec(rows, unit, first)]
    return specs + [chunk_spec(rows, unit)] * (tp - 2)


def column_squares(me, base, near, received, extras, right, ds, unit, first, count, previous=None):
    rows = base.shape[0]
    rank, cols = right.shape
    pieces = [base, near, *received]
    specs = piece_specs(len(extras), rows, unit, cols // unit, first)
    in_specs = [specs[d] for d in ds] + [left_spec(rank, max(rows, BLOCK))] * len(ds) + [chunk_spec(rank, unit, first)]
    args = [pieces[d] for d in ds] + [extras[d] for d in ds] + [right]
    if previous is not None:
        in_specs.append(chunk_spec(1, unit))
        args.append(previous)
    return pl.pallas_call(
        functools.partial(squares_kernel, len(ds)),
        out_shape=jax.ShapeDtypeStruct((1, count * unit), jnp.float32),
        grid_spec=pltpu.PrefetchScalarGridSpec(
            num_scalar_prefetch=1,
            grid=(count,),
            in_specs=in_specs,
            out_specs=chunk_spec(1, unit),
        ),
        compiler_params=PARAMS,
        cost_estimate=cost(len(ds) * rows, count * unit, rank, 1),
    )(me, *args)


def sender_squares(me, base, extras, rank, unit, first, count, lane):
    rows = base.shape[0]
    tp = len(extras)
    groups = base.shape[1] // (tp * unit)
    return pl.pallas_call(
        functools.partial(sender_squares_kernel, tp),
        out_shape=jax.ShapeDtypeStruct((tp, count * unit), jnp.float32),
        grid_spec=pltpu.PrefetchScalarGridSpec(
            num_scalar_prefetch=1,
            grid=(count,),
            in_specs=[group_spec(rows, unit, groups, first, d) for d in range(tp)]
            + [chunk_spec(rank, unit, lane // unit)] * tp
            + [left_spec(rank, lane)],
            out_specs=chunk_spec(tp, unit),
        ),
        compiler_params=PARAMS,
        cost_estimate=cost(tp * rows, count * unit, rank, 1),
    )(me, *[base] * tp, *extras, extras[0])


def export_kernel(tp, ds, first, me_ref, *refs):
    number = len(ds)
    pieces, extras = refs[:number], refs[number : 2 * number]
    right_ref, squares_ref, mag_ref = refs[2 * number : 2 * number + 3]
    out_ref, scales_ref = refs[-2:]
    rows, cols = pieces[0].shape
    step = pl.program_id(0)
    if len(refs) > 2 * number + 5:
        @pl.when(step == 0)
        def _():
            scales_ref[...] = refs[2 * number + 4][...]

    factor = mag_ref[...] / jnp.sqrt(squares_ref[...] + EPSILON)
    right = right_ref[...]
    lane = lax.broadcasted_iota(jnp.int32, (1, scales_ref.shape[1]), 1)
    per_step = cols // BLOCK

    def merge(i, r, height):
        combined = pieces[i][pl.ds(r, height), :].astype(jnp.float32) + low_rank(extras[i], r, height, right)
        return (combined * factor).astype(jnp.bfloat16)

    def finish(merged, span, block):
        line = scales_ref[pl.ds(block, 1), :]
        for j in range(per_step):
            tile = merged[:, j * BLOCK : (j + 1) * BLOCK].astype(jnp.float32)
            largest = jnp.max(jnp.max(jnp.abs(tile), axis=0, keepdims=True), axis=1, keepdims=True)
            out_ref[span, pl.ds(j * BLOCK, BLOCK)] = (tile * (1.0 / (largest + EPSILON))).astype(jnp.bfloat16)
            line = jnp.where(lane == (first + step) * per_step + j, largest, line)
        scales_ref[pl.ds(block, 1), :] = line

    if rows % BLOCK == 0:
        for i, d in enumerate(ds):
            place = me_ref[0] ^ d
            start = place * rows if out_ref.shape[0] > rows else 0
            for r in range(0, rows, BLOCK):
                span = pl.ds(pl.multiple_of(start + r, BLOCK), BLOCK)
                finish(merge(i, r, BLOCK), span, place * (rows // BLOCK) + r // BLOCK)
    else:
        for i, d in enumerate(ds):
            out_ref[pl.ds(pl.multiple_of((me_ref[0] ^ d) * rows, rows), rows), :] = merge(i, 0, rows)
        for block in range(tp * rows // BLOCK):
            span = pl.ds(block * BLOCK, BLOCK)
            finish(out_ref[span, :], span, block)


def export_chunk(me, base, near, received, extras, right, squares, mag, ds, unit, first, count, previous):
    rows = base.shape[0]
    rank, cols = right.shape
    tp = len(extras)
    groups = cols // unit
    result = (
        jax.ShapeDtypeStruct((tp * rows, cols), jnp.bfloat16),
        jax.ShapeDtypeStruct((tp * rows // BLOCK, cols // BLOCK), jnp.float32),
    )
    pieces = [base, near, *received]
    specs = piece_specs(tp, rows, unit, groups, first)
    in_specs = (
        [specs[d] for d in ds]
        + [left_spec(rank, max(rows, BLOCK))] * len(ds)
        + [chunk_spec(rank, unit, first), chunk_spec(1, unit), group_spec(1, unit, groups, first)]
    )
    args = [pieces[d] for d in ds] + [extras[d] for d in ds] + [right, squares, mag]
    aliases = {}
    if previous is not None:
        in_specs += [pl.BlockSpec(memory_space=pl.ANY), whole_spec(previous[1])]
        args += list(previous)
        aliases = {len(args) - 1: 0}
    if len(ds) == 1:
        out_spec = pl.BlockSpec((rows, unit), lambda j, me: (me[0] ^ ds[0], first + j))
    else:
        out_spec = chunk_spec(tp * rows, unit, first)
    return pl.pallas_call(
        functools.partial(export_kernel, tp, ds, first),
        out_shape=result,
        grid_spec=pltpu.PrefetchScalarGridSpec(
            num_scalar_prefetch=1,
            grid=(count,),
            in_specs=in_specs,
            out_specs=(out_spec, whole_spec(result[1])),
        ),
        input_output_aliases=aliases,
        compiler_params=PARAMS,
        cost_estimate=cost(len(ds) * rows, count * unit, rank, 2),
    )(me, *args)


def body(tp, fsdp, base, left, right, magnitude):
    rows, rank = left.shape
    cols = right.shape[1]
    blocks = cols // BLOCK
    chunks, early = chunk_blocks(blocks)
    mag = magnitude.reshape(1, -1)
    me = lax.axis_index("tp").astype(jnp.int32).reshape(1)
    lane = -(-rows // BLOCK) * BLOCK
    left = jnp.pad(left.T, ((0, 0), (0, lane - rows)))
    late = (chunks[early][0], chunks[-1][1])
    far = range(2, tp)
    received = {}

    def span(k):
        a, b = chunks[k]
        return a * BLOCK, (b - a) * BLOCK

    def units(k):
        a, b = chunks[k]
        width = width_of(a, b, blocks)
        return width * BLOCK, a // width, (b - a) // width

    def send(k, pieces):
        received[k] = [swap(piece, d, tp) for d, piece in zip(far, pieces)]

    pieces = []
    for d in far:
        if d % 2 == 0:
            piece, own = pack_first(me, base, tp, d, left, right, (late[0] * BLOCK, late[1] * BLOCK), span(0)[1])
        else:
            piece = pack(after(me, own), base, tp, (d,), *span(0))[0]
        pieces.append(piece)
    send(0, pieces)
    pieces = pack(after(me, *pieces), base, tp, far, *span(1))
    send(1, pieces)
    near = lax.all_to_all(
        pack_near(after(me, *pieces), base, tp), "tp", 0, 0, tiled=True,
        axis_index_groups=[[i, i + 1] for i in range(0, tp, 2)],
    )

    even = [own] + [received[0][d - 2][rows:, : own.shape[1]] for d in far[::2]]
    odd = swap(jnp.concatenate(even), 1, tp)
    extras = []
    for i in range(tp // 2):
        extras += [even[i], odd[i * rank : (i + 1) * rank]]

    apart = rows % BLOCK == 0 and len(chunks) == early + 1
    every = tuple(range(tp))
    result = None
    token = ()
    totals = {}

    def export(k, ds):
        nonlocal result
        result = export_chunk(me, base, near, received.get(k, ()), extras, right, totals[k], mag, ds, *units(k), result)

    for k in range(len(chunks)):
        following = k + AHEAD
        if following < len(chunks):
            turn = after(me, *received[k], *token)
            if following == CARRIER:
                width = width_of(late[0], late[1] - late[0], blocks, lane // BLOCK)
                sums = sender_squares(
                    turn, base, extras, rank, width * BLOCK, late[0] // width, (late[1] - late[0]) // width, lane
                )
                sums = sums[0::2] + swap(sums[1::2], 1, tp)
                late_sums = sums[:1]
                send(following, pack_carrier(turn, base, tp, far, terms_of(sums), *span(following)))
            else:
                send(following, pack(turn, base, tp, far, *span(following)))
        if k < early:
            if apart and k == early - 1:
                export(early, every[:2])
                token = (result[1],)
            turn = after(me, *token)
            local = None
            for ds in (every[:-1], every[-1:]) if apart and k == early - 1 else (every,):
                local = column_squares(turn, base, near, received[k], extras, right, ds, *units(k), local)
            if k == CARRIER:
                for piece in received[k][::2]:
                    parts = after(piece, *token)[rows : rows + TERMS, : late_sums.shape[1]].astype(jnp.float32)
                    late_sums = late_sums + jnp.sum(parts, axis=0, keepdims=True)
                local = jnp.concatenate([local, late_sums], axis=1)
            total = lax.psum(local, "fsdp") if k < early - 1 else total_of(local, fsdp, "fsdp")
            totals[k] = total[:, : span(k)[1]]
            if k == CARRIER:
                for i in range(early, len(chunks)):
                    start = span(k)[1] + span(i)[0] - late[0] * BLOCK
                    totals[i] = total[:, start : start + span(i)[1]]
        if apart and k == early:
            for d in far:
                export(k, (d,))
        else:
            export(k, every)
        token = (result[1],)
    return result


def solution(mesh):
    in_specs = (P(("fsdp", "tp"), None), P(("fsdp", "tp"), None), P(None, "tp"), P())
    out_specs = (P("fsdp", "tp"), P("fsdp", "tp"))
    return jax.shard_map(
        functools.partial(body, mesh.shape["tp"], mesh.shape["fsdp"]), mesh=mesh, in_specs=in_specs, out_specs=out_specs, check_vma=False
    )
```

```python
import functools

import jax
import jax.numpy as jnp
from jax import lax
from jax.experimental import pallas as pl
from jax.experimental.pallas import tpu as pltpu
from jax.sharding import PartitionSpec as P

BLOCK = 128
EPSILON = 1e-06
EARLY = (8, 8, 8, 8, 8, 8)
LATE = (4,)
AHEAD = 2
SCALE = 3
CARRIER = 3
TERMS = 3
SUMS_ROWS = 16
PARAMS = pltpu.CompilerParams(vmem_limit_bytes=52 * 2**20)
MOVE_PARAMS = pltpu.CompilerParams(vmem_limit_bytes=56 * 2**20)


def chunk_blocks(total):
    parts = EARLY + LATE
    bounds = [total * sum(parts[:i]) // sum(parts) for i in range(len(parts) + 1)]
    chunks = [(a, b) for a, b in zip(bounds, bounds[1:]) if b > a]
    return chunks, sum(a < bounds[len(EARLY)] for a, _ in chunks)


def width_of(*counts):
    return max(d for d in (4, 2, 1) if all(count % d == 0 for count in counts))


def after(value, *others):
    return lax.optimization_barrier((value, *others))[0]


def swap(array, d, size, axis="tp"):
    return lax.ppermute(array, axis, [(i, i ^ d) for i in range(size)])


def total_of(array, size, axis):
    d = 1
    while d < size:
        others = (d,) if 2 * d == size else (d, 2 * d, 3 * d)
        array = array + sum(swap(array, other, size, axis) for other in others)
        d *= 1 + len(others)
    return array


def move_kernel(moves, number, direct, me_ref, *refs):
    plan = moves(me_ref[0])
    holds = () if direct else refs[-len(plan) - 2 : -2]
    sources, targets = refs[:number], refs[number : len(refs) - len(holds) - 2]
    came, went = refs[-2:]
    ins, outs = [], []
    for i, (source, row, col, rows, cols, target, to_row, to_col) in enumerate(plan):
        block = sources[source].at[pl.ds(row, rows), pl.ds(col, cols)]
        place = targets[target].at[pl.ds(to_row, rows), pl.ds(to_col, cols)]
        ins.append(pltpu.make_async_copy(block, place if direct else holds[i], came.at[i]))
        if not direct:
            outs.append(pltpu.make_async_copy(holds[i], place, went.at[i]))
    for copy in ins:
        copy.start()
    for i, copy in enumerate(ins):
        copy.wait()
        if not direct:
            outs[i].start()
    for copy in outs:
        copy.wait()


def move(me, arrays, shapes, moves, direct=False):
    dtype = arrays[0].dtype
    plan = moves(0)
    kind = pltpu.VMEM if direct else jax.ShapeDtypeStruct
    space = pltpu.VMEM if direct else pl.ANY
    return pl.pallas_call(
        functools.partial(move_kernel, moves, len(arrays), direct),
        out_shape=[kind(shape, dtype) for shape in shapes],
        grid_spec=pltpu.PrefetchScalarGridSpec(
            num_scalar_prefetch=1,
            grid=(1,),
            in_specs=[pl.BlockSpec(memory_space=pl.ANY)] * len(arrays),
            out_specs=[pl.BlockSpec(memory_space=space)] * len(shapes),
            scratch_shapes=[pltpu.VMEM((rows, cols), dtype) for _, _, _, rows, cols, *_ in (() if direct else plan)]
            + [pltpu.SemaphoreType.DMA((len(plan),))] * 2,
        ),
        compiler_params=MOVE_PARAMS,
        cost_estimate=cost(sum(rows * cols for rows, cols in shapes), 1, 0, 2),
    )(me, *arrays)


def parts_of(rows):
    height = rows // 8 if rows % BLOCK == 0 else rows
    return [(r, height) for r in range(0, rows, height)]


def column_moves(me, rows, cols, group, first, target):
    col = pl.multiple_of(me * group + first, BLOCK)
    return [(0, r, col, height, cols, target, r, 0) for r, height in parts_of(rows)]


def group_spec(rows, unit, groups, first, d=0):
    return pl.BlockSpec((rows, unit), lambda j, me: (0, (me[0] ^ d) * groups + first + j))


def chunk_spec(rows, unit, first=0):
    return pl.BlockSpec((rows, unit), lambda j, me: (0, first + j))


def left_spec(rank, unit):
    return pl.BlockSpec((rank, unit), lambda j, me: (0, 0))


def whole_spec(array):
    return pl.BlockSpec(array.shape, lambda j, me: (0, 0))


def cost(rows, cols, rank, passes):
    return pl.CostEstimate(
        flops=2 * rows * cols * rank // SCALE, bytes_accessed=2 * passes * rows * cols // SCALE, transcendentals=0
    )


def pack(me, base, tp, distances, first, cols):
    rows, group = base.shape[0], base.shape[1] // tp

    def moves(me):
        return [m for i, d in enumerate(distances) for m in column_moves(me ^ d, rows, cols, group, first, i)]

    return move(me, [base], [(rows, cols)] * len(distances), moves)


def pack_first(me, base, tp, d, left, right, late, cols):
    rows, group = base.shape[0], base.shape[1] // tp
    rank, lane = left.shape
    late_cols = late[1] - late[0]

    def moves(me):
        extras = [
            (1, 0, 0, rank, lane, 0, rows, 0),
            (1, 0, 0, rank, lane, 1, 0, 0),
            (2, 0, late[0], rank, late_cols, 0, rows, lane),
            (2, 0, late[0], rank, late_cols, 1, 0, lane),
        ]
        return column_moves(me ^ d, rows, cols, group, 0, 0) + extras

    return move(me, [base, left, right], [(rows + rank, cols), (rank, lane + late_cols)], moves, direct=True)


def pack_carrier(me, base, tp, distances, terms, first, cols):
    rows, group = base.shape[0], base.shape[1] // tp

    def moves(me):
        result = []
        for i, d in enumerate(distances):
            result += column_moves(me ^ d, rows, cols, group, first, i)
            if d % 2 == 0:
                result.append((1, d // 2 * SUMS_ROWS, 0, SUMS_ROWS, terms.shape[1], i, rows, 0))
        return result

    return move(me, [base, terms], [(rows + (d + 1) % 2 * SUMS_ROWS, cols) for d in distances], moves)


def pack_near(me, base, tp):
    rows, group = base.shape[0], base.shape[1] // tp

    def moves(me):
        result = []
        for s in range(2):
            for source, r, col, *rest in column_moves((me // 2) * 2 + s, rows, group, group, 0, 0):
                result.append((source, r, col, *rest[:-2], s * rows + r, 0))
        return result

    return move(me, [base], [(2 * rows, group)], moves)[0]


def near_spec(rows, unit, first):
    return pl.BlockSpec((rows, unit), lambda j, me: ((me[0] % 2) ^ 1, first + j))


def low_rank(extra_ref, start, height, right):
    left = extra_ref[pl.ds(0, right.shape[0]), pl.ds(start, height)]
    return lax.dot_general(left, right, (((0,), (0,)), ((), ())), preferred_element_type=jnp.float32)


def squares_of(piece_ref, extra_ref, right):
    rows, cols = piece_ref.shape
    height = min(rows, BLOCK)
    total = jnp.zeros((8, cols), jnp.float32)
    for r in range(0, rows, height):
        combined = piece_ref[pl.ds(r, height), :].astype(jnp.float32) + low_rank(extra_ref, r, height, right)
        total = total + jnp.sum((combined * combined).reshape(height // 8, 8, cols), axis=0)
    return total


def squares_kernel(number, me_ref, *refs):
    pieces, extras, right_ref, out_ref = refs[:number], refs[number : 2 * number], refs[2 * number], refs[-1]
    right = right_ref[...]
    total = sum(squares_of(piece, extra, right) for piece, extra in zip(pieces, extras))
    total = jnp.sum(total, axis=0, keepdims=True)
    out_ref[...] = total + refs[-2][...] if len(refs) > 2 * number + 2 else total


def sender_squares_kernel(tp, me_ref, *refs):
    pieces, rights, left, sums_ref = refs[:tp], refs[tp : 2 * tp], refs[-2], refs[-1]
    for d in range(tp):
        sums_ref[pl.ds(d, 1), :] = jnp.sum(squares_of(pieces[d], left, rights[d][...]), axis=0, keepdims=True)


def terms_kernel(sums_ref, terms_ref):
    line = lax.broadcasted_iota(jnp.int32, (SUMS_ROWS, sums_ref.shape[1]), 0)
    for i in range(sums_ref.shape[0]):
        sums = sums_ref[pl.ds(i, 1), :]
        block = jnp.zeros(line.shape, jnp.float32)
        for term in range(TERMS):
            part = sums.astype(jnp.bfloat16).astype(jnp.float32)
            block = jnp.where(line == term, part, block)
            sums = sums - part
        terms_ref[pl.ds(i * SUMS_ROWS, SUMS_ROWS), :] = block.astype(jnp.bfloat16)


def terms_of(sums):
    rows, cols = sums.shape
    return pl.pallas_call(
        terms_kernel,
        out_shape=jax.ShapeDtypeStruct((rows * SUMS_ROWS, cols), jnp.bfloat16),
        compiler_params=PARAMS,
        cost_estimate=cost(rows, cols, 0, 2),
    )(sums)


def piece_specs(tp, rows, unit, groups, first):
    specs = [group_spec(rows, unit, groups, first), near_spec(rows, unit, first)]
    return specs + [chunk_spec(rows, unit)] * (tp - 2)


def column_squares(me, base, near, received, extras, right, ds, unit, first, count, previous=None):
    rows = base.shape[0]
    rank, cols = right.shape
    pieces = [base, near, *received]
    specs = piece_specs(len(extras), rows, unit, cols // unit, first)
    in_specs = [specs[d] for d in ds] + [left_spec(rank, max(rows, BLOCK))] * len(ds) + [chunk_spec(rank, unit, first)]
    args = [pieces[d] for d in ds] + [extras[d] for d in ds] + [right]
    if previous is not None:
        in_specs.append(chunk_spec(1, unit))
        args.append(previous)
    return pl.pallas_call(
        functools.partial(squares_kernel, len(ds)),
        out_shape=jax.ShapeDtypeStruct((1, count * unit), jnp.float32),
        grid_spec=pltpu.PrefetchScalarGridSpec(
            num_scalar_prefetch=1,
            grid=(count,),
            in_specs=in_specs,
            out_specs=chunk_spec(1, unit),
        ),
        compiler_params=PARAMS,
        cost_estimate=cost(len(ds) * rows, count * unit, rank, 1),
    )(me, *args)


def sender_squares(me, base, extras, rank, unit, first, count, lane):
    rows = base.shape[0]
    tp = len(extras)
    groups = base.shape[1] // (tp * unit)
    return pl.pallas_call(
        functools.partial(sender_squares_kernel, tp),
        out_shape=jax.ShapeDtypeStruct((tp, count * unit), jnp.float32),
        grid_spec=pltpu.PrefetchScalarGridSpec(
            num_scalar_prefetch=1,
            grid=(count,),
            in_specs=[group_spec(rows, unit, groups, first, d) for d in range(tp)]
            + [chunk_spec(rank, unit, lane // unit)] * tp
            + [left_spec(rank, lane)],
            out_specs=chunk_spec(tp, unit),
        ),
        compiler_params=PARAMS,
        cost_estimate=cost(tp * rows, count * unit, rank, 1),
    )(me, *[base] * tp, *extras, extras[0])


def export_kernel(tp, ds, first, me_ref, *refs):
    number = len(ds)
    pieces, extras = refs[:number], refs[number : 2 * number]
    right_ref, squares_ref, mag_ref = refs[2 * number : 2 * number + 3]
    out_ref, scales_ref = refs[-2:]
    rows, cols = pieces[0].shape
    step = pl.program_id(0)
    if len(refs) > 2 * number + 5:
        @pl.when(step == 0)
        def _():
            scales_ref[...] = refs[2 * number + 4][...]

    factor = mag_ref[...] / jnp.sqrt(squares_ref[...] + EPSILON)
    right = right_ref[...]
    lane = lax.broadcasted_iota(jnp.int32, (1, scales_ref.shape[1]), 1)
    per_step = cols // BLOCK

    def merge(i, r, height):
        combined = pieces[i][pl.ds(r, height), :].astype(jnp.float32) + low_rank(extras[i], r, height, right)
        return (combined * factor).astype(jnp.bfloat16)

    def finish(merged, span, block):
        line = scales_ref[pl.ds(block, 1), :]
        for j in range(per_step):
            tile = merged[:, j * BLOCK : (j + 1) * BLOCK].astype(jnp.float32)
            largest = jnp.max(jnp.max(jnp.abs(tile), axis=0, keepdims=True), axis=1, keepdims=True)
            out_ref[span, pl.ds(j * BLOCK, BLOCK)] = (tile * (1.0 / (largest + EPSILON))).astype(jnp.bfloat16)
            line = jnp.where(lane == (first + step) * per_step + j, largest, line)
        scales_ref[pl.ds(block, 1), :] = line

    if rows % BLOCK == 0:
        for i, d in enumerate(ds):
            place = me_ref[0] ^ d
            start = place * rows if out_ref.shape[0] > rows else 0
            for r in range(0, rows, BLOCK):
                span = pl.ds(pl.multiple_of(start + r, BLOCK), BLOCK)
                finish(merge(i, r, BLOCK), span, place * (rows // BLOCK) + r // BLOCK)
    else:
        for i, d in enumerate(ds):
            out_ref[pl.ds(pl.multiple_of((me_ref[0] ^ d) * rows, rows), rows), :] = merge(i, 0, rows)
        for block in range(tp * rows // BLOCK):
            span = pl.ds(block * BLOCK, BLOCK)
            finish(out_ref[span, :], span, block)


def export_chunk(me, base, near, received, extras, right, squares, mag, ds, unit, first, count, previous):
    rows = base.shape[0]
    rank, cols = right.shape
    tp = len(extras)
    groups = cols // unit
    result = (
        jax.ShapeDtypeStruct((tp * rows, cols), jnp.bfloat16),
        jax.ShapeDtypeStruct((tp * rows // BLOCK, cols // BLOCK), jnp.float32),
    )
    pieces = [base, near, *received]
    specs = piece_specs(tp, rows, unit, groups, first)
    in_specs = (
        [specs[d] for d in ds]
        + [left_spec(rank, max(rows, BLOCK))] * len(ds)
        + [chunk_spec(rank, unit, first), chunk_spec(1, unit), group_spec(1, unit, groups, first)]
    )
    args = [pieces[d] for d in ds] + [extras[d] for d in ds] + [right, squares, mag]
    aliases = {}
    if previous is not None:
        in_specs += [pl.BlockSpec(memory_space=pl.ANY), whole_spec(previous[1])]
        args += list(previous)
        aliases = {len(args) - 1: 0}
    if len(ds) == 1:
        out_spec = pl.BlockSpec((rows, unit), lambda j, me: (me[0] ^ ds[0], first + j))
    else:
        out_spec = chunk_spec(tp * rows, unit, first)
    return pl.pallas_call(
        functools.partial(export_kernel, tp, ds, first),
        out_shape=result,
        grid_spec=pltpu.PrefetchScalarGridSpec(
            num_scalar_prefetch=1,
            grid=(count,),
            in_specs=in_specs,
            out_specs=(out_spec, whole_spec(result[1])),
        ),
        input_output_aliases=aliases,
        compiler_params=PARAMS,
        cost_estimate=cost(len(ds) * rows, count * unit, rank, 2),
    )(me, *args)


def body(tp, fsdp, base, left, right, magnitude):
    rows, rank = left.shape
    cols = right.shape[1]
    blocks = cols // BLOCK
    chunks, early = chunk_blocks(blocks)
    mag = magnitude.reshape(1, -1)
    me = lax.axis_index("tp").astype(jnp.int32).reshape(1)
    lane = -(-rows // BLOCK) * BLOCK
    left = jnp.pad(left.T, ((0, 0), (0, lane - rows)))
    late = (chunks[early][0], chunks[-1][1])
    far = range(2, tp)
    received = {}

    def span(k):
        a, b = chunks[k]
        return a * BLOCK, (b - a) * BLOCK

    def units(k):
        a, b = chunks[k]
        width = width_of(a, b, blocks)
        return width * BLOCK, a // width, (b - a) // width

    def send(k, pieces):
        received[k] = [swap(piece, d, tp) for d, piece in zip(far, pieces)]

    pieces = []
    for d in far:
        if d % 2 == 0:
            piece, own = pack_first(me, base, tp, d, left, right, (late[0] * BLOCK, late[1] * BLOCK), span(0)[1])
        else:
            piece = pack(after(me, own), base, tp, (d,), *span(0))[0]
        pieces.append(piece)
    send(0, pieces)
    pieces = pack(after(me, *pieces), base, tp, far, *span(1))
    send(1, pieces)
    near = lax.all_to_all(
        pack_near(after(me, *pieces), base, tp), "tp", 0, 0, tiled=True,
        axis_index_groups=[[i, i + 1] for i in range(0, tp, 2)],
    )

    even = [own] + [received[0][d - 2][rows:, : own.shape[1]] for d in far[::2]]
    odd = swap(jnp.concatenate(even), 1, tp)
    extras = []
    for i in range(tp // 2):
        extras += [even[i], odd[i * rank : (i + 1) * rank]]

    apart = rows % BLOCK == 0 and len(chunks) == early + 1
    every = tuple(range(tp))
    result = None
    token = ()
    totals = {}

    def export(k, ds):
        nonlocal result
        result = export_chunk(me, base, near, received.get(k, ()), extras, right, totals[k], mag, ds, *units(k), result)

    for k in range(len(chunks)):
        following = k + AHEAD
        if following < len(chunks):
            turn = after(me, *received[k], *token)
            if following == CARRIER:
                width = width_of(late[0], late[1] - late[0], blocks, lane // BLOCK)
                sums = sender_squares(
                    turn, base, extras, rank, width * BLOCK, late[0] // width, (late[1] - late[0]) // width, lane
                )
                sums = sums[0::2] + swap(sums[1::2], 1, tp)
                late_sums = sums[:1]
                send(following, pack_carrier(turn, base, tp, far, terms_of(sums), *span(following)))
            else:
                send(following, pack(turn, base, tp, far, *span(following)))
        if k < early:
            if apart and k == early - 1:
                export(early, every[:2])
                token = (result[1],)
            turn = after(me, *token)
            local = None
            for ds in (every[:-1], every[-1:]) if apart and k == early - 1 else (every,):
                local = column_squares(turn, base, near, received[k], extras, right, ds, *units(k), local)
            if k == CARRIER:
                for piece in received[k][::2]:
                    parts = after(piece, *token)[rows : rows + TERMS, : late_sums.shape[1]].astype(jnp.float32)
                    late_sums = late_sums + jnp.sum(parts, axis=0, keepdims=True)
                local = jnp.concatenate([local, late_sums], axis=1)
            total = lax.psum(local, "fsdp") if k < early - 1 else total_of(local, fsdp, "fsdp")
            totals[k] = total[:, : span(k)[1]]
            if k == CARRIER:
                for i in range(early, len(chunks)):
                    start = span(k)[1] + span(i)[0] - late[0] * BLOCK
                    totals[i] = total[:, start : start + span(i)[1]]
        if apart and k == early:
            for d in far:
                export(k, (d,))
        else:
            export(k, every)
        token = (result[1],)
    return result


def solution(mesh):
    in_specs = (P(("fsdp", "tp"), None), P(("fsdp", "tp"), None), P(None, "tp"), P())
    out_specs = (P("fsdp", "tp"), P("fsdp", "tp"))
    return jax.shard_map(
        functools.partial(body, mesh.shape["tp"], mesh.shape["fsdp"]), mesh=mesh, in_specs=in_specs, out_specs=out_specs, check_vma=False
    )
```

```python
import functools

import jax
import jax.numpy as jnp
from jax import lax
from jax.experimental import pallas as pl
from jax.experimental.pallas import tpu as pltpu
from jax.sharding import PartitionSpec as P

BLOCK = 128
EPSILON = 1e-06
EARLY = (8, 8, 8, 8, 8, 8)
LATE = (4,)
AHEAD = 2
SCALE = 3
CARRIER = 4
TERMS = 3
SUMS_ROWS = 16
PARAMS = pltpu.CompilerParams(vmem_limit_bytes=52 * 2**20)
MOVE_PARAMS = pltpu.CompilerParams(vmem_limit_bytes=56 * 2**20)


def chunk_blocks(total):
    parts = EARLY + LATE
    bounds = [total * sum(parts[:i]) // sum(parts) for i in range(len(parts) + 1)]
    chunks = [(a, b) for a, b in zip(bounds, bounds[1:]) if b > a]
    return chunks, sum(a < bounds[len(EARLY)] for a, _ in chunks)


def width_of(*counts):
    return max(d for d in (4, 2, 1) if all(count % d == 0 for count in counts))


def after(value, *others):
    return lax.optimization_barrier((value, *others))[0]


def swap(array, d, size, axis="tp"):
    return lax.ppermute(array, axis, [(i, i ^ d) for i in range(size)])


def total_of(array, size, axis):
    d = 1
    while d < size:
        others = (d,) if 2 * d == size else (d, 2 * d, 3 * d)
        array = array + sum(swap(array, other, size, axis) for other in others)
        d *= 1 + len(others)
    return array


def move_kernel(moves, number, direct, me_ref, *refs):
    plan = moves(me_ref[0], me_ref[1])
    holds = () if direct else refs[-len(plan) - 2 : -2]
    sources, targets = refs[:number], refs[number : len(refs) - len(holds) - 2]
    came, went = refs[-2:]
    ins, outs = [], []
    for i, (source, row, col, rows, cols, target, to_row, to_col) in enumerate(plan):
        block = sources[source].at[pl.ds(row, rows), pl.ds(col, cols)]
        place = targets[target].at[pl.ds(to_row, rows), pl.ds(to_col, cols)]
        ins.append(pltpu.make_async_copy(block, place if direct else holds[i], came.at[i]))
        if not direct:
            outs.append(pltpu.make_async_copy(holds[i], place, went.at[i]))
    for copy in ins:
        copy.start()
    for i, copy in enumerate(ins):
        copy.wait()
        if not direct:
            outs[i].start()
    for copy in outs:
        copy.wait()


def move(me, arrays, shapes, moves, direct=False):
    dtype = arrays[0].dtype
    plan = moves(0, 0)
    kind = pltpu.VMEM if direct else jax.ShapeDtypeStruct
    space = pltpu.VMEM if direct else pl.ANY
    return pl.pallas_call(
        functools.partial(move_kernel, moves, len(arrays), direct),
        out_shape=[kind(shape, dtype) for shape in shapes],
        grid_spec=pltpu.PrefetchScalarGridSpec(
            num_scalar_prefetch=1,
            grid=(1,),
            in_specs=[pl.BlockSpec(memory_space=pl.ANY)] * len(arrays),
            out_specs=[pl.BlockSpec(memory_space=space)] * len(shapes),
            scratch_shapes=[pltpu.VMEM((rows, cols), dtype) for _, _, _, rows, cols, *_ in (() if direct else plan)]
            + [pltpu.SemaphoreType.DMA((len(plan),))] * 2,
        ),
        compiler_params=MOVE_PARAMS,
        cost_estimate=cost(sum(rows * cols for rows, cols in shapes), 1, 0, 2),
    )(me, *arrays)


def parts_of(rows):
    height = rows // 8 if rows % BLOCK == 0 else rows
    return [(r, height) for r in range(0, rows, height)]


def column_moves(me, rows, cols, group, first, target):
    col = pl.multiple_of(me * group + first, BLOCK)
    return [(0, r, col, height, cols, target, r, 0) for r, height in parts_of(rows)]


def group_spec(rows, unit, groups, first, d=0):
    return pl.BlockSpec((rows, unit), lambda j, me: (0, (me[0] ^ d) * groups + first + j))


def chunk_spec(rows, unit, first=0):
    return pl.BlockSpec((rows, unit), lambda j, me: (0, first + j))


def left_spec(rank, unit):
    return pl.BlockSpec((rank, unit), lambda j, me: (0, 0))


def whole_spec(array):
    return pl.BlockSpec(array.shape, lambda j, me: (0, 0))


def cost(rows, cols, rank, passes):
    return pl.CostEstimate(
        flops=2 * rows * cols * rank // SCALE, bytes_accessed=2 * passes * rows * cols // SCALE, transcendentals=0
    )


def pack(me, base, tp, distances, first, cols):
    rows, group = base.shape[0], base.shape[1] // tp

    def moves(me, line):
        return [m for i, d in enumerate(distances) for m in column_moves(me ^ d, rows, cols, group, first, i)]

    return move(me, [base], [(rows, cols)] * len(distances), moves)


def pack_first(me, base, tp, d, left, right, late, cols):
    rows, group = base.shape[0], base.shape[1] // tp
    rank, lane = left.shape
    late_cols = late[1] - late[0]
    half, quarter = rank // 2, rank // 4

    def moves(me, line):
        result = column_moves(me ^ d, rows, cols, group, 0, 0)
        for i in range(2):
            result.append((1, i * half, 0, half, lane, 0, rows, i * lane))
            row = pl.multiple_of(line % 2 * half + i * quarter, quarter)
            result.append((2, row, late[0], quarter, late_cols, 0, rows + half, i * late_cols))
        return result

    return move(me, [base, left, right], [(rows + half + quarter, cols)], moves, direct=True)[0]


def pack_carrier(me, base, tp, distances, terms, first, cols):
    rows, group = base.shape[0], base.shape[1] // tp

    def moves(me, line):
        result = []
        for i, d in enumerate(distances):
            result += column_moves(me ^ d, rows, cols, group, first, i)
            if d % 2 == 0:
                result.append((1, d // 2 * SUMS_ROWS, 0, SUMS_ROWS, terms.shape[1], i, rows, 0))
        return result

    return move(me, [base, terms], [(rows + (d + 1) % 2 * SUMS_ROWS, cols) for d in distances], moves)


def pack_near(me, base, tp):
    rows, group = base.shape[0], base.shape[1] // tp

    def moves(me, line):
        result = []
        for s in range(2):
            for source, r, col, *rest in column_moves((me // 2) * 2 + s, rows, group, group, 0, 0):
                result.append((source, r, col, *rest[:-2], s * rows + r, 0))
        return result

    return move(me, [base], [(2 * rows, group)], moves)[0]


def near_spec(rows, unit, first):
    return pl.BlockSpec((rows, unit), lambda j, me: ((me[0] % 2) ^ 1, first + j))


def low_rank(extra_ref, start, height, right):
    left = extra_ref[pl.ds(0, right.shape[0]), pl.ds(start, height)]
    return lax.dot_general(left, right, (((0,), (0,)), ((), ())), preferred_element_type=jnp.float32)


def squares_of(piece_ref, extra_ref, right):
    rows, cols = piece_ref.shape
    height = min(rows, BLOCK)
    total = jnp.zeros((8, cols), jnp.float32)
    for r in range(0, rows, height):
        combined = piece_ref[pl.ds(r, height), :].astype(jnp.float32) + low_rank(extra_ref, r, height, right)
        total = total + jnp.sum((combined * combined).reshape(height // 8, 8, cols), axis=0)
    return total


def squares_kernel(number, me_ref, *refs):
    pieces, extras, right_ref, out_ref = refs[:number], refs[number : 2 * number], refs[2 * number], refs[-1]
    right = right_ref[...]
    total = sum(squares_of(piece, extra, right) for piece, extra in zip(pieces, extras))
    total = jnp.sum(total, axis=0, keepdims=True)
    out_ref[...] = total + refs[-2][...] if len(refs) > 2 * number + 2 else total


def sender_squares_kernel(tp, me_ref, *refs):
    pieces, rights, left, sums_ref = refs[:tp], refs[tp : 2 * tp], refs[-2], refs[-1]
    for d in range(tp):
        sums_ref[pl.ds(d, 1), :] = jnp.sum(squares_of(pieces[d], left, rights[d][...]), axis=0, keepdims=True)


def terms_kernel(sums_ref, terms_ref):
    line = lax.broadcasted_iota(jnp.int32, (SUMS_ROWS, sums_ref.shape[1]), 0)
    for i in range(sums_ref.shape[0]):
        sums = sums_ref[pl.ds(i, 1), :]
        block = jnp.zeros(line.shape, jnp.float32)
        for term in range(TERMS):
            part = sums.astype(jnp.bfloat16).astype(jnp.float32)
            block = jnp.where(line == term, part, block)
            sums = sums - part
        terms_ref[pl.ds(i * SUMS_ROWS, SUMS_ROWS), :] = block.astype(jnp.bfloat16)


def terms_of(sums):
    rows, cols = sums.shape
    return pl.pallas_call(
        terms_kernel,
        out_shape=jax.ShapeDtypeStruct((rows * SUMS_ROWS, cols), jnp.bfloat16),
        compiler_params=PARAMS,
        cost_estimate=cost(rows, cols, 0, 2),
    )(sums)


def piece_specs(tp, rows, unit, groups, first):
    specs = [group_spec(rows, unit, groups, first), near_spec(rows, unit, first)]
    return specs + [chunk_spec(rows, unit)] * (tp - 2)


def column_squares(me, base, near, received, extras, right, ds, unit, first, count, previous=None):
    rows = base.shape[0]
    rank, cols = right.shape
    pieces = [base, near, *received]
    specs = piece_specs(len(extras), rows, unit, cols // unit, first)
    in_specs = [specs[d] for d in ds] + [left_spec(rank, max(rows, BLOCK))] * len(ds) + [chunk_spec(rank, unit, first)]
    args = [pieces[d] for d in ds] + [extras[d] for d in ds] + [right]
    if previous is not None:
        in_specs.append(chunk_spec(1, unit))
        args.append(previous)
    return pl.pallas_call(
        functools.partial(squares_kernel, len(ds)),
        out_shape=jax.ShapeDtypeStruct((1, count * unit), jnp.float32),
        grid_spec=pltpu.PrefetchScalarGridSpec(
            num_scalar_prefetch=1,
            grid=(count,),
            in_specs=in_specs,
            out_specs=chunk_spec(1, unit),
        ),
        compiler_params=PARAMS,
        cost_estimate=cost(len(ds) * rows, count * unit, rank, 1),
    )(me, *args)


def sender_squares(me, base, left, rights, unit, first, count):
    rows = base.shape[0]
    tp = len(rights)
    groups = base.shape[1] // (tp * unit)
    rank = left.shape[0]
    return pl.pallas_call(
        functools.partial(sender_squares_kernel, tp),
        out_shape=jax.ShapeDtypeStruct((tp, count * unit), jnp.float32),
        grid_spec=pltpu.PrefetchScalarGridSpec(
            num_scalar_prefetch=1,
            grid=(count,),
            in_specs=[group_spec(rows, unit, groups, first, d) for d in range(tp)]
            + [chunk_spec(rank, unit)] * tp
            + [whole_spec(left)],
            out_specs=chunk_spec(tp, unit),
        ),
        compiler_params=PARAMS,
        cost_estimate=cost(tp * rows, count * unit, rank, 1),
    )(me, *[base] * tp, *rights, left)


def export_kernel(tp, ds, first, me_ref, *refs):
    number = len(ds)
    pieces, extras = refs[:number], refs[number : 2 * number]
    right_ref, squares_ref, mag_ref = refs[2 * number : 2 * number + 3]
    out_ref, scales_ref = refs[-2:]
    rows, cols = pieces[0].shape
    step = pl.program_id(0)
    if len(refs) > 2 * number + 5:
        @pl.when(step == 0)
        def _():
            scales_ref[...] = refs[2 * number + 4][...]

    factor = mag_ref[...] / jnp.sqrt(squares_ref[...] + EPSILON)
    right = right_ref[...]
    lane = lax.broadcasted_iota(jnp.int32, (1, scales_ref.shape[1]), 1)
    per_step = cols // BLOCK

    def merge(i, r, height):
        combined = pieces[i][pl.ds(r, height), :].astype(jnp.float32) + low_rank(extras[i], r, height, right)
        return (combined * factor).astype(jnp.bfloat16)

    def finish(merged, span, block):
        line = scales_ref[pl.ds(block, 1), :]
        for j in range(per_step):
            tile = merged[:, j * BLOCK : (j + 1) * BLOCK].astype(jnp.float32)
            largest = jnp.max(jnp.max(jnp.abs(tile), axis=0, keepdims=True), axis=1, keepdims=True)
            out_ref[span, pl.ds(j * BLOCK, BLOCK)] = (tile * (1.0 / (largest + EPSILON))).astype(jnp.bfloat16)
            line = jnp.where(lane == (first + step) * per_step + j, largest, line)
        scales_ref[pl.ds(block, 1), :] = line

    if rows % BLOCK == 0:
        for i, d in enumerate(ds):
            place = me_ref[0] ^ d
            start = place * rows if out_ref.shape[0] > rows else 0
            for r in range(0, rows, BLOCK):
                span = pl.ds(pl.multiple_of(start + r, BLOCK), BLOCK)
                finish(merge(i, r, BLOCK), span, place * (rows // BLOCK) + r // BLOCK)
    else:
        for i, d in enumerate(ds):
            out_ref[pl.ds(pl.multiple_of((me_ref[0] ^ d) * rows, rows), rows), :] = merge(i, 0, rows)
        for block in range(tp * rows // BLOCK):
            span = pl.ds(block * BLOCK, BLOCK)
            finish(out_ref[span, :], span, block)


def export_chunk(me, base, near, received, extras, right, squares, mag, ds, unit, first, count, previous):
    rows = base.shape[0]
    rank, cols = right.shape
    tp = len(extras)
    groups = cols // unit
    result = (
        jax.ShapeDtypeStruct((tp * rows, cols), jnp.bfloat16),
        jax.ShapeDtypeStruct((tp * rows // BLOCK, cols // BLOCK), jnp.float32),
    )
    pieces = [base, near, *received]
    specs = piece_specs(tp, rows, unit, groups, first)
    in_specs = (
        [specs[d] for d in ds]
        + [left_spec(rank, max(rows, BLOCK))] * len(ds)
        + [chunk_spec(rank, unit, first), chunk_spec(1, unit), group_spec(1, unit, groups, first)]
    )
    args = [pieces[d] for d in ds] + [extras[d] for d in ds] + [right, squares, mag]
    aliases = {}
    if previous is not None:
        in_specs += [pl.BlockSpec(memory_space=pl.ANY), whole_spec(previous[1])]
        args += list(previous)
        aliases = {len(args) - 1: 0}
    if len(ds) == 1:
        out_spec = pl.BlockSpec((rows, unit), lambda j, me: (me[0] ^ ds[0], first + j))
    else:
        out_spec = chunk_spec(tp * rows, unit, first)
    return pl.pallas_call(
        functools.partial(export_kernel, tp, ds, first),
        out_shape=result,
        grid_spec=pltpu.PrefetchScalarGridSpec(
            num_scalar_prefetch=1,
            grid=(count,),
            in_specs=in_specs,
            out_specs=(out_spec, whole_spec(result[1])),
        ),
        input_output_aliases=aliases,
        compiler_params=PARAMS,
        cost_estimate=cost(len(ds) * rows, count * unit, rank, 2),
    )(me, *args)


def body(tp, fsdp, base, left, right, magnitude):
    rows, rank = left.shape
    cols = right.shape[1]
    blocks = cols // BLOCK
    chunks, early = chunk_blocks(blocks)
    mag = magnitude.reshape(1, -1)
    line = lax.axis_index("fsdp").astype(jnp.int32)
    me = jnp.stack([lax.axis_index("tp").astype(jnp.int32), line])
    lane = -(-rows // BLOCK) * BLOCK
    left = jnp.pad(left.T, ((0, 0), (0, lane - rows)))
    late = (chunks[early][0], chunks[-1][1])
    far = range(2, tp)
    received = {}

    def span(k):
        a, b = chunks[k]
        return a * BLOCK, (b - a) * BLOCK

    def units(k):
        a, b = chunks[k]
        width = width_of(a, b, blocks)
        return width * BLOCK, a // width, (b - a) // width

    def send(k, pieces):
        received[k] = [swap(piece, d, tp) for d, piece in zip(far, pieces)]

    pieces = []
    for d in far:
        if d % 2 == 0:
            piece = pack_first(me, base, tp, d, left, right, (late[0] * BLOCK, late[1] * BLOCK), span(0)[1])
        else:
            piece = pack(after(me, *pieces), base, tp, (d,), *span(0))[0]
        pieces.append(piece)
    send(0, pieces)
    pieces = pack(after(me, *pieces), base, tp, far, *span(1))
    send(1, pieces)
    near = lax.all_to_all(
        pack_near(after(me, *pieces), base, tp), "tp", 0, 0, tiled=True,
        axis_index_groups=[[i, i + 1] for i in range(0, tp, 2)],
    )

    def unfold(block, width):
        return jnp.concatenate([block[:, :width], block[:, width : 2 * width]])

    def alternate(even):
        odd = swap(jnp.concatenate(even), 1, tp)
        return [array for i, own in enumerate(even) for array in (own, odd[i * rank : (i + 1) * rank])]

    arrived = [received[0][d - 2] for d in far[::2]]
    half, late_cols = rank // 2, (late[1] - late[0]) * BLOCK
    extras = alternate([left] + [unfold(piece[rows : rows + half], lane) for piece in arrived])

    def late_rights():
        mine = jnp.concatenate([unfold(piece[rows + half :], late_cols) for piece in arrived], axis=1)
        other = swap(mine, 1, fsdp, "fsdp")
        both = jnp.where(line % 2 == 0, jnp.concatenate([mine, other]), jnp.concatenate([other, mine]))
        even = [right[:, late[0] * BLOCK : late[1] * BLOCK]]
        even += [both[:, i * late_cols : (i + 1) * late_cols] for i in range(len(arrived))]
        return alternate(even)

    apart = rows % BLOCK == 0 and len(chunks) == early + 1
    every = tuple(range(tp))
    result = None
    token = ()
    totals = {}

    def export(k, ds):
        nonlocal result
        result = export_chunk(me, base, near, received.get(k, ()), extras, right, totals[k], mag, ds, *units(k), result)

    for k in range(len(chunks)):
        following = k + AHEAD
        if following < len(chunks):
            turn = after(me, *received[k], *token)
            if following == CARRIER:
                width = width_of(late[0], late[1] - late[0], blocks)
                sums = sender_squares(
                    turn, base, left, late_rights(), width * BLOCK, late[0] // width, (late[1] - late[0]) // width
                )
                sums = sums[0::2] + swap(sums[1::2], 1, tp)
                late_sums = sums[:1]
                send(following, pack_carrier(turn, base, tp, far, terms_of(sums), *span(following)))
            else:
                send(following, pack(turn, base, tp, far, *span(following)))
        if k < early:
            if apart and k == early - 1:
                export(early, every[:2])
                token = (result[1],)
            turn = after(me, *token)
            local = None
            for ds in (every[:-1], every[-1:]) if apart and k == early - 1 else (every,):
                local = column_squares(turn, base, near, received[k], extras, right, ds, *units(k), local)
            if k == CARRIER:
                for piece in received[k][::2]:
                    parts = after(piece, *token)[rows : rows + TERMS, : late_sums.shape[1]].astype(jnp.float32)
                    late_sums = late_sums + jnp.sum(parts, axis=0, keepdims=True)
                local = jnp.concatenate([local, late_sums], axis=1)
            total = lax.psum(local, "fsdp") if k < early - 1 else total_of(local, fsdp, "fsdp")
            totals[k] = total[:, : span(k)[1]]
            if k == CARRIER:
                for i in range(early, len(chunks)):
                    start = span(k)[1] + span(i)[0] - late[0] * BLOCK
                    totals[i] = total[:, start : start + span(i)[1]]
        if apart and k == early:
            for d in far:
                export(k, (d,))
        else:
            export(k, every)
        token = (result[1],)
    return result


def solution(mesh):
    in_specs = (P(("fsdp", "tp"), None), P(("fsdp", "tp"), None), P(None, "tp"), P())
    out_specs = (P("fsdp", "tp"), P("fsdp", "tp"))
    return jax.shard_map(
        functools.partial(body, mesh.shape["tp"], mesh.shape["fsdp"]), mesh=mesh, in_specs=in_specs, out_specs=out_specs, check_vma=False
    )
```

```python
import functools

import jax
import jax.numpy as jnp
from jax import lax
from jax.experimental import pallas as pl
from jax.experimental.pallas import tpu as pltpu
from jax.sharding import PartitionSpec as P

BLOCK = 128
EPSILON = 1e-06
EARLY = (8, 8, 8, 8, 8, 8)
LATE = (4,)
AHEAD = 2
SCALE = 3
CARRIER = 4
TERMS = 3
SUMS_ROWS = 16
PARAMS = pltpu.CompilerParams(vmem_limit_bytes=52 * 2**20)
MOVE_PARAMS = pltpu.CompilerParams(vmem_limit_bytes=56 * 2**20)


def chunk_blocks(total):
    parts = EARLY + LATE
    bounds = [total * sum(parts[:i]) // sum(parts) for i in range(len(parts) + 1)]
    chunks = [(a, b) for a, b in zip(bounds, bounds[1:]) if b > a]
    return chunks, sum(a < bounds[len(EARLY)] for a, _ in chunks)


def width_of(*counts):
    return max(d for d in (4, 2, 1) if all(count % d == 0 for count in counts))


def after(value, *others):
    return lax.optimization_barrier((value, *others))[0]


def swap(array, d, size, axis="tp"):
    return lax.ppermute(array, axis, [(i, i ^ d) for i in range(size)])


def total_of(array, size, axis):
    d = 1
    while d < size:
        others = (d,) if 2 * d == size else (d, 2 * d, 3 * d)
        array = array + sum(swap(array, other, size, axis) for other in others)
        d *= 1 + len(others)
    return array


def move_kernel(moves, number, direct, me_ref, *refs):
    plan = moves(me_ref[0])
    holds = () if direct else refs[-len(plan) - 2 : -2]
    sources, targets = refs[:number], refs[number : len(refs) - len(holds) - 2]
    came, went = refs[-2:]
    ins, outs = [], []
    for i, (source, row, col, rows, cols, target, to_row, to_col) in enumerate(plan):
        block = sources[source].at[pl.ds(row, rows), pl.ds(col, cols)]
        place = targets[target].at[pl.ds(to_row, rows), pl.ds(to_col, cols)]
        ins.append(pltpu.make_async_copy(block, place if direct else holds[i], came.at[i]))
        if not direct:
            outs.append(pltpu.make_async_copy(holds[i], place, went.at[i]))
    for copy in ins:
        copy.start()
    for i, copy in enumerate(ins):
        copy.wait()
        if not direct:
            outs[i].start()
    for copy in outs:
        copy.wait()


def move(me, arrays, shapes, moves, direct=False):
    dtype = arrays[0].dtype
    plan = moves(0)
    kind = pltpu.VMEM if direct else jax.ShapeDtypeStruct
    space = pltpu.VMEM if direct else pl.ANY
    return pl.pallas_call(
        functools.partial(move_kernel, moves, len(arrays), direct),
        out_shape=[kind(shape, dtype) for shape in shapes],
        grid_spec=pltpu.PrefetchScalarGridSpec(
            num_scalar_prefetch=1,
            grid=(1,),
            in_specs=[pl.BlockSpec(memory_space=pl.ANY)] * len(arrays),
            out_specs=[pl.BlockSpec(memory_space=space)] * len(shapes),
            scratch_shapes=[pltpu.VMEM((rows, cols), dtype) for _, _, _, rows, cols, *_ in (() if direct else plan)]
            + [pltpu.SemaphoreType.DMA((len(plan),))] * 2,
        ),
        compiler_params=MOVE_PARAMS,
        cost_estimate=cost(sum(rows * cols for rows, cols in shapes), 1, 0, 2),
    )(me, *arrays)


def parts_of(rows):
    height = rows // 8 if rows % BLOCK == 0 else rows
    return [(r, height) for r in range(0, rows, height)]


def column_moves(me, rows, cols, group, first, target):
    col = pl.multiple_of(me * group + first, BLOCK)
    return [(0, r, col, height, cols, target, r, 0) for r, height in parts_of(rows)]


def group_spec(rows, unit, groups, first, d=0):
    return pl.BlockSpec((rows, unit), lambda j, me: (0, (me[0] ^ d) * groups + first + j))


def chunk_spec(rows, unit, first=0):
    return pl.BlockSpec((rows, unit), lambda j, me: (0, first + j))


def left_spec(rank, unit):
    return pl.BlockSpec((rank, unit), lambda j, me: (0, 0))


def whole_spec(array):
    return pl.BlockSpec(array.shape, lambda j, me: (0, 0))


def cost(rows, cols, rank, passes):
    return pl.CostEstimate(
        flops=2 * rows * cols * rank // SCALE, bytes_accessed=2 * passes * rows * cols // SCALE, transcendentals=0
    )


def pack(me, base, tp, distances, first, cols):
    rows, group = base.shape[0], base.shape[1] // tp

    def moves(me):
        return [m for i, d in enumerate(distances) for m in column_moves(me ^ d, rows, cols, group, first, i)]

    return move(me, [base], [(rows, cols)] * len(distances), moves)


def pack_first(place, base, tp, d, left, right, late, cols):
    rows, group = base.shape[0], base.shape[1] // tp
    rank, lane = left.shape
    late_cols = late[1] - late[0]
    half, quarter = rank // 2, rank // 4

    def moves(place):
        line, me = place // tp, place % tp
        result = column_moves(me ^ d, rows, cols, group, 0, 0)
        for i in range(2):
            result.append((1, i * half, 0, half, lane, 0, rows, i * lane))
            row = pl.multiple_of(line % 2 * half + i * quarter, quarter)
            result.append((2, row, late[0], quarter, late_cols, 0, rows + half, i * late_cols))
        return result

    return move(place, [base, left, right], [(rows + half + quarter, cols)], moves, direct=True)[0]


def pack_carrier(me, base, tp, distances, terms, first, cols):
    rows, group = base.shape[0], base.shape[1] // tp

    def moves(me):
        result = []
        for i, d in enumerate(distances):
            result += column_moves(me ^ d, rows, cols, group, first, i)
            if d % 2 == 0:
                result.append((1, d // 2 * SUMS_ROWS, 0, SUMS_ROWS, terms.shape[1], i, rows, 0))
        return result

    return move(me, [base, terms], [(rows + (d + 1) % 2 * SUMS_ROWS, cols) for d in distances], moves)


def pack_near(me, base, tp):
    rows, group = base.shape[0], base.shape[1] // tp

    def moves(me):
        result = []
        for s in range(2):
            for source, r, col, *rest in column_moves((me // 2) * 2 + s, rows, group, group, 0, 0):
                result.append((source, r, col, *rest[:-2], s * rows + r, 0))
        return result

    return move(me, [base], [(2 * rows, group)], moves)[0]


def near_spec(rows, unit, first):
    return pl.BlockSpec((rows, unit), lambda j, me: ((me[0] % 2) ^ 1, first + j))


def low_rank(extra_ref, start, height, right):
    left = extra_ref[pl.ds(0, right.shape[0]), pl.ds(start, height)]
    return lax.dot_general(left, right, (((0,), (0,)), ((), ())), preferred_element_type=jnp.float32)


def squares_of(piece_ref, extra_ref, right):
    rows, cols = piece_ref.shape
    height = min(rows, BLOCK)
    total = jnp.zeros((8, cols), jnp.float32)
    for r in range(0, rows, height):
        combined = piece_ref[pl.ds(r, height), :].astype(jnp.float32) + low_rank(extra_ref, r, height, right)
        total = total + jnp.sum((combined * combined).reshape(height // 8, 8, cols), axis=0)
    return total


def squares_kernel(number, me_ref, *refs):
    pieces, extras, right_ref, out_ref = refs[:number], refs[number : 2 * number], refs[2 * number], refs[-1]
    right = right_ref[...]
    total = sum(squares_of(piece, extra, right) for piece, extra in zip(pieces, extras))
    total = jnp.sum(total, axis=0, keepdims=True)
    out_ref[...] = total + refs[-2][...] if len(refs) > 2 * number + 2 else total


def sender_squares_kernel(tp, me_ref, *refs):
    pieces, rights, left, sums_ref = refs[:tp], refs[tp : 2 * tp], refs[-2], refs[-1]
    for d in range(tp):
        sums_ref[pl.ds(d, 1), :] = jnp.sum(squares_of(pieces[d], left, rights[d][...]), axis=0, keepdims=True)


def terms_kernel(sums_ref, terms_ref):
    line = lax.broadcasted_iota(jnp.int32, (SUMS_ROWS, sums_ref.shape[1]), 0)
    for i in range(sums_ref.shape[0]):
        sums = sums_ref[pl.ds(i, 1), :]
        block = jnp.zeros(line.shape, jnp.float32)
        for term in range(TERMS):
            part = sums.astype(jnp.bfloat16).astype(jnp.float32)
            block = jnp.where(line == term, part, block)
            sums = sums - part
        terms_ref[pl.ds(i * SUMS_ROWS, SUMS_ROWS), :] = block.astype(jnp.bfloat16)


def terms_of(sums):
    rows, cols = sums.shape
    return pl.pallas_call(
        terms_kernel,
        out_shape=jax.ShapeDtypeStruct((rows * SUMS_ROWS, cols), jnp.bfloat16),
        compiler_params=PARAMS,
        cost_estimate=cost(rows, cols, 0, 2),
    )(sums)


def piece_specs(tp, rows, unit, groups, first):
    specs = [group_spec(rows, unit, groups, first), near_spec(rows, unit, first)]
    return specs + [chunk_spec(rows, unit)] * (tp - 2)


def column_squares(me, base, near, received, extras, right, ds, unit, first, count, previous=None):
    rows = base.shape[0]
    rank, cols = right.shape
    pieces = [base, near, *received]
    specs = piece_specs(len(extras), rows, unit, cols // unit, first)
    in_specs = [specs[d] for d in ds] + [left_spec(rank, max(rows, BLOCK))] * len(ds) + [chunk_spec(rank, unit, first)]
    args = [pieces[d] for d in ds] + [extras[d] for d in ds] + [right]
    if previous is not None:
        in_specs.append(chunk_spec(1, unit))
        args.append(previous)
    return pl.pallas_call(
        functools.partial(squares_kernel, len(ds)),
        out_shape=jax.ShapeDtypeStruct((1, count * unit), jnp.float32),
        grid_spec=pltpu.PrefetchScalarGridSpec(
            num_scalar_prefetch=1,
            grid=(count,),
            in_specs=in_specs,
            out_specs=chunk_spec(1, unit),
        ),
        compiler_params=PARAMS,
        cost_estimate=cost(len(ds) * rows, count * unit, rank, 1),
    )(me, *args)


def sender_squares(me, base, left, rights, unit, first, count):
    rows = base.shape[0]
    tp = len(rights)
    groups = base.shape[1] // (tp * unit)
    rank = left.shape[0]
    return pl.pallas_call(
        functools.partial(sender_squares_kernel, tp),
        out_shape=jax.ShapeDtypeStruct((tp, count * unit), jnp.float32),
        grid_spec=pltpu.PrefetchScalarGridSpec(
            num_scalar_prefetch=1,
            grid=(count,),
            in_specs=[group_spec(rows, unit, groups, first, d) for d in range(tp)]
            + [chunk_spec(rank, unit)] * tp
            + [whole_spec(left)],
            out_specs=chunk_spec(tp, unit),
        ),
        compiler_params=PARAMS,
        cost_estimate=cost(tp * rows, count * unit, rank, 1),
    )(me, *[base] * tp, *rights, left)


def export_kernel(tp, ds, first, me_ref, *refs):
    number = len(ds)
    pieces, extras = refs[:number], refs[number : 2 * number]
    right_ref, squares_ref, mag_ref = refs[2 * number : 2 * number + 3]
    out_ref, scales_ref = refs[-2:]
    rows, cols = pieces[0].shape
    step = pl.program_id(0)
    if len(refs) > 2 * number + 5:
        @pl.when(step == 0)
        def _():
            scales_ref[...] = refs[2 * number + 4][...]

    factor = mag_ref[...] / jnp.sqrt(squares_ref[...] + EPSILON)
    right = right_ref[...]
    lane = lax.broadcasted_iota(jnp.int32, (1, scales_ref.shape[1]), 1)
    per_step = cols // BLOCK

    def merge(i, r, height):
        combined = pieces[i][pl.ds(r, height), :].astype(jnp.float32) + low_rank(extras[i], r, height, right)
        return (combined * factor).astype(jnp.bfloat16)

    def finish(merged, span, block):
        line = scales_ref[pl.ds(block, 1), :]
        for j in range(per_step):
            tile = merged[:, j * BLOCK : (j + 1) * BLOCK].astype(jnp.float32)
            largest = jnp.max(jnp.max(jnp.abs(tile), axis=0, keepdims=True), axis=1, keepdims=True)
            out_ref[span, pl.ds(j * BLOCK, BLOCK)] = (tile * (1.0 / (largest + EPSILON))).astype(jnp.bfloat16)
            line = jnp.where(lane == (first + step) * per_step + j, largest, line)
        scales_ref[pl.ds(block, 1), :] = line

    if rows % BLOCK == 0:
        for i, d in enumerate(ds):
            place = me_ref[0] ^ d
            start = place * rows if out_ref.shape[0] > rows else 0
            for r in range(0, rows, BLOCK):
                span = pl.ds(pl.multiple_of(start + r, BLOCK), BLOCK)
                finish(merge(i, r, BLOCK), span, place * (rows // BLOCK) + r // BLOCK)
    else:
        for i, d in enumerate(ds):
            out_ref[pl.ds(pl.multiple_of((me_ref[0] ^ d) * rows, rows), rows), :] = merge(i, 0, rows)
        for block in range(tp * rows // BLOCK):
            span = pl.ds(block * BLOCK, BLOCK)
            finish(out_ref[span, :], span, block)


def export_chunk(me, base, near, received, extras, right, squares, mag, ds, unit, first, count, previous):
    rows = base.shape[0]
    rank, cols = right.shape
    tp = len(extras)
    groups = cols // unit
    result = (
        jax.ShapeDtypeStruct((tp * rows, cols), jnp.bfloat16),
        jax.ShapeDtypeStruct((tp * rows // BLOCK, cols // BLOCK), jnp.float32),
    )
    pieces = [base, near, *received]
    specs = piece_specs(tp, rows, unit, groups, first)
    in_specs = (
        [specs[d] for d in ds]
        + [left_spec(rank, max(rows, BLOCK))] * len(ds)
        + [chunk_spec(rank, unit, first), chunk_spec(1, unit), group_spec(1, unit, groups, first)]
    )
    args = [pieces[d] for d in ds] + [extras[d] for d in ds] + [right, squares, mag]
    aliases = {}
    if previous is not None:
        in_specs += [pl.BlockSpec(memory_space=pl.ANY), whole_spec(previous[1])]
        args += list(previous)
        aliases = {len(args) - 1: 0}
    if len(ds) == 1:
        out_spec = pl.BlockSpec((rows, unit), lambda j, me: (me[0] ^ ds[0], first + j))
    else:
        out_spec = chunk_spec(tp * rows, unit, first)
    return pl.pallas_call(
        functools.partial(export_kernel, tp, ds, first),
        out_shape=result,
        grid_spec=pltpu.PrefetchScalarGridSpec(
            num_scalar_prefetch=1,
            grid=(count,),
            in_specs=in_specs,
            out_specs=(out_spec, whole_spec(result[1])),
        ),
        input_output_aliases=aliases,
        compiler_params=PARAMS,
        cost_estimate=cost(len(ds) * rows, count * unit, rank, 2),
    )(me, *args)


def body(tp, fsdp, base, left, right, magnitude):
    rows, rank = left.shape
    cols = right.shape[1]
    blocks = cols // BLOCK
    chunks, early = chunk_blocks(blocks)
    mag = magnitude.reshape(1, -1)
    line = lax.axis_index("fsdp").astype(jnp.int32)
    me = lax.axis_index("tp").astype(jnp.int32).reshape(1)
    place = me + tp * line
    lane = -(-rows // BLOCK) * BLOCK
    left = jnp.pad(left.T, ((0, 0), (0, lane - rows)))
    late = (chunks[early][0], chunks[-1][1])
    far = range(2, tp)
    received = {}

    def span(k):
        a, b = chunks[k]
        return a * BLOCK, (b - a) * BLOCK

    def units(k):
        a, b = chunks[k]
        width = width_of(a, b, blocks)
        return width * BLOCK, a // width, (b - a) // width

    def send(k, pieces):
        received[k] = [swap(piece, d, tp) for d, piece in zip(far, pieces)]

    pieces = []
    for d in far:
        if d % 2 == 0:
            piece = pack_first(place, base, tp, d, left, right, (late[0] * BLOCK, late[1] * BLOCK), span(0)[1])
        else:
            piece = pack(after(me, *pieces), base, tp, (d,), *span(0))[0]
        pieces.append(piece)
    send(0, pieces)
    pieces = pack(after(me, *pieces), base, tp, far, *span(1))
    send(1, pieces)
    near = lax.all_to_all(
        pack_near(after(me, *pieces), base, tp), "tp", 0, 0, tiled=True,
        axis_index_groups=[[i, i + 1] for i in range(0, tp, 2)],
    )

    def unfold(block, width):
        return jnp.concatenate([block[:, :width], block[:, width : 2 * width]])

    def alternate(even):
        odd = swap(jnp.concatenate(even), 1, tp)
        return [array for i, own in enumerate(even) for array in (own, odd[i * rank : (i + 1) * rank])]

    arrived = [received[0][d - 2] for d in far[::2]]
    half, late_cols = rank // 2, (late[1] - late[0]) * BLOCK
    extras = alternate([left] + [unfold(piece[rows : rows + half], lane) for piece in arrived])

    def late_rights():
        mine = jnp.concatenate([unfold(piece[rows + half :], late_cols) for piece in arrived], axis=1)
        other = swap(mine, 1, fsdp, "fsdp")
        both = jnp.where(line % 2 == 0, jnp.concatenate([mine, other]), jnp.concatenate([other, mine]))
        even = [right[:, late[0] * BLOCK : late[1] * BLOCK]]
        even += [both[:, i * late_cols : (i + 1) * late_cols] for i in range(len(arrived))]
        return alternate(even)

    apart = rows % BLOCK == 0 and len(chunks) == early + 1
    every = tuple(range(tp))
    result = None
    token = ()
    totals = {}

    def export(k, ds):
        nonlocal result
        result = export_chunk(me, base, near, received.get(k, ()), extras, right, totals[k], mag, ds, *units(k), result)

    for k in range(len(chunks)):
        following = k + AHEAD
        if following < len(chunks):
            turn = after(me, *received[k], *token)
            if following == CARRIER:
                width = width_of(late[0], late[1] - late[0], blocks)
                sums = sender_squares(
                    turn, base, left, late_rights(), width * BLOCK, late[0] // width, (late[1] - late[0]) // width
                )
                sums = sums[0::2] + swap(sums[1::2], 1, tp)
                late_sums = sums[:1]
                send(following, pack_carrier(turn, base, tp, far, terms_of(sums), *span(following)))
            elif following == len(chunks) - 1:
                pieces = []
                for d in far:
                    pieces += pack(after(turn, *pieces), base, tp, (d,), *span(following))
                send(following, pieces)
            else:
                send(following, pack(turn, base, tp, far, *span(following)))
        if k < early:
            if apart and k == early - 1:
                export(early, every[:2])
                token = (result[1],)
            turn = after(me, *token)
            local = None
            for ds in (every[:-1], every[-1:]) if apart and k == early - 1 else (every,):
                local = column_squares(turn, base, near, received[k], extras, right, ds, *units(k), local)
            if k == CARRIER:
                for piece in received[k][::2]:
                    parts = after(piece, *token)[rows : rows + TERMS, : late_sums.shape[1]].astype(jnp.float32)
                    late_sums = late_sums + jnp.sum(parts, axis=0, keepdims=True)
                local = jnp.concatenate([local, late_sums], axis=1)
            total = lax.psum(local, "fsdp") if k < early - 1 else total_of(local, fsdp, "fsdp")
            totals[k] = total[:, : span(k)[1]]
            if k == CARRIER:
                for i in range(early, len(chunks)):
                    start = span(k)[1] + span(i)[0] - late[0] * BLOCK
                    totals[i] = total[:, start : start + span(i)[1]]
        if apart and k == early:
            for d in far:
                export(k, (d,))
        else:
            export(k, every)
        token = (result[1],)
    return result


def solution(mesh):
    in_specs = (P(("fsdp", "tp"), None), P(("fsdp", "tp"), None), P(None, "tp"), P())
    out_specs = (P("fsdp", "tp"), P("fsdp", "tp"))
    return jax.shard_map(
        functools.partial(body, mesh.shape["tp"], mesh.shape["fsdp"]), mesh=mesh, in_specs=in_specs, out_specs=out_specs, check_vma=False
    )
```

```python
import functools

import jax
import jax.numpy as jnp
from jax import lax
from jax.experimental import pallas as pl
from jax.experimental.pallas import tpu as pltpu
from jax.sharding import PartitionSpec as P

BLOCK = 128
EPSILON = 1e-06
EARLY = (8, 8, 8, 8, 8, 8)
LATE = (4,)
AHEAD = 2
SCALE = 3
CARRIER = 4
TERMS = 3
SUMS_ROWS = 16
PARAMS = pltpu.CompilerParams(vmem_limit_bytes=48 * 2**20)
MOVE_PARAMS = pltpu.CompilerParams(vmem_limit_bytes=48 * 2**20)


def chunk_blocks(total):
    parts = EARLY + LATE
    bounds = [total * sum(parts[:i]) // sum(parts) for i in range(len(parts) + 1)]
    chunks = [(a, b) for a, b in zip(bounds, bounds[1:]) if b > a]
    return chunks, sum(a < bounds[len(EARLY)] for a, _ in chunks)


def width_of(*counts):
    return max(d for d in (4, 2, 1) if all(count % d == 0 for count in counts))


def after(value, *others):
    return lax.optimization_barrier((value, *others))[0]


def swap(array, d, size, axis="tp"):
    return lax.ppermute(array, axis, [(i, i ^ d) for i in range(size)])


def total_of(array, size, axis):
    d = 1
    while d < size:
        others = (d,) if 2 * d == size else (d, 2 * d, 3 * d)
        array = array + sum(swap(array, other, size, axis) for other in others)
        d *= 1 + len(others)
    return array


def move_kernel(moves, number, direct, me_ref, *refs):
    plan = moves(me_ref[0])
    holds = () if direct else refs[-len(plan) - 2 : -2]
    sources, targets = refs[:number], refs[number : len(refs) - len(holds) - 2]
    came, went = refs[-2:]
    ins, outs = [], []
    for i, (source, row, col, rows, cols, target, to_row, to_col) in enumerate(plan):
        block = sources[source].at[pl.ds(row, rows), pl.ds(col, cols)]
        place = targets[target].at[pl.ds(to_row, rows), pl.ds(to_col, cols)]
        ins.append(pltpu.make_async_copy(block, place if direct else holds[i], came.at[i]))
        if not direct:
            outs.append(pltpu.make_async_copy(holds[i], place, went.at[i]))
    for copy in ins:
        copy.start()
    for i, copy in enumerate(ins):
        copy.wait()
        if not direct:
            outs[i].start()
    for copy in outs:
        copy.wait()


def move(me, arrays, shapes, moves, direct=False):
    dtype = arrays[0].dtype
    plan = moves(0)
    kind = pltpu.VMEM if direct else jax.ShapeDtypeStruct
    space = pltpu.VMEM if direct else pl.ANY
    return pl.pallas_call(
        functools.partial(move_kernel, moves, len(arrays), direct),
        out_shape=[kind(shape, dtype) for shape in shapes],
        grid_spec=pltpu.PrefetchScalarGridSpec(
            num_scalar_prefetch=1,
            grid=(1,),
            in_specs=[pl.BlockSpec(memory_space=pl.ANY)] * len(arrays),
            out_specs=[pl.BlockSpec(memory_space=space)] * len(shapes),
            scratch_shapes=[pltpu.VMEM((rows, cols), dtype) for _, _, _, rows, cols, *_ in (() if direct else plan)]
            + [pltpu.SemaphoreType.DMA((len(plan),))] * 2,
        ),
        compiler_params=MOVE_PARAMS,
        cost_estimate=cost(sum(rows * cols for rows, cols in shapes), 1, 0, 2),
    )(me, *arrays)


def parts_of(rows):
    height = rows // 8 if rows % BLOCK == 0 else rows
    return [(r, height) for r in range(0, rows, height)]


def column_moves(me, rows, cols, group, first, target):
    col = pl.multiple_of(me * group + first, BLOCK)
    return [(0, r, col, height, cols, target, r, 0) for r, height in parts_of(rows)]


def group_spec(rows, unit, groups, first, d=0):
    return pl.BlockSpec((rows, unit), lambda j, me: (0, (me[0] ^ d) * groups + first + j))


def chunk_spec(rows, unit, first=0):
    return pl.BlockSpec((rows, unit), lambda j, me: (0, first + j))


def left_spec(rank, unit):
    return pl.BlockSpec((rank, unit), lambda j, me: (0, 0))


def whole_spec(array):
    return pl.BlockSpec(array.shape, lambda j, me: (0, 0))


def cost(rows, cols, rank, passes):
    return pl.CostEstimate(
        flops=2 * rows * cols * rank // SCALE, bytes_accessed=2 * passes * rows * cols // SCALE, transcendentals=0
    )


def pack(me, base, tp, distances, first, cols):
    rows, group = base.shape[0], base.shape[1] // tp

    def moves(me):
        return [m for i, d in enumerate(distances) for m in column_moves(me ^ d, rows, cols, group, first, i)]

    return move(me, [base], [(rows, cols)] * len(distances), moves, direct=True)


def pack_first(place, base, tp, d, left, right, late, cols):
    rows, group = base.shape[0], base.shape[1] // tp
    rank, lane = left.shape
    late_cols = late[1] - late[0]
    half, quarter = rank // 2, rank // 4

    def moves(place):
        line, me = place // tp, place % tp
        result = column_moves(me ^ d, rows, cols, group, 0, 0)
        for i in range(2):
            result.append((1, i * half, 0, half, lane, 0, rows, i * lane))
            row = pl.multiple_of(line % 2 * half + i * quarter, quarter)
            result.append((2, row, late[0], quarter, late_cols, 0, rows + half, i * late_cols))
        return result

    return move(place, [base, left, right], [(rows + half + quarter, cols)], moves, direct=True)[0]


def pack_carrier(me, base, tp, distances, terms, first, cols):
    rows, group = base.shape[0], base.shape[1] // tp

    def moves(me):
        result = []
        for i, d in enumerate(distances):
            result += column_moves(me ^ d, rows, cols, group, first, i)
            if d % 2 == 0:
                result.append((1, d // 2 * SUMS_ROWS, 0, SUMS_ROWS, terms.shape[1], i, rows, 0))
        return result

    return move(me, [base, terms], [(rows + (d + 1) % 2 * SUMS_ROWS, cols) for d in distances], moves, direct=True)


def pack_near(me, base, tp):
    rows, group = base.shape[0], base.shape[1] // tp

    def moves(me):
        result = []
        for s in range(2):
            for source, r, col, *rest in column_moves((me // 2) * 2 + s, rows, group, group, 0, 0):
                result.append((source, r, col, *rest[:-2], s * rows + r, 0))
        return result

    return move(me, [base], [(2 * rows, group)], moves)[0]


def near_spec(rows, unit, first):
    return pl.BlockSpec((rows, unit), lambda j, me: ((me[0] % 2) ^ 1, first + j))


def low_rank(extra_ref, start, height, right):
    left = extra_ref[pl.ds(0, right.shape[0]), pl.ds(start, height)]
    return lax.dot_general(left, right, (((0,), (0,)), ((), ())), preferred_element_type=jnp.float32)


def squares_of(piece_ref, extra_ref, right):
    rows, cols = piece_ref.shape
    height = min(rows, BLOCK)
    total = jnp.zeros((8, cols), jnp.float32)
    for r in range(0, rows, height):
        combined = piece_ref[pl.ds(r, height), :].astype(jnp.float32) + low_rank(extra_ref, r, height, right)
        total = total + jnp.sum((combined * combined).reshape(height // 8, 8, cols), axis=0)
    return total


def squares_kernel(number, me_ref, *refs):
    pieces, extras, right_ref, out_ref = refs[:number], refs[number : 2 * number], refs[2 * number], refs[-1]
    right = right_ref[...]
    total = sum(squares_of(piece, extra, right) for piece, extra in zip(pieces, extras))
    total = jnp.sum(total, axis=0, keepdims=True)
    out_ref[...] = total + refs[-2][...] if len(refs) > 2 * number + 2 else total


def sender_squares_kernel(tp, me_ref, *refs):
    pieces, rights, left, sums_ref = refs[:tp], refs[tp : 2 * tp], refs[-2], refs[-1]
    for d in range(tp):
        sums_ref[pl.ds(d, 1), :] = jnp.sum(squares_of(pieces[d], left, rights[d][...]), axis=0, keepdims=True)


def terms_kernel(sums_ref, terms_ref):
    line = lax.broadcasted_iota(jnp.int32, (SUMS_ROWS, sums_ref.shape[1]), 0)
    for i in range(sums_ref.shape[0]):
        sums = sums_ref[pl.ds(i, 1), :]
        block = jnp.zeros(line.shape, jnp.float32)
        for term in range(TERMS):
            part = sums.astype(jnp.bfloat16).astype(jnp.float32)
            block = jnp.where(line == term, part, block)
            sums = sums - part
        terms_ref[pl.ds(i * SUMS_ROWS, SUMS_ROWS), :] = block.astype(jnp.bfloat16)


def terms_of(sums):
    rows, cols = sums.shape
    return pl.pallas_call(
        terms_kernel,
        out_shape=jax.ShapeDtypeStruct((rows * SUMS_ROWS, cols), jnp.bfloat16),
        compiler_params=PARAMS,
        cost_estimate=cost(rows, cols, 0, 2),
    )(sums)


def piece_specs(tp, rows, unit, groups, first):
    specs = [group_spec(rows, unit, groups, first), near_spec(rows, unit, first)]
    return specs + [chunk_spec(rows, unit)] * (tp - 2)


def column_squares(me, base, near, received, extras, right, ds, unit, first, count, previous=None):
    rows = base.shape[0]
    rank, cols = right.shape
    pieces = [base, near, *received]
    specs = piece_specs(len(extras), rows, unit, cols // unit, first)
    in_specs = [specs[d] for d in ds] + [left_spec(rank, max(rows, BLOCK))] * len(ds) + [chunk_spec(rank, unit, first)]
    args = [pieces[d] for d in ds] + [extras[d] for d in ds] + [right]
    if previous is not None:
        in_specs.append(chunk_spec(1, unit))
        args.append(previous)
    return pl.pallas_call(
        functools.partial(squares_kernel, len(ds)),
        out_shape=jax.ShapeDtypeStruct((1, count * unit), jnp.float32),
        grid_spec=pltpu.PrefetchScalarGridSpec(
            num_scalar_prefetch=1,
            grid=(count,),
            in_specs=in_specs,
            out_specs=chunk_spec(1, unit),
        ),
        compiler_params=PARAMS,
        cost_estimate=cost(len(ds) * rows, count * unit, rank, 1),
    )(me, *args)


def sender_squares(me, base, left, rights, unit, first, count):
    rows = base.shape[0]
    tp = len(rights)
    groups = base.shape[1] // (tp * unit)
    rank = left.shape[0]
    return pl.pallas_call(
        functools.partial(sender_squares_kernel, tp),
        out_shape=jax.ShapeDtypeStruct((tp, count * unit), jnp.float32),
        grid_spec=pltpu.PrefetchScalarGridSpec(
            num_scalar_prefetch=1,
            grid=(count,),
            in_specs=[group_spec(rows, unit, groups, first, d) for d in range(tp)]
            + [chunk_spec(rank, unit)] * tp
            + [whole_spec(left)],
            out_specs=chunk_spec(tp, unit),
        ),
        compiler_params=PARAMS,
        cost_estimate=cost(tp * rows, count * unit, rank, 1),
    )(me, *[base] * tp, *rights, left)


def export_kernel(tp, ds, first, me_ref, *refs):
    number = len(ds)
    pieces, extras = refs[:number], refs[number : 2 * number]
    right_ref, squares_ref, mag_ref = refs[2 * number : 2 * number + 3]
    out_ref, scales_ref = refs[-2:]
    rows, cols = pieces[0].shape
    step = pl.program_id(0)
    if len(refs) > 2 * number + 5:
        @pl.when(step == 0)
        def _():
            scales_ref[...] = refs[2 * number + 4][...]

    factor = mag_ref[...] / jnp.sqrt(squares_ref[...] + EPSILON)
    right = right_ref[...]
    lane = lax.broadcasted_iota(jnp.int32, (1, scales_ref.shape[1]), 1)
    per_step = cols // BLOCK

    def merge(i, r, height):
        combined = pieces[i][pl.ds(r, height), :].astype(jnp.float32) + low_rank(extras[i], r, height, right)
        return (combined * factor).astype(jnp.bfloat16)

    def finish(merged, span, block):
        line = scales_ref[pl.ds(block, 1), :]
        for j in range(per_step):
            tile = merged[:, j * BLOCK : (j + 1) * BLOCK].astype(jnp.float32)
            largest = jnp.max(jnp.max(jnp.abs(tile), axis=0, keepdims=True), axis=1, keepdims=True)
            out_ref[span, pl.ds(j * BLOCK, BLOCK)] = (tile * (1.0 / (largest + EPSILON))).astype(jnp.bfloat16)
            line = jnp.where(lane == (first + step) * per_step + j, largest, line)
        scales_ref[pl.ds(block, 1), :] = line

    if rows % BLOCK == 0:
        for i, d in enumerate(ds):
            place = me_ref[0] ^ d
            start = place * rows if out_ref.shape[0] > rows else 0
            for r in range(0, rows, BLOCK):
                span = pl.ds(pl.multiple_of(start + r, BLOCK), BLOCK)
                finish(merge(i, r, BLOCK), span, place * (rows // BLOCK) + r // BLOCK)
    else:
        for i, d in enumerate(ds):
            out_ref[pl.ds(pl.multiple_of((me_ref[0] ^ d) * rows, rows), rows), :] = merge(i, 0, rows)
        for block in range(tp * rows // BLOCK):
            span = pl.ds(block * BLOCK, BLOCK)
            finish(out_ref[span, :], span, block)


def export_chunk(me, base, near, received, extras, right, squares, mag, ds, unit, first, count, previous):
    rows = base.shape[0]
    rank, cols = right.shape
    tp = len(extras)
    groups = cols // unit
    result = (
        jax.ShapeDtypeStruct((tp * rows, cols), jnp.bfloat16),
        jax.ShapeDtypeStruct((tp * rows // BLOCK, cols // BLOCK), jnp.float32),
    )
    pieces = [base, near, *received]
    specs = piece_specs(tp, rows, unit, groups, first)
    in_specs = (
        [specs[d] for d in ds]
        + [left_spec(rank, max(rows, BLOCK))] * len(ds)
        + [chunk_spec(rank, unit, first), chunk_spec(1, unit), group_spec(1, unit, groups, first)]
    )
    args = [pieces[d] for d in ds] + [extras[d] for d in ds] + [right, squares, mag]
    aliases = {}
    if previous is not None:
        in_specs += [pl.BlockSpec(memory_space=pl.ANY), whole_spec(previous[1])]
        args += list(previous)
        aliases = {len(args) - 1: 0}
    if len(ds) == 1:
        out_spec = pl.BlockSpec((rows, unit), lambda j, me: (me[0] ^ ds[0], first + j))
    else:
        out_spec = chunk_spec(tp * rows, unit, first)
    return pl.pallas_call(
        functools.partial(export_kernel, tp, ds, first),
        out_shape=result,
        grid_spec=pltpu.PrefetchScalarGridSpec(
            num_scalar_prefetch=1,
            grid=(count,),
            in_specs=in_specs,
            out_specs=(out_spec, whole_spec(result[1])),
        ),
        input_output_aliases=aliases,
        compiler_params=PARAMS,
        cost_estimate=cost(len(ds) * rows, count * unit, rank, 2),
    )(me, *args)


def body(tp, fsdp, base, left, right, magnitude):
    rows, rank = left.shape
    cols = right.shape[1]
    blocks = cols // BLOCK
    chunks, early = chunk_blocks(blocks)
    mag = magnitude.reshape(1, -1)
    line = lax.axis_index("fsdp").astype(jnp.int32)
    me = lax.axis_index("tp").astype(jnp.int32).reshape(1)
    place = me + tp * line
    lane = -(-rows // BLOCK) * BLOCK
    left = jnp.pad(left.T, ((0, 0), (0, lane - rows)))
    late = (chunks[early][0], chunks[-1][1])
    far = range(2, tp)
    received = {}

    def span(k):
        a, b = chunks[k]
        return a * BLOCK, (b - a) * BLOCK

    def units(k):
        a, b = chunks[k]
        width = width_of(a, b, blocks)
        return width * BLOCK, a // width, (b - a) // width

    def send(k, pieces):
        received[k] = [swap(piece, d, tp) for d, piece in zip(far, pieces)]

    pieces = []
    for d in far:
        if d % 2 == 0:
            piece = pack_first(place, base, tp, d, left, right, (late[0] * BLOCK, late[1] * BLOCK), span(0)[1])
        else:
            piece = pack(after(me, *pieces), base, tp, (d,), *span(0))[0]
        pieces.append(piece)
    send(0, pieces)
    pieces = pack(after(me, *pieces), base, tp, far, *span(1))
    send(1, pieces)
    near = lax.all_to_all(
        pack_near(after(me, *pieces), base, tp), "tp", 0, 0, tiled=True,
        axis_index_groups=[[i, i + 1] for i in range(0, tp, 2)],
    )

    def unfold(block, width):
        return jnp.concatenate([block[:, :width], block[:, width : 2 * width]])

    def alternate(even):
        odd = swap(jnp.concatenate(even), 1, tp)
        return [array for i, own in enumerate(even) for array in (own, odd[i * rank : (i + 1) * rank])]

    arrived = [received[0][d - 2] for d in far[::2]]
    half, late_cols = rank // 2, (late[1] - late[0]) * BLOCK
    extras = alternate([left] + [unfold(piece[rows : rows + half], lane) for piece in arrived])

    def late_rights():
        mine = jnp.concatenate([unfold(piece[rows + half :], late_cols) for piece in arrived], axis=1)
        other = swap(mine, 1, fsdp, "fsdp")
        both = jnp.where(line % 2 == 0, jnp.concatenate([mine, other]), jnp.concatenate([other, mine]))
        even = [right[:, late[0] * BLOCK : late[1] * BLOCK]]
        even += [both[:, i * late_cols : (i + 1) * late_cols] for i in range(len(arrived))]
        return alternate(even)

    apart = rows % BLOCK == 0 and len(chunks) == early + 1
    every = tuple(range(tp))
    result = None
    token = ()
    totals = {}

    def export(k, ds):
        nonlocal result
        result = export_chunk(me, base, near, received.get(k, ()), extras, right, totals[k], mag, ds, *units(k), result)

    for k in range(len(chunks)):
        following = k + AHEAD
        if following < len(chunks):
            turn = after(me, *received[k], *token)
            if following == CARRIER:
                width = width_of(late[0], late[1] - late[0], blocks)
                sums = sender_squares(
                    turn, base, left, late_rights(), width * BLOCK, late[0] // width, (late[1] - late[0]) // width
                )
                sums = sums[0::2] + swap(sums[1::2], 1, tp)
                late_sums = sums[:1]
                send(following, pack_carrier(turn, base, tp, far, terms_of(sums), *span(following)))
            elif following == len(chunks) - 1:
                pieces = []
                for d in far:
                    pieces += pack(after(turn, *pieces), base, tp, (d,), *span(following))
                send(following, pieces)
            else:
                send(following, pack(turn, base, tp, far, *span(following)))
        if k < early:
            if apart and k == early - 1:
                export(early, every[:2])
                token = (result[1],)
            turn = after(me, *token)
            local = None
            for ds in (every[:-1], every[-1:]) if apart and k == early - 1 else (every,):
                local = column_squares(turn, base, near, received[k], extras, right, ds, *units(k), local)
            if k == CARRIER:
                for piece in received[k][::2]:
                    parts = after(piece, *token)[rows : rows + TERMS, : late_sums.shape[1]].astype(jnp.float32)
                    late_sums = late_sums + jnp.sum(parts, axis=0, keepdims=True)
                local = jnp.concatenate([local, late_sums], axis=1)
            total = lax.psum(local, "fsdp") if k < early - 1 else total_of(local, fsdp, "fsdp")
            totals[k] = total[:, : span(k)[1]]
            if k == CARRIER:
                for i in range(early, len(chunks)):
                    start = span(k)[1] + span(i)[0] - late[0] * BLOCK
                    totals[i] = total[:, start : start + span(i)[1]]
        if apart and k == early:
            for d in far:
                export(k, (d,))
        else:
            export(k, every)
        token = (result[1],)
    return result


def solution(mesh):
    in_specs = (P(("fsdp", "tp"), None), P(("fsdp", "tp"), None), P(None, "tp"), P())
    out_specs = (P("fsdp", "tp"), P("fsdp", "tp"))
    return jax.shard_map(
        functools.partial(body, mesh.shape["tp"], mesh.shape["fsdp"]), mesh=mesh, in_specs=in_specs, out_specs=out_specs, check_vma=False
    )
```

```python
import functools

import jax
import jax.numpy as jnp
from jax import lax
from jax.experimental import pallas as pl
from jax.experimental.pallas import tpu as pltpu
from jax.sharding import PartitionSpec as P

BLOCK = 128
EPSILON = 1e-06
EARLY = (12, 12, 12, 12)
LATE = (4,)
AHEAD = 2
SCALE = 3
CARRIER = 2
TERMS = 3
SUMS_ROWS = 16
PARAMS = pltpu.CompilerParams(vmem_limit_bytes=52 * 2**20)
MOVE_PARAMS = pltpu.CompilerParams(vmem_limit_bytes=56 * 2**20)


def chunk_blocks(total):
    parts = EARLY + LATE
    bounds = [total * sum(parts[:i]) // sum(parts) for i in range(len(parts) + 1)]
    chunks = [(a, b) for a, b in zip(bounds, bounds[1:]) if b > a]
    return chunks, sum(a < bounds[len(EARLY)] for a, _ in chunks)


def width_of(*counts):
    return max(d for d in (4, 2, 1) if all(count % d == 0 for count in counts))


def after(value, *others):
    return lax.optimization_barrier((value, *others))[0]


def swap(array, d, size, axis="tp"):
    return lax.ppermute(array, axis, [(i, i ^ d) for i in range(size)])


def total_of(array, size, axis):
    d = 1
    while d < size:
        others = (d,) if 2 * d == size else (d, 2 * d, 3 * d)
        array = array + sum(swap(array, other, size, axis) for other in others)
        d *= 1 + len(others)
    return array


def move_kernel(moves, number, direct, me_ref, *refs):
    plan = moves(me_ref[0])
    holds = () if direct else refs[-len(plan) - 2 : -2]
    sources, targets = refs[:number], refs[number : len(refs) - len(holds) - 2]
    came, went = refs[-2:]
    ins, outs = [], []
    for i, (source, row, col, rows, cols, target, to_row, to_col) in enumerate(plan):
        block = sources[source].at[pl.ds(row, rows), pl.ds(col, cols)]
        place = targets[target].at[pl.ds(to_row, rows), pl.ds(to_col, cols)]
        ins.append(pltpu.make_async_copy(block, place if direct else holds[i], came.at[i]))
        if not direct:
            outs.append(pltpu.make_async_copy(holds[i], place, went.at[i]))
    for copy in ins:
        copy.start()
    for i, copy in enumerate(ins):
        copy.wait()
        if not direct:
            outs[i].start()
    for copy in outs:
        copy.wait()


def move(me, arrays, shapes, moves, direct=False):
    dtype = arrays[0].dtype
    plan = moves(0)
    kind = pltpu.VMEM if direct else jax.ShapeDtypeStruct
    space = pltpu.VMEM if direct else pl.ANY
    return pl.pallas_call(
        functools.partial(move_kernel, moves, len(arrays), direct),
        out_shape=[kind(shape, dtype) for shape in shapes],
        grid_spec=pltpu.PrefetchScalarGridSpec(
            num_scalar_prefetch=1,
            grid=(1,),
            in_specs=[pl.BlockSpec(memory_space=pl.ANY)] * len(arrays),
            out_specs=[pl.BlockSpec(memory_space=space)] * len(shapes),
            scratch_shapes=[pltpu.VMEM((rows, cols), dtype) for _, _, _, rows, cols, *_ in (() if direct else plan)]
            + [pltpu.SemaphoreType.DMA((len(plan),))] * 2,
        ),
        compiler_params=MOVE_PARAMS,
        cost_estimate=cost(sum(rows * cols for rows, cols in shapes), 1, 0, 2),
    )(me, *arrays)


def parts_of(rows):
    height = rows // 8 if rows % BLOCK == 0 else rows
    return [(r, height) for r in range(0, rows, height)]


def column_moves(me, rows, cols, group, first, target):
    col = pl.multiple_of(me * group + first, BLOCK)
    return [(0, r, col, height, cols, target, r, 0) for r, height in parts_of(rows)]


def group_spec(rows, unit, groups, first, d=0):
    return pl.BlockSpec((rows, unit), lambda j, me: (0, (me[0] ^ d) * groups + first + j))


def chunk_spec(rows, unit, first=0):
    return pl.BlockSpec((rows, unit), lambda j, me: (0, first + j))


def left_spec(rank, unit):
    return pl.BlockSpec((rank, unit), lambda j, me: (0, 0))


def whole_spec(array):
    return pl.BlockSpec(array.shape, lambda j, me: (0, 0))


def cost(rows, cols, rank, passes):
    return pl.CostEstimate(
        flops=2 * rows * cols * rank // SCALE, bytes_accessed=2 * passes * rows * cols // SCALE, transcendentals=0
    )


def pack(me, base, tp, distances, first, cols):
    rows, group = base.shape[0], base.shape[1] // tp

    def moves(me):
        return [m for i, d in enumerate(distances) for m in column_moves(me ^ d, rows, cols, group, first, i)]

    return move(me, [base], [(rows, cols)] * len(distances), moves)


def pack_first(place, base, tp, d, left, right, late, cols):
    rows, group = base.shape[0], base.shape[1] // tp
    rank, lane = left.shape
    half = rank // 2

    def moves(place):
        line, me = place // tp, place % tp
        result = column_moves(me ^ d, rows, cols, group, 0, 0)
        for i in range(2):
            result.append((1, i * half, 0, half, lane, 0, rows, i * lane))
        row = pl.multiple_of(line % 2 * half, half)
        result.append((2, row, late[0], half, late[1] - late[0], 0, rows, 2 * lane))
        return result

    return move(place, [base, left, right], [(rows + half, cols)], moves, direct=True)[0]


def pack_carrier(me, base, tp, distances, terms, first, cols):
    rows, group = base.shape[0], base.shape[1] // tp

    def moves(me):
        result = []
        for i, d in enumerate(distances):
            result += column_moves(me ^ d, rows, cols, group, first, i)
            if d % 2 == 0:
                result.append((1, d // 2 * SUMS_ROWS, 0, SUMS_ROWS, terms.shape[1], i, rows, 0))
        return result

    return move(me, [base, terms], [(rows + (d + 1) % 2 * SUMS_ROWS, cols) for d in distances], moves)


def pack_near(me, base, tp):
    rows, group = base.shape[0], base.shape[1] // tp

    def moves(me):
        result = []
        for s in range(2):
            for source, r, col, *rest in column_moves((me // 2) * 2 + s, rows, group, group, 0, 0):
                result.append((source, r, col, *rest[:-2], s * rows + r, 0))
        return result

    return move(me, [base], [(2 * rows, group)], moves)[0]


def near_spec(rows, unit, first):
    return pl.BlockSpec((rows, unit), lambda j, me: ((me[0] % 2) ^ 1, first + j))


def low_rank(extra_ref, start, height, right):
    left = extra_ref[pl.ds(0, right.shape[0]), pl.ds(start, height)]
    return lax.dot_general(left, right, (((0,), (0,)), ((), ())), preferred_element_type=jnp.float32)


def squares_of(piece_ref, extra_ref, right):
    rows, cols = piece_ref.shape
    height = min(rows, BLOCK)
    total = jnp.zeros((8, cols), jnp.float32)
    for r in range(0, rows, height):
        combined = piece_ref[pl.ds(r, height), :].astype(jnp.float32) + low_rank(extra_ref, r, height, right)
        total = total + jnp.sum((combined * combined).reshape(height // 8, 8, cols), axis=0)
    return total


def squares_kernel(number, me_ref, *refs):
    pieces, extras, right_ref, out_ref = refs[:number], refs[number : 2 * number], refs[2 * number], refs[-1]
    right = right_ref[...]
    total = sum(squares_of(piece, extra, right) for piece, extra in zip(pieces, extras))
    total = jnp.sum(total, axis=0, keepdims=True)
    out_ref[...] = total + refs[-2][...] if len(refs) > 2 * number + 2 else total


def sender_squares_kernel(tp, me_ref, *refs):
    pieces, rights, left, sums_ref = refs[:tp], refs[tp : 2 * tp], refs[-2], refs[-1]
    for d in range(tp):
        sums_ref[pl.ds(d, 1), :] = jnp.sum(squares_of(pieces[d], left, rights[d][...]), axis=0, keepdims=True)


def terms_kernel(sums_ref, terms_ref):
    line = lax.broadcasted_iota(jnp.int32, (SUMS_ROWS, sums_ref.shape[1]), 0)
    for i in range(sums_ref.shape[0]):
        sums = sums_ref[pl.ds(i, 1), :]
        block = jnp.zeros(line.shape, jnp.float32)
        for term in range(TERMS):
            part = sums.astype(jnp.bfloat16).astype(jnp.float32)
            block = jnp.where(line == term, part, block)
            sums = sums - part
        terms_ref[pl.ds(i * SUMS_ROWS, SUMS_ROWS), :] = block.astype(jnp.bfloat16)


def terms_of(sums):
    rows, cols = sums.shape
    return pl.pallas_call(
        terms_kernel,
        out_shape=jax.ShapeDtypeStruct((rows * SUMS_ROWS, cols), jnp.bfloat16),
        compiler_params=PARAMS,
        cost_estimate=cost(rows, cols, 0, 2),
    )(sums)


def piece_specs(tp, rows, unit, groups, first):
    specs = [group_spec(rows, unit, groups, first), near_spec(rows, unit, first)]
    return specs + [chunk_spec(rows, unit)] * (tp - 2)


def column_squares(me, base, near, received, extras, right, ds, unit, first, count, previous=None):
    rows = base.shape[0]
    rank, cols = right.shape
    pieces = [base, near, *received]
    specs = piece_specs(len(extras), rows, unit, cols // unit, first)
    in_specs = [specs[d] for d in ds] + [left_spec(rank, max(rows, BLOCK))] * len(ds) + [chunk_spec(rank, unit, first)]
    args = [pieces[d] for d in ds] + [extras[d] for d in ds] + [right]
    if previous is not None:
        in_specs.append(chunk_spec(1, unit))
        args.append(previous)
    return pl.pallas_call(
        functools.partial(squares_kernel, len(ds)),
        out_shape=jax.ShapeDtypeStruct((1, count * unit), jnp.float32),
        grid_spec=pltpu.PrefetchScalarGridSpec(
            num_scalar_prefetch=1,
            grid=(count,),
            in_specs=in_specs,
            out_specs=chunk_spec(1, unit),
        ),
        compiler_params=PARAMS,
        cost_estimate=cost(len(ds) * rows, count * unit, rank, 1),
    )(me, *args)


def sender_squares(me, base, left, rights, unit, first, count):
    rows = base.shape[0]
    tp = len(rights)
    groups = base.shape[1] // (tp * unit)
    rank = left.shape[0]
    return pl.pallas_call(
        functools.partial(sender_squares_kernel, tp),
        out_shape=jax.ShapeDtypeStruct((tp, count * unit), jnp.float32),
        grid_spec=pltpu.PrefetchScalarGridSpec(
            num_scalar_prefetch=1,
            grid=(count,),
            in_specs=[group_spec(rows, unit, groups, first, d) for d in range(tp)]
            + [chunk_spec(rank, unit)] * tp
            + [whole_spec(left)],
            out_specs=chunk_spec(tp, unit),
        ),
        compiler_params=PARAMS,
        cost_estimate=cost(tp * rows, count * unit, rank, 1),
    )(me, *[base] * tp, *rights, left)


def export_kernel(tp, ds, first, me_ref, *refs):
    number = len(ds)
    pieces, extras = refs[:number], refs[number : 2 * number]
    right_ref, squares_ref, mag_ref = refs[2 * number : 2 * number + 3]
    out_ref, scales_ref = refs[-2:]
    rows, cols = pieces[0].shape
    step = pl.program_id(0)
    if len(refs) > 2 * number + 5:
        @pl.when(step == 0)
        def _():
            scales_ref[...] = refs[2 * number + 4][...]

    factor = mag_ref[...] / jnp.sqrt(squares_ref[...] + EPSILON)
    right = right_ref[...]
    lane = lax.broadcasted_iota(jnp.int32, (1, scales_ref.shape[1]), 1)
    per_step = cols // BLOCK

    def merge(i, r, height):
        combined = pieces[i][pl.ds(r, height), :].astype(jnp.float32) + low_rank(extras[i], r, height, right)
        return (combined * factor).astype(jnp.bfloat16)

    def finish(merged, span, block):
        line = scales_ref[pl.ds(block, 1), :]
        for j in range(per_step):
            tile = merged[:, j * BLOCK : (j + 1) * BLOCK].astype(jnp.float32)
            largest = jnp.max(jnp.max(jnp.abs(tile), axis=0, keepdims=True), axis=1, keepdims=True)
            out_ref[span, pl.ds(j * BLOCK, BLOCK)] = (tile * (1.0 / (largest + EPSILON))).astype(jnp.bfloat16)
            line = jnp.where(lane == (first + step) * per_step + j, largest, line)
        scales_ref[pl.ds(block, 1), :] = line

    if rows % BLOCK == 0:
        for i, d in enumerate(ds):
            place = me_ref[0] ^ d
            start = place * rows if out_ref.shape[0] > rows else 0
            for r in range(0, rows, BLOCK):
                span = pl.ds(pl.multiple_of(start + r, BLOCK), BLOCK)
                finish(merge(i, r, BLOCK), span, place * (rows // BLOCK) + r // BLOCK)
    else:
        for i, d in enumerate(ds):
            out_ref[pl.ds(pl.multiple_of((me_ref[0] ^ d) * rows, rows), rows), :] = merge(i, 0, rows)
        for block in range(tp * rows // BLOCK):
            span = pl.ds(block * BLOCK, BLOCK)
            finish(out_ref[span, :], span, block)


def export_chunk(me, base, near, received, extras, right, squares, mag, ds, unit, first, count, previous):
    rows = base.shape[0]
    rank, cols = right.shape
    tp = len(extras)
    groups = cols // unit
    result = (
        jax.ShapeDtypeStruct((tp * rows, cols), jnp.bfloat16),
        jax.ShapeDtypeStruct((tp * rows // BLOCK, cols // BLOCK), jnp.float32),
    )
    pieces = [base, near, *received]
    specs = piece_specs(tp, rows, unit, groups, first)
    in_specs = (
        [specs[d] for d in ds]
        + [left_spec(rank, max(rows, BLOCK))] * len(ds)
        + [chunk_spec(rank, unit, first), chunk_spec(1, unit), group_spec(1, unit, groups, first)]
    )
    args = [pieces[d] for d in ds] + [extras[d] for d in ds] + [right, squares, mag]
    aliases = {}
    if previous is not None:
        in_specs += [pl.BlockSpec(memory_space=pl.ANY), whole_spec(previous[1])]
        args += list(previous)
        aliases = {len(args) - 1: 0}
    if len(ds) == 1:
        out_spec = pl.BlockSpec((rows, unit), lambda j, me: (me[0] ^ ds[0], first + j))
    else:
        out_spec = chunk_spec(tp * rows, unit, first)
    return pl.pallas_call(
        functools.partial(export_kernel, tp, ds, first),
        out_shape=result,
        grid_spec=pltpu.PrefetchScalarGridSpec(
            num_scalar_prefetch=1,
            grid=(count,),
            in_specs=in_specs,
            out_specs=(out_spec, whole_spec(result[1])),
        ),
        input_output_aliases=aliases,
        compiler_params=PARAMS,
        cost_estimate=cost(len(ds) * rows, count * unit, rank, 2),
    )(me, *args)


def body(tp, fsdp, base, left, right, magnitude):
    rows, rank = left.shape
    cols = right.shape[1]
    blocks = cols // BLOCK
    chunks, early = chunk_blocks(blocks)
    mag = magnitude.reshape(1, -1)
    line = lax.axis_index("fsdp").astype(jnp.int32)
    me = lax.axis_index("tp").astype(jnp.int32).reshape(1)
    place = me + tp * line
    lane = -(-rows // BLOCK) * BLOCK
    left = jnp.pad(left.T, ((0, 0), (0, lane - rows)))
    late = (chunks[early][0], chunks[-1][1])
    far = range(2, tp)
    received = {}

    def span(k):
        a, b = chunks[k]
        return a * BLOCK, (b - a) * BLOCK

    def units(k):
        a, b = chunks[k]
        width = width_of(a, b, blocks)
        return width * BLOCK, a // width, (b - a) // width

    def send(k, pieces):
        received[k] = [swap(piece, d, tp) for d, piece in zip(far, pieces)]

    pieces = []
    for d in far:
        if d % 2 == 0:
            piece = pack_first(place, base, tp, d, left, right, (late[0] * BLOCK, late[1] * BLOCK), span(0)[1])
        else:
            piece = pack(after(me, *pieces), base, tp, (d,), *span(0))[0]
        pieces.append(piece)
    send(0, pieces)
    pieces = pack(after(me, *pieces), base, tp, far, *span(1))
    send(1, pieces)
    near = lax.all_to_all(
        pack_near(after(me, *pieces), base, tp), "tp", 0, 0, tiled=True,
        axis_index_groups=[[i, i + 1] for i in range(0, tp, 2)],
    )

    def alternate(even):
        odd = swap(jnp.concatenate(even), 1, tp)
        return [array for i, own in enumerate(even) for array in (own, odd[i * rank : (i + 1) * rank])]

    arrived = [received[0][d - 2] for d in far[::2]]
    half, late_cols = rank // 2, (late[1] - late[0]) * BLOCK
    halves = [[piece[rows : rows + half, i * lane : (i + 1) * lane] for i in range(2)] for piece in arrived]
    extras = alternate([left] + [jnp.concatenate(pair) for pair in halves])

    def late_rights():
        mine = jnp.concatenate([piece[rows:, 2 * lane : 2 * lane + late_cols] for piece in arrived], axis=1)
        other = swap(mine, 1, fsdp, "fsdp")
        both = jnp.where(line % 2 == 0, jnp.concatenate([mine, other]), jnp.concatenate([other, mine]))
        even = [right[:, late[0] * BLOCK : late[1] * BLOCK]]
        even += [both[:, i * late_cols : (i + 1) * late_cols] for i in range(len(arrived))]
        return alternate(even)

    apart = rows % BLOCK == 0 and len(chunks) == early + 1
    every = tuple(range(tp))
    result = None
    token = ()
    totals = {}

    def export(k, ds):
        nonlocal result
        result = export_chunk(me, base, near, received.get(k, ()), extras, right, totals[k], mag, ds, *units(k), result)

    for k in range(len(chunks)):
        following = k + AHEAD
        if following < len(chunks):
            turn = after(me, *received[k], *token)
            if following == CARRIER:
                width = width_of(late[0], late[1] - late[0], blocks)
                sums = sender_squares(
                    turn, base, left, late_rights(), width * BLOCK, late[0] // width, (late[1] - late[0]) // width
                )
                sums = sums[0::2] + swap(sums[1::2], 1, tp)
                late_sums = sums[:1]
                send(following, pack_carrier(turn, base, tp, far, terms_of(sums), *span(following)))
            elif following == len(chunks) - 1:
                pieces = []
                for d in far:
                    pieces += pack(after(turn, *pieces), base, tp, (d,), *span(following))
                send(following, pieces)
            else:
                send(following, pack(turn, base, tp, far, *span(following)))
        if k < early:
            if apart and k == early - 1:
                export(early, every[:2])
                token = (result[1],)
            turn = after(me, *token)
            local = None
            for ds in (every[:-1], every[-1:]) if apart and k == early - 1 else (every,):
                local = column_squares(turn, base, near, received[k], extras, right, ds, *units(k), local)
            if k == CARRIER:
                for piece in received[k][::2]:
                    parts = after(piece, *token)[rows : rows + TERMS, : late_sums.shape[1]].astype(jnp.float32)
                    late_sums = late_sums + jnp.sum(parts, axis=0, keepdims=True)
                local = jnp.concatenate([local, late_sums], axis=1)
            total = lax.psum(local, "fsdp") if k < early - 1 else total_of(local, fsdp, "fsdp")
            totals[k] = total[:, : span(k)[1]]
            if k == CARRIER:
                for i in range(early, len(chunks)):
                    start = span(k)[1] + span(i)[0] - late[0] * BLOCK
                    totals[i] = total[:, start : start + span(i)[1]]
        if apart and k == early:
            for d in far:
                export(k, (d,))
        else:
            export(k, every)
        token = (result[1],)
    return result


def solution(mesh):
    in_specs = (P(("fsdp", "tp"), None), P(("fsdp", "tp"), None), P(None, "tp"), P())
    out_specs = (P("fsdp", "tp"), P("fsdp", "tp"))
    return jax.shard_map(
        functools.partial(body, mesh.shape["tp"], mesh.shape["fsdp"]), mesh=mesh, in_specs=in_specs, out_specs=out_specs, check_vma=False
    )
```

```python
import functools

import jax
import jax.numpy as jnp
from jax import lax
from jax.experimental import pallas as pl
from jax.experimental.pallas import tpu as pltpu
from jax.sharding import PartitionSpec as P

BLOCK = 128
EPSILON = 1e-06
EARLY = (12, 12, 12, 6, 6)
LATE = (4,)
AHEAD = 2
SCALE = 3
CARRIER = 2
TERMS = 3
SUMS_ROWS = 16
PARAMS = pltpu.CompilerParams(vmem_limit_bytes=52 * 2**20)
MOVE_PARAMS = pltpu.CompilerParams(vmem_limit_bytes=56 * 2**20)


def chunk_blocks(total):
    parts = EARLY + LATE
    bounds = [total * sum(parts[:i]) // sum(parts) for i in range(len(parts) + 1)]
    chunks = [(a, b) for a, b in zip(bounds, bounds[1:]) if b > a]
    return chunks, sum(a < bounds[len(EARLY)] for a, _ in chunks)


def width_of(*counts):
    return max(d for d in (4, 2, 1) if all(count % d == 0 for count in counts))


def after(value, *others):
    return lax.optimization_barrier((value, *others))[0]


def swap(array, d, size, axis="tp"):
    return lax.ppermute(array, axis, [(i, i ^ d) for i in range(size)])


def total_of(array, size, axis):
    d = 1
    while d < size:
        others = (d,) if 2 * d == size else (d, 2 * d, 3 * d)
        array = array + sum(swap(array, other, size, axis) for other in others)
        d *= 1 + len(others)
    return array


def move_kernel(moves, number, direct, me_ref, *refs):
    plan = moves(me_ref[0])
    holds = () if direct else refs[-len(plan) - 2 : -2]
    sources, targets = refs[:number], refs[number : len(refs) - len(holds) - 2]
    came, went = refs[-2:]
    ins, outs = [], []
    for i, (source, row, col, rows, cols, target, to_row, to_col) in enumerate(plan):
        block = sources[source].at[pl.ds(row, rows), pl.ds(col, cols)]
        place = targets[target].at[pl.ds(to_row, rows), pl.ds(to_col, cols)]
        ins.append(pltpu.make_async_copy(block, place if direct else holds[i], came.at[i]))
        if not direct:
            outs.append(pltpu.make_async_copy(holds[i], place, went.at[i]))
    for copy in ins:
        copy.start()
    for i, copy in enumerate(ins):
        copy.wait()
        if not direct:
            outs[i].start()
    for copy in outs:
        copy.wait()


def move(me, arrays, shapes, moves, direct=False):
    dtype = arrays[0].dtype
    plan = moves(0)
    kind = pltpu.VMEM if direct else jax.ShapeDtypeStruct
    space = pltpu.VMEM if direct else pl.ANY
    return pl.pallas_call(
        functools.partial(move_kernel, moves, len(arrays), direct),
        out_shape=[kind(shape, dtype) for shape in shapes],
        grid_spec=pltpu.PrefetchScalarGridSpec(
            num_scalar_prefetch=1,
            grid=(1,),
            in_specs=[pl.BlockSpec(memory_space=pl.ANY)] * len(arrays),
            out_specs=[pl.BlockSpec(memory_space=space)] * len(shapes),
            scratch_shapes=[pltpu.VMEM((rows, cols), dtype) for _, _, _, rows, cols, *_ in (() if direct else plan)]
            + [pltpu.SemaphoreType.DMA((len(plan),))] * 2,
        ),
        compiler_params=MOVE_PARAMS,
        cost_estimate=cost(sum(rows * cols for rows, cols in shapes), 1, 0, 2),
    )(me, *arrays)


def parts_of(rows):
    height = rows // 8 if rows % BLOCK == 0 else rows
    return [(r, height) for r in range(0, rows, height)]


def column_moves(me, rows, cols, group, first, target):
    col = pl.multiple_of(me * group + first, BLOCK)
    return [(0, r, col, height, cols, target, r, 0) for r, height in parts_of(rows)]


def group_spec(rows, unit, groups, first, d=0):
    return pl.BlockSpec((rows, unit), lambda j, me: (0, (me[0] ^ d) * groups + first + j))


def chunk_spec(rows, unit, first=0):
    return pl.BlockSpec((rows, unit), lambda j, me: (0, first + j))


def left_spec(rank, unit):
    return pl.BlockSpec((rank, unit), lambda j, me: (0, 0))


def whole_spec(array):
    return pl.BlockSpec(array.shape, lambda j, me: (0, 0))


def cost(rows, cols, rank, passes):
    return pl.CostEstimate(
        flops=2 * rows * cols * rank // SCALE, bytes_accessed=2 * passes * rows * cols // SCALE, transcendentals=0
    )


def pack(me, base, tp, distances, first, cols):
    rows, group = base.shape[0], base.shape[1] // tp

    def moves(me):
        return [m for i, d in enumerate(distances) for m in column_moves(me ^ d, rows, cols, group, first, i)]

    return move(me, [base], [(rows, cols)] * len(distances), moves)


def pack_first(place, base, tp, d, left, right, late, cols):
    rows, group = base.shape[0], base.shape[1] // tp
    rank, lane = left.shape
    half = rank // 2

    def moves(place):
        line, me = place // tp, place % tp
        result = column_moves(me ^ d, rows, cols, group, 0, 0)
        for i in range(2):
            result.append((1, i * half, 0, half, lane, 0, rows, i * lane))
        row = pl.multiple_of(line % 2 * half, half)
        result.append((2, row, late[0], half, late[1] - late[0], 0, rows, 2 * lane))
        return result

    return move(place, [base, left, right], [(rows + half, cols)], moves, direct=True)[0]


def pack_carrier(me, base, tp, distances, terms, first, cols):
    rows, group = base.shape[0], base.shape[1] // tp

    def moves(me):
        result = []
        for i, d in enumerate(distances):
            result += column_moves(me ^ d, rows, cols, group, first, i)
            if d % 2 == 0:
                result.append((1, d // 2 * SUMS_ROWS, 0, SUMS_ROWS, terms.shape[1], i, rows, 0))
        return result

    return move(me, [base, terms], [(rows + (d + 1) % 2 * SUMS_ROWS, cols) for d in distances], moves)


def pack_near(me, base, tp):
    rows, group = base.shape[0], base.shape[1] // tp

    def moves(me):
        result = []
        for s in range(2):
            for source, r, col, *rest in column_moves((me // 2) * 2 + s, rows, group, group, 0, 0):
                result.append((source, r, col, *rest[:-2], s * rows + r, 0))
        return result

    return move(me, [base], [(2 * rows, group)], moves)[0]


def near_spec(rows, unit, first):
    return pl.BlockSpec((rows, unit), lambda j, me: ((me[0] % 2) ^ 1, first + j))


def low_rank(extra_ref, start, height, right):
    left = extra_ref[pl.ds(0, right.shape[0]), pl.ds(start, height)]
    return lax.dot_general(left, right, (((0,), (0,)), ((), ())), preferred_element_type=jnp.float32)


def squares_of(piece_ref, extra_ref, right):
    rows, cols = piece_ref.shape
    height = min(rows, BLOCK)
    total = jnp.zeros((8, cols), jnp.float32)
    for r in range(0, rows, height):
        combined = piece_ref[pl.ds(r, height), :].astype(jnp.float32) + low_rank(extra_ref, r, height, right)
        total = total + jnp.sum((combined * combined).reshape(height // 8, 8, cols), axis=0)
    return total


def squares_kernel(number, me_ref, *refs):
    pieces, extras, right_ref, out_ref = refs[:number], refs[number : 2 * number], refs[2 * number], refs[-1]
    right = right_ref[...]
    total = sum(squares_of(piece, extra, right) for piece, extra in zip(pieces, extras))
    total = jnp.sum(total, axis=0, keepdims=True)
    out_ref[...] = total + refs[-2][...] if len(refs) > 2 * number + 2 else total


def sender_squares_kernel(tp, me_ref, *refs):
    pieces, rights, left, sums_ref = refs[:tp], refs[tp : 2 * tp], refs[-2], refs[-1]
    for d in range(tp):
        sums_ref[pl.ds(d, 1), :] = jnp.sum(squares_of(pieces[d], left, rights[d][...]), axis=0, keepdims=True)


def terms_kernel(sums_ref, terms_ref):
    line = lax.broadcasted_iota(jnp.int32, (SUMS_ROWS, sums_ref.shape[1]), 0)
    for i in range(sums_ref.shape[0]):
        sums = sums_ref[pl.ds(i, 1), :]
        block = jnp.zeros(line.shape, jnp.float32)
        for term in range(TERMS):
            part = sums.astype(jnp.bfloat16).astype(jnp.float32)
            block = jnp.where(line == term, part, block)
            sums = sums - part
        terms_ref[pl.ds(i * SUMS_ROWS, SUMS_ROWS), :] = block.astype(jnp.bfloat16)


def terms_of(sums):
    rows, cols = sums.shape
    return pl.pallas_call(
        terms_kernel,
        out_shape=jax.ShapeDtypeStruct((rows * SUMS_ROWS, cols), jnp.bfloat16),
        compiler_params=PARAMS,
        cost_estimate=cost(rows, cols, 0, 2),
    )(sums)


def piece_specs(tp, rows, unit, groups, first):
    specs = [group_spec(rows, unit, groups, first), near_spec(rows, unit, first)]
    return specs + [chunk_spec(rows, unit)] * (tp - 2)


def column_squares(me, base, near, received, extras, right, ds, unit, first, count, previous=None):
    rows = base.shape[0]
    rank, cols = right.shape
    pieces = [base, near, *received]
    specs = piece_specs(len(extras), rows, unit, cols // unit, first)
    in_specs = [specs[d] for d in ds] + [left_spec(rank, max(rows, BLOCK))] * len(ds) + [chunk_spec(rank, unit, first)]
    args = [pieces[d] for d in ds] + [extras[d] for d in ds] + [right]
    if previous is not None:
        in_specs.append(chunk_spec(1, unit))
        args.append(previous)
    return pl.pallas_call(
        functools.partial(squares_kernel, len(ds)),
        out_shape=jax.ShapeDtypeStruct((1, count * unit), jnp.float32),
        grid_spec=pltpu.PrefetchScalarGridSpec(
            num_scalar_prefetch=1,
            grid=(count,),
            in_specs=in_specs,
            out_specs=chunk_spec(1, unit),
        ),
        compiler_params=PARAMS,
        cost_estimate=cost(len(ds) * rows, count * unit, rank, 1),
    )(me, *args)


def sender_squares(me, base, left, rights, unit, first, count):
    rows = base.shape[0]
    tp = len(rights)
    groups = base.shape[1] // (tp * unit)
    rank = left.shape[0]
    return pl.pallas_call(
        functools.partial(sender_squares_kernel, tp),
        out_shape=jax.ShapeDtypeStruct((tp, count * unit), jnp.float32),
        grid_spec=pltpu.PrefetchScalarGridSpec(
            num_scalar_prefetch=1,
            grid=(count,),
            in_specs=[group_spec(rows, unit, groups, first, d) for d in range(tp)]
            + [chunk_spec(rank, unit)] * tp
            + [whole_spec(left)],
            out_specs=chunk_spec(tp, unit),
        ),
        compiler_params=PARAMS,
        cost_estimate=cost(tp * rows, count * unit, rank, 1),
    )(me, *[base] * tp, *rights, left)


def export_kernel(tp, ds, first, me_ref, *refs):
    number = len(ds)
    pieces, extras = refs[:number], refs[number : 2 * number]
    right_ref, squares_ref, mag_ref = refs[2 * number : 2 * number + 3]
    out_ref, scales_ref = refs[-2:]
    rows, cols = pieces[0].shape
    step = pl.program_id(0)
    if len(refs) > 2 * number + 5:
        @pl.when(step == 0)
        def _():
            scales_ref[...] = refs[2 * number + 4][...]

    factor = mag_ref[...] / jnp.sqrt(squares_ref[...] + EPSILON)
    right = right_ref[...]
    lane = lax.broadcasted_iota(jnp.int32, (1, scales_ref.shape[1]), 1)
    per_step = cols // BLOCK

    def merge(i, r, height):
        combined = pieces[i][pl.ds(r, height), :].astype(jnp.float32) + low_rank(extras[i], r, height, right)
        return (combined * factor).astype(jnp.bfloat16)

    def finish(merged, span, block):
        line = scales_ref[pl.ds(block, 1), :]
        for j in range(per_step):
            tile = merged[:, j * BLOCK : (j + 1) * BLOCK].astype(jnp.float32)
            largest = jnp.max(jnp.max(jnp.abs(tile), axis=0, keepdims=True), axis=1, keepdims=True)
            out_ref[span, pl.ds(j * BLOCK, BLOCK)] = (tile * (1.0 / (largest + EPSILON))).astype(jnp.bfloat16)
            line = jnp.where(lane == (first + step) * per_step + j, largest, line)
        scales_ref[pl.ds(block, 1), :] = line

    if rows % BLOCK == 0:
        for i, d in enumerate(ds):
            place = me_ref[0] ^ d
            start = place * rows if out_ref.shape[0] > rows else 0
            for r in range(0, rows, BLOCK):
                span = pl.ds(pl.multiple_of(start + r, BLOCK), BLOCK)
                finish(merge(i, r, BLOCK), span, place * (rows // BLOCK) + r // BLOCK)
    else:
        for i, d in enumerate(ds):
            out_ref[pl.ds(pl.multiple_of((me_ref[0] ^ d) * rows, rows), rows), :] = merge(i, 0, rows)
        for block in range(tp * rows // BLOCK):
            span = pl.ds(block * BLOCK, BLOCK)
            finish(out_ref[span, :], span, block)


def export_chunk(me, base, near, received, extras, right, squares, mag, ds, unit, first, count, previous):
    rows = base.shape[0]
    rank, cols = right.shape
    tp = len(extras)
    groups = cols // unit
    result = (
        jax.ShapeDtypeStruct((tp * rows, cols), jnp.bfloat16),
        jax.ShapeDtypeStruct((tp * rows // BLOCK, cols // BLOCK), jnp.float32),
    )
    pieces = [base, near, *received]
    specs = piece_specs(tp, rows, unit, groups, first)
    in_specs = (
        [specs[d] for d in ds]
        + [left_spec(rank, max(rows, BLOCK))] * len(ds)
        + [chunk_spec(rank, unit, first), chunk_spec(1, unit), group_spec(1, unit, groups, first)]
    )
    args = [pieces[d] for d in ds] + [extras[d] for d in ds] + [right, squares, mag]
    aliases = {}
    if previous is not None:
        in_specs += [pl.BlockSpec(memory_space=pl.ANY), whole_spec(previous[1])]
        args += list(previous)
        aliases = {len(args) - 1: 0}
    if len(ds) == 1:
        out_spec = pl.BlockSpec((rows, unit), lambda j, me: (me[0] ^ ds[0], first + j))
    else:
        out_spec = chunk_spec(tp * rows, unit, first)
    return pl.pallas_call(
        functools.partial(export_kernel, tp, ds, first),
        out_shape=result,
        grid_spec=pltpu.PrefetchScalarGridSpec(
            num_scalar_prefetch=1,
            grid=(count,),
            in_specs=in_specs,
            out_specs=(out_spec, whole_spec(result[1])),
        ),
        input_output_aliases=aliases,
        compiler_params=PARAMS,
        cost_estimate=cost(len(ds) * rows, count * unit, rank, 2),
    )(me, *args)


def body(tp, fsdp, base, left, right, magnitude):
    rows, rank = left.shape
    cols = right.shape[1]
    blocks = cols // BLOCK
    chunks, early = chunk_blocks(blocks)
    mag = magnitude.reshape(1, -1)
    line = lax.axis_index("fsdp").astype(jnp.int32)
    me = lax.axis_index("tp").astype(jnp.int32).reshape(1)
    place = me + tp * line
    lane = -(-rows // BLOCK) * BLOCK
    left = jnp.pad(left.T, ((0, 0), (0, lane - rows)))
    late = (chunks[early][0], chunks[-1][1])
    far = range(2, tp)
    received = {}

    def span(k):
        a, b = chunks[k]
        return a * BLOCK, (b - a) * BLOCK

    def units(k):
        a, b = chunks[k]
        width = width_of(a, b, blocks)
        return width * BLOCK, a // width, (b - a) // width

    def send(k, pieces):
        received[k] = [swap(piece, d, tp) for d, piece in zip(far, pieces)]

    pieces = []
    for d in far:
        if d % 2 == 0:
            piece = pack_first(place, base, tp, d, left, right, (late[0] * BLOCK, late[1] * BLOCK), span(0)[1])
        else:
            piece = pack(after(me, *pieces), base, tp, (d,), *span(0))[0]
        pieces.append(piece)
    send(0, pieces)
    pieces = pack(after(me, *pieces), base, tp, far, *span(1))
    send(1, pieces)
    near = lax.all_to_all(
        pack_near(after(me, *pieces), base, tp), "tp", 0, 0, tiled=True,
        axis_index_groups=[[i, i + 1] for i in range(0, tp, 2)],
    )

    def alternate(even):
        odd = swap(jnp.concatenate(even), 1, tp)
        return [array for i, own in enumerate(even) for array in (own, odd[i * rank : (i + 1) * rank])]

    arrived = [received[0][d - 2] for d in far[::2]]
    half, late_cols = rank // 2, (late[1] - late[0]) * BLOCK
    halves = [[piece[rows : rows + half, i * lane : (i + 1) * lane] for i in range(2)] for piece in arrived]
    extras = alternate([left] + [jnp.concatenate(pair) for pair in halves])

    def late_rights():
        mine = jnp.concatenate([piece[rows:, 2 * lane : 2 * lane + late_cols] for piece in arrived], axis=1)
        other = swap(mine, 1, fsdp, "fsdp")
        both = jnp.where(line % 2 == 0, jnp.concatenate([mine, other]), jnp.concatenate([other, mine]))
        even = [right[:, late[0] * BLOCK : late[1] * BLOCK]]
        even += [both[:, i * late_cols : (i + 1) * late_cols] for i in range(len(arrived))]
        return alternate(even)

    apart = rows % BLOCK == 0 and len(chunks) == early + 1
    every = tuple(range(tp))
    result = None
    token = ()
    totals = {}

    def export(k, ds):
        nonlocal result
        result = export_chunk(me, base, near, received.get(k, ()), extras, right, totals[k], mag, ds, *units(k), result)

    for k in range(len(chunks)):
        following = k + AHEAD
        if following < len(chunks):
            turn = after(me, *received[k], *token)
            if following == CARRIER:
                width = width_of(late[0], late[1] - late[0], blocks)
                sums = sender_squares(
                    turn, base, left, late_rights(), width * BLOCK, late[0] // width, (late[1] - late[0]) // width
                )
                sums = sums[0::2] + swap(sums[1::2], 1, tp)
                late_sums = sums[:1]
                send(following, pack_carrier(turn, base, tp, far, terms_of(sums), *span(following)))
            elif following == len(chunks) - 1:
                pieces = []
                for d in far:
                    pieces += pack(after(turn, *pieces), base, tp, (d,), *span(following))
                send(following, pieces)
            else:
                send(following, pack(turn, base, tp, far, *span(following)))
        if k < early:
            if apart and k == early - 1:
                export(early, every[:2])
                token = (result[1],)
            turn = after(me, *token)
            local = None
            for ds in (every[:-1], every[-1:]) if apart and k == early - 1 else (every,):
                local = column_squares(turn, base, near, received[k], extras, right, ds, *units(k), local)
            if k == CARRIER:
                for piece in received[k][::2]:
                    parts = after(piece, *token)[rows : rows + TERMS, : late_sums.shape[1]].astype(jnp.float32)
                    late_sums = late_sums + jnp.sum(parts, axis=0, keepdims=True)
                local = jnp.concatenate([local, late_sums], axis=1)
            total = lax.psum(local, "fsdp") if k < early - 1 else total_of(local, fsdp, "fsdp")
            totals[k] = total[:, : span(k)[1]]
            if k == CARRIER:
                for i in range(early, len(chunks)):
                    start = span(k)[1] + span(i)[0] - late[0] * BLOCK
                    totals[i] = total[:, start : start + span(i)[1]]
        if apart and k == early:
            for d in far:
                export(k, (d,))
        else:
            export(k, every)
        token = (result[1],)
    return result


def solution(mesh):
    in_specs = (P(("fsdp", "tp"), None), P(("fsdp", "tp"), None), P(None, "tp"), P())
    out_specs = (P("fsdp", "tp"), P("fsdp", "tp"))
    return jax.shard_map(
        functools.partial(body, mesh.shape["tp"], mesh.shape["fsdp"]), mesh=mesh, in_specs=in_specs, out_specs=out_specs, check_vma=False
    )
```

```python
import functools

import jax
import jax.numpy as jnp
from jax import lax
from jax.experimental import pallas as pl
from jax.experimental.pallas import tpu as pltpu
from jax.sharding import PartitionSpec as P

BLOCK = 128
EPSILON = 1e-06
EARLY = (8, 8, 8, 8, 8, 8)
LATE = (4,)
AHEAD = 2
SCALE = 3
CARRIER = 4
TERMS = 3
SUMS_ROWS = 16
PARAMS = pltpu.CompilerParams(vmem_limit_bytes=52 * 2**20)
MOVE_PARAMS = pltpu.CompilerParams(vmem_limit_bytes=56 * 2**20)


def chunk_blocks(total):
    parts = EARLY + LATE
    bounds = [total * sum(parts[:i]) // sum(parts) for i in range(len(parts) + 1)]
    chunks = [(a, b) for a, b in zip(bounds, bounds[1:]) if b > a]
    return chunks, sum(a < bounds[len(EARLY)] for a, _ in chunks)


def width_of(*counts):
    return max(d for d in (4, 2, 1) if all(count % d == 0 for count in counts))


def after(value, *others):
    return lax.optimization_barrier((value, *others))[0]


def swap(array, d, size, axis="tp"):
    return lax.ppermute(array, axis, [(i, i ^ d) for i in range(size)])


def total_of(array, size, axis):
    d = 1
    while d < size:
        others = (d,) if 2 * d == size else (d, 2 * d, 3 * d)
        array = array + sum(swap(array, other, size, axis) for other in others)
        d *= 1 + len(others)
    return array


def move_kernel(moves, number, direct, me_ref, *refs):
    plan = moves(me_ref[0])
    holds = () if direct else refs[-len(plan) - 2 : -2]
    sources, targets = refs[:number], refs[number : len(refs) - len(holds) - 2]
    came, went = refs[-2:]
    ins, outs = [], []
    for i, (source, row, col, rows, cols, target, to_row, to_col) in enumerate(plan):
        block = sources[source].at[pl.ds(row, rows), pl.ds(col, cols)]
        place = targets[target].at[pl.ds(to_row, rows), pl.ds(to_col, cols)]
        ins.append(pltpu.make_async_copy(block, place if direct else holds[i], came.at[i]))
        if not direct:
            outs.append(pltpu.make_async_copy(holds[i], place, went.at[i]))
    for copy in ins:
        copy.start()
    for i, copy in enumerate(ins):
        copy.wait()
        if not direct:
            outs[i].start()
    for copy in outs:
        copy.wait()


def move(me, arrays, shapes, moves, direct=False):
    dtype = arrays[0].dtype
    plan = moves(0)
    kind = pltpu.VMEM if direct else jax.ShapeDtypeStruct
    space = pltpu.VMEM if direct else pl.ANY
    return pl.pallas_call(
        functools.partial(move_kernel, moves, len(arrays), direct),
        out_shape=[kind(shape, dtype) for shape in shapes],
        grid_spec=pltpu.PrefetchScalarGridSpec(
            num_scalar_prefetch=1,
            grid=(1,),
            in_specs=[pl.BlockSpec(memory_space=pl.ANY)] * len(arrays),
            out_specs=[pl.BlockSpec(memory_space=space)] * len(shapes),
            scratch_shapes=[pltpu.VMEM((rows, cols), dtype) for _, _, _, rows, cols, *_ in (() if direct else plan)]
            + [pltpu.SemaphoreType.DMA((len(plan),))] * 2,
        ),
        compiler_params=MOVE_PARAMS,
        cost_estimate=cost(sum(rows * cols for rows, cols in shapes), 1, 0, 2),
    )(me, *arrays)


def parts_of(rows):
    height = rows // 2 if rows % BLOCK == 0 else rows
    return [(r, height) for r in range(0, rows, height)]


def column_moves(me, rows, cols, group, first, target):
    col = pl.multiple_of(me * group + first, BLOCK)
    return [(0, r, col, height, cols, target, r, 0) for r, height in parts_of(rows)]


def group_spec(rows, unit, groups, first, d=0):
    return pl.BlockSpec((rows, unit), lambda j, me: (0, (me[0] ^ d) * groups + first + j))


def chunk_spec(rows, unit, first=0):
    return pl.BlockSpec((rows, unit), lambda j, me: (0, first + j))


def left_spec(rank, unit):
    return pl.BlockSpec((rank, unit), lambda j, me: (0, 0))


def whole_spec(array):
    return pl.BlockSpec(array.shape, lambda j, me: (0, 0))


def cost(rows, cols, rank, passes):
    return pl.CostEstimate(
        flops=2 * rows * cols * rank // SCALE, bytes_accessed=2 * passes * rows * cols // SCALE, transcendentals=0
    )


def pack(me, base, tp, distances, first, cols):
    rows, group = base.shape[0], base.shape[1] // tp

    def moves(me):
        return [m for i, d in enumerate(distances) for m in column_moves(me ^ d, rows, cols, group, first, i)]

    return move(me, [base], [(rows, cols)] * len(distances), moves)


def pack_first(place, base, tp, d, left, right, late, cols):
    rows, group = base.shape[0], base.shape[1] // tp
    rank, lane = left.shape
    late_cols = late[1] - late[0]
    half, quarter = rank // 2, rank // 4

    def moves(place):
        line, me = place // tp, place % tp
        result = column_moves(me ^ d, rows, cols, group, 0, 0)
        for i in range(2):
            result.append((1, i * half, 0, half, lane, 0, rows, i * lane))
            row = pl.multiple_of(line % 2 * half + i * quarter, quarter)
            result.append((2, row, late[0], quarter, late_cols, 0, rows + half, i * late_cols))
        return result

    return move(place, [base, left, right], [(rows + half + quarter, cols)], moves, direct=True)[0]


def pack_carrier(me, base, tp, distances, terms, first, cols):
    rows, group = base.shape[0], base.shape[1] // tp

    def moves(me):
        result = []
        for i, d in enumerate(distances):
            result += column_moves(me ^ d, rows, cols, group, first, i)
            if d % 2 == 0:
                result.append((1, d // 2 * SUMS_ROWS, 0, SUMS_ROWS, terms.shape[1], i, rows, 0))
        return result

    return move(me, [base, terms], [(rows + (d + 1) % 2 * SUMS_ROWS, cols) for d in distances], moves)


def pack_near(me, base, tp):
    rows, group = base.shape[0], base.shape[1] // tp

    def moves(me):
        result = []
        for s in range(2):
            for source, r, col, *rest in column_moves((me // 2) * 2 + s, rows, group, group, 0, 0):
                result.append((source, r, col, *rest[:-2], s * rows + r, 0))
        return result

    return move(me, [base], [(2 * rows, group)], moves)[0]


def near_spec(rows, unit, first):
    return pl.BlockSpec((rows, unit), lambda j, me: ((me[0] % 2) ^ 1, first + j))


def low_rank(extra_ref, start, height, right):
    left = extra_ref[pl.ds(0, right.shape[0]), pl.ds(start, height)]
    return lax.dot_general(left, right, (((0,), (0,)), ((), ())), preferred_element_type=jnp.float32)


def squares_of(piece_ref, extra_ref, right):
    rows, cols = piece_ref.shape
    height = min(rows, BLOCK)
    total = jnp.zeros((8, cols), jnp.float32)
    for r in range(0, rows, height):
        combined = piece_ref[pl.ds(r, height), :].astype(jnp.float32) + low_rank(extra_ref, r, height, right)
        total = total + jnp.sum((combined * combined).reshape(height // 8, 8, cols), axis=0)
    return total


def squares_kernel(number, me_ref, *refs):
    pieces, extras, right_ref, out_ref = refs[:number], refs[number : 2 * number], refs[2 * number], refs[-1]
    right = right_ref[...]
    total = sum(squares_of(piece, extra, right) for piece, extra in zip(pieces, extras))
    total = jnp.sum(total, axis=0, keepdims=True)
    out_ref[...] = total + refs[-2][...] if len(refs) > 2 * number + 2 else total


def sender_squares_kernel(tp, me_ref, *refs):
    pieces, rights, left, sums_ref = refs[:tp], refs[tp : 2 * tp], refs[-2], refs[-1]
    for d in range(tp):
        sums_ref[pl.ds(d, 1), :] = jnp.sum(squares_of(pieces[d], left, rights[d][...]), axis=0, keepdims=True)


def terms_kernel(sums_ref, terms_ref):
    line = lax.broadcasted_iota(jnp.int32, (SUMS_ROWS, sums_ref.shape[1]), 0)
    for i in range(sums_ref.shape[0]):
        sums = sums_ref[pl.ds(i, 1), :]
        block = jnp.zeros(line.shape, jnp.float32)
        for term in range(TERMS):
            part = sums.astype(jnp.bfloat16).astype(jnp.float32)
            block = jnp.where(line == term, part, block)
            sums = sums - part
        terms_ref[pl.ds(i * SUMS_ROWS, SUMS_ROWS), :] = block.astype(jnp.bfloat16)


def terms_of(sums):
    rows, cols = sums.shape
    return pl.pallas_call(
        terms_kernel,
        out_shape=jax.ShapeDtypeStruct((rows * SUMS_ROWS, cols), jnp.bfloat16),
        compiler_params=PARAMS,
        cost_estimate=cost(rows, cols, 0, 2),
    )(sums)


def piece_specs(tp, rows, unit, groups, first):
    specs = [group_spec(rows, unit, groups, first), near_spec(rows, unit, first)]
    return specs + [chunk_spec(rows, unit)] * (tp - 2)


def column_squares(me, base, near, received, extras, right, ds, unit, first, count, previous=None):
    rows = base.shape[0]
    rank, cols = right.shape
    pieces = [base, near, *received]
    specs = piece_specs(len(extras), rows, unit, cols // unit, first)
    in_specs = [specs[d] for d in ds] + [left_spec(rank, max(rows, BLOCK))] * len(ds) + [chunk_spec(rank, unit, first)]
    args = [pieces[d] for d in ds] + [extras[d] for d in ds] + [right]
    if previous is not None:
        in_specs.append(chunk_spec(1, unit))
        args.append(previous)
    return pl.pallas_call(
        functools.partial(squares_kernel, len(ds)),
        out_shape=jax.ShapeDtypeStruct((1, count * unit), jnp.float32),
        grid_spec=pltpu.PrefetchScalarGridSpec(
            num_scalar_prefetch=1,
            grid=(count,),
            in_specs=in_specs,
            out_specs=chunk_spec(1, unit),
        ),
        compiler_params=PARAMS,
        cost_estimate=cost(len(ds) * rows, count * unit, rank, 1),
    )(me, *args)


def sender_squares(me, base, left, rights, unit, first, count):
    rows = base.shape[0]
    tp = len(rights)
    groups = base.shape[1] // (tp * unit)
    rank = left.shape[0]
    return pl.pallas_call(
        functools.partial(sender_squares_kernel, tp),
        out_shape=jax.ShapeDtypeStruct((tp, count * unit), jnp.float32),
        grid_spec=pltpu.PrefetchScalarGridSpec(
            num_scalar_prefetch=1,
            grid=(count,),
            in_specs=[group_spec(rows, unit, groups, first, d) for d in range(tp)]
            + [chunk_spec(rank, unit)] * tp
            + [whole_spec(left)],
            out_specs=chunk_spec(tp, unit),
        ),
        compiler_params=PARAMS,
        cost_estimate=cost(tp * rows, count * unit, rank, 1),
    )(me, *[base] * tp, *rights, left)


def export_kernel(tp, ds, first, me_ref, *refs):
    number = len(ds)
    pieces, extras = refs[:number], refs[number : 2 * number]
    right_ref, squares_ref, mag_ref = refs[2 * number : 2 * number + 3]
    out_ref, scales_ref = refs[-2:]
    rows, cols = pieces[0].shape
    step = pl.program_id(0)
    if len(refs) > 2 * number + 5:
        @pl.when(step == 0)
        def _():
            scales_ref[...] = refs[2 * number + 4][...]

    factor = mag_ref[...] / jnp.sqrt(squares_ref[...] + EPSILON)
    right = right_ref[...]
    lane = lax.broadcasted_iota(jnp.int32, (1, scales_ref.shape[1]), 1)
    per_step = cols // BLOCK

    def merge(i, r, height):
        combined = pieces[i][pl.ds(r, height), :].astype(jnp.float32) + low_rank(extras[i], r, height, right)
        return (combined * factor).astype(jnp.bfloat16)

    def finish(merged, span, block):
        line = scales_ref[pl.ds(block, 1), :]
        for j in range(per_step):
            tile = merged[:, j * BLOCK : (j + 1) * BLOCK].astype(jnp.float32)
            largest = jnp.max(jnp.max(jnp.abs(tile), axis=0, keepdims=True), axis=1, keepdims=True)
            out_ref[span, pl.ds(j * BLOCK, BLOCK)] = (tile * (1.0 / (largest + EPSILON))).astype(jnp.bfloat16)
            line = jnp.where(lane == (first + step) * per_step + j, largest, line)
        scales_ref[pl.ds(block, 1), :] = line

    if rows % BLOCK == 0:
        for i, d in enumerate(ds):
            place = me_ref[0] ^ d
            start = place * rows if out_ref.shape[0] > rows else 0
            for r in range(0, rows, BLOCK):
                span = pl.ds(pl.multiple_of(start + r, BLOCK), BLOCK)
                finish(merge(i, r, BLOCK), span, place * (rows // BLOCK) + r // BLOCK)
    else:
        for i, d in enumerate(ds):
            out_ref[pl.ds(pl.multiple_of((me_ref[0] ^ d) * rows, rows), rows), :] = merge(i, 0, rows)
        for block in range(tp * rows // BLOCK):
            span = pl.ds(block * BLOCK, BLOCK)
            finish(out_ref[span, :], span, block)


def export_chunk(me, base, near, received, extras, right, squares, mag, ds, unit, first, count, previous):
    rows = base.shape[0]
    rank, cols = right.shape
    tp = len(extras)
    groups = cols // unit
    result = (
        jax.ShapeDtypeStruct((tp * rows, cols), jnp.bfloat16),
        jax.ShapeDtypeStruct((tp * rows // BLOCK, cols // BLOCK), jnp.float32),
    )
    pieces = [base, near, *received]
    specs = piece_specs(tp, rows, unit, groups, first)
    in_specs = (
        [specs[d] for d in ds]
        + [left_spec(rank, max(rows, BLOCK))] * len(ds)
        + [chunk_spec(rank, unit, first), chunk_spec(1, unit), group_spec(1, unit, groups, first)]
    )
    args = [pieces[d] for d in ds] + [extras[d] for d in ds] + [right, squares, mag]
    aliases = {}
    if previous is not None:
        in_specs += [pl.BlockSpec(memory_space=pl.ANY), whole_spec(previous[1])]
        args += list(previous)
        aliases = {len(args) - 1: 0}
    if len(ds) == 1:
        out_spec = pl.BlockSpec((rows, unit), lambda j, me: (me[0] ^ ds[0], first + j))
    else:
        out_spec = chunk_spec(tp * rows, unit, first)
    return pl.pallas_call(
        functools.partial(export_kernel, tp, ds, first),
        out_shape=result,
        grid_spec=pltpu.PrefetchScalarGridSpec(
            num_scalar_prefetch=1,
            grid=(count,),
            in_specs=in_specs,
            out_specs=(out_spec, whole_spec(result[1])),
        ),
        input_output_aliases=aliases,
        compiler_params=PARAMS,
        cost_estimate=cost(len(ds) * rows, count * unit, rank, 2),
    )(me, *args)


def body(tp, fsdp, base, left, right, magnitude):
    rows, rank = left.shape
    cols = right.shape[1]
    blocks = cols // BLOCK
    chunks, early = chunk_blocks(blocks)
    mag = magnitude.reshape(1, -1)
    line = lax.axis_index("fsdp").astype(jnp.int32)
    me = lax.axis_index("tp").astype(jnp.int32).reshape(1)
    place = me + tp * line
    lane = -(-rows // BLOCK) * BLOCK
    left = jnp.pad(left.T, ((0, 0), (0, lane - rows)))
    late = (chunks[early][0], chunks[-1][1])
    far = range(2, tp)
    received = {}

    def span(k):
        a, b = chunks[k]
        return a * BLOCK, (b - a) * BLOCK

    def units(k):
        a, b = chunks[k]
        width = width_of(a, b, blocks)
        return width * BLOCK, a // width, (b - a) // width

    def send(k, pieces):
        received[k] = [swap(piece, d, tp) for d, piece in zip(far, pieces)]

    pieces = []
    for d in far:
        if d % 2 == 0:
            piece = pack_first(place, base, tp, d, left, right, (late[0] * BLOCK, late[1] * BLOCK), span(0)[1])
        else:
            piece = pack(after(me, *pieces), base, tp, (d,), *span(0))[0]
        pieces.append(piece)
    send(0, pieces)
    pieces = pack(after(me, *pieces), base, tp, far, *span(1))
    send(1, pieces)
    near = lax.all_to_all(
        pack_near(after(me, *pieces), base, tp), "tp", 0, 0, tiled=True,
        axis_index_groups=[[i, i + 1] for i in range(0, tp, 2)],
    )

    def unfold(block, width):
        return jnp.concatenate([block[:, :width], block[:, width : 2 * width]])

    def alternate(even):
        odd = swap(jnp.concatenate(even), 1, tp)
        return [array for i, own in enumerate(even) for array in (own, odd[i * rank : (i + 1) * rank])]

    arrived = [received[0][d - 2] for d in far[::2]]
    half, late_cols = rank // 2, (late[1] - late[0]) * BLOCK
    extras = alternate([left] + [unfold(piece[rows : rows + half], lane) for piece in arrived])

    def late_rights():
        mine = jnp.concatenate([unfold(piece[rows + half :], late_cols) for piece in arrived], axis=1)
        other = swap(mine, 1, fsdp, "fsdp")
        both = jnp.where(line % 2 == 0, jnp.concatenate([mine, other]), jnp.concatenate([other, mine]))
        even = [right[:, late[0] * BLOCK : late[1] * BLOCK]]
        even += [both[:, i * late_cols : (i + 1) * late_cols] for i in range(len(arrived))]
        return alternate(even)

    apart = rows % BLOCK == 0 and len(chunks) == early + 1
    every = tuple(range(tp))
    result = None
    token = ()
    totals = {}

    def export(k, ds):
        nonlocal result
        result = export_chunk(me, base, near, received.get(k, ()), extras, right, totals[k], mag, ds, *units(k), result)

    for k in range(len(chunks)):
        following = k + AHEAD
        if following < len(chunks):
            turn = after(me, *received[k], *token)
            if following == CARRIER:
                width = width_of(late[0], late[1] - late[0], blocks)
                sums = sender_squares(
                    turn, base, left, late_rights(), width * BLOCK, late[0] // width, (late[1] - late[0]) // width
                )
                sums = sums[0::2] + swap(sums[1::2], 1, tp)
                late_sums = sums[:1]
                send(following, pack_carrier(turn, base, tp, far, terms_of(sums), *span(following)))
            elif following == len(chunks) - 1:
                pieces = []
                for d in far:
                    pieces += pack(after(turn, *pieces), base, tp, (d,), *span(following))
                send(following, pieces)
            else:
                send(following, pack(turn, base, tp, far, *span(following)))
        if k < early:
            if apart and k == early - 1:
                export(early, every[:2])
                token = (result[1],)
            turn = after(me, *token)
            local = None
            for ds in (every[:-1], every[-1:]) if apart and k == early - 1 else (every,):
                local = column_squares(turn, base, near, received[k], extras, right, ds, *units(k), local)
            if k == CARRIER:
                for piece in received[k][::2]:
                    parts = after(piece, *token)[rows : rows + TERMS, : late_sums.shape[1]].astype(jnp.float32)
                    late_sums = late_sums + jnp.sum(parts, axis=0, keepdims=True)
                local = jnp.concatenate([local, late_sums], axis=1)
            total = lax.psum(local, "fsdp") if k < early - 1 else total_of(local, fsdp, "fsdp")
            totals[k] = total[:, : span(k)[1]]
            if k == CARRIER:
                for i in range(early, len(chunks)):
                    start = span(k)[1] + span(i)[0] - late[0] * BLOCK
                    totals[i] = total[:, start : start + span(i)[1]]
        if apart and k == early:
            for d in far:
                export(k, (d,))
        else:
            export(k, every)
        token = (result[1],)
    return result


def solution(mesh):
    in_specs = (P(("fsdp", "tp"), None), P(("fsdp", "tp"), None), P(None, "tp"), P())
    out_specs = (P("fsdp", "tp"), P("fsdp", "tp"))
    return jax.shard_map(
        functools.partial(body, mesh.shape["tp"], mesh.shape["fsdp"]), mesh=mesh, in_specs=in_specs, out_specs=out_specs, check_vma=False
    )
```
